32 devices in a mesh: rep: 2 (over x), blk: 16 (over z, y, core).
Axes of the slice: x: 2, y: 2, z: 4, core: 2. Of those that a mesh axis runs over, the one named last changes fastest.
Arguments:
- hidden: bfloat16 [128, 12288], P(('rep', 'blk')), parts along dimension 0, may hold values from -6 to 6
- ln_gain: float32 [12288], replicated, may hold values from 0.1 to 1.9
- ln_shift: float32 [12288], replicated, may hold values from -2 to 2
- lists: int32 [8, 6], P('rep'), parts along dimension 0, may hold values from 0 to 15, as said below
- counts: int32 [8], P('rep'), parts along dimension 0, may hold values from 1 to 6
- block_slot: int32 [16], replicated, may hold values from 0 to 15, each once
- w_in: bfloat16 [12288, 2048], P(None, 'blk'), may hold values from -0.0546875 to 0.0546875
- b_in: float32 [2048], P('blk'), may hold values from -3 to 3
- w_out: bfloat16 [2048, 12288], P('blk'), may hold values from -0.3125 to 0.3125
- low_in: bfloat16 [12288, 512], P('blk'), may hold values from -0.0546875 to 0.0546875
- low_bias: float32 [512], replicated, may hold values from -3 to 3
- low_out: bfloat16 [512, 12288], P(None, 'blk'), may hold values from -0.25 to 0.25
Outputs:
- mixed: bfloat16 [128, 12288], P(('rep', 'blk')), parts along dimension 0
The draws below stay inside these ranges and needn't reach their ends.
There are 2 independent parts, one for each index of `rep`. The reference program is written for one: setup_inputs(seed, part) draws one part's arguments, and reference() takes and returns one part's arrays. A program takes and returns all parts, laid end to end along the dimension named above; an argument that names none is the same for every part. Nothing has to cross between parts.
Inputs may be any that keep to these rules, and one draw needn't show every extreme that they name: `lists`: entries of one group's list are distinct block ids. Among the live entries of all groups, no block is listed by more than 2 groups, and some block is listed by exactly that many.
All inputs are finite; a program needn't handle non-finite values.
Results may differ from the reference program's by a relative error of at most 0.0063.
Values may be sent and summed in bfloat16 or wider, within the bound.
No kernel may reach another device: no remote copies, remote signals or barrier semaphores. Data moves between devices by JAX's collectives and lax.ppermute only.
A program may use at most 64 MiB of HBM per device.

```python
import jax
import jax.numpy as jnp
from jax import lax

D = 12288
BLOCK = 128
RANK = 512
GROUP = 16
NBLOCKS = 16
TOPB = 6
ROWS = 64
GROUPS = 4


def draw_lists(key, part):
    key = jax.random.fold_in(key, 11)
    first, second = jax.random.split(key)
    order = jax.random.permutation(first, NBLOCKS).astype(jnp.int32)
    rank = jax.random.permutation(second, GROUPS).astype(jnp.int32)
    lead = order[rank % 2]
    cold = NBLOCKS - 2
    steps = jnp.arange(1, TOPB, dtype=jnp.int32)
    rest = order[2 + (rank[:, None] * (TOPB - 1) + steps[None, :] - 1) % cold]
    return jnp.concatenate([lead[:, None], rest], axis=1).astype(jnp.int32)


def draw_counts(key, part):
    key = jax.random.fold_in(key, 23)
    first, second = jax.random.split(key)
    values = jax.random.randint(first, (GROUPS,), 1, TOPB + 1).astype(jnp.int32)
    which = jax.random.permutation(second, GROUPS).astype(jnp.int32)
    values = values.at[which[0]].set(TOPB).at[which[1]].set(1)
    return values.astype(jnp.int32)


def levels(rng, extent, shards, least, high):
    def one(position, shards_of):
        steps = jax.random.uniform(jax.random.fold_in(jax.random.fold_in(rng, 6), position), (shards_of,), jnp.float32, least / len(shards), high / len(shards))
        return jnp.repeat(jnp.exp(steps), extent[position] // shards_of).reshape((-1,) + (1,) * (len(extent) - position - 1))

    loudness = one(*shards[0])
    for cut in shards[1:]:
        loudness = loudness * one(*cut)
    return loudness


def noise(stream_key, dims, spread, limit, pieces=(), held_as=jnp.bfloat16):
    factor_of = levels(stream_key, dims, pieces, -0.22, 0.18) if pieces else 1.0
    entries = jax.random.normal(stream_key, dims, jnp.float32) * spread * factor_of
    return jnp.minimum(jnp.maximum(entries, -limit), limit).astype(held_as)


def setup_inputs(seed: int = 0, part: int = 0) -> dict:
    key_list = jax.random.split(jax.random.key(seed), 13)
    own_keys = jax.random.split(jax.random.fold_in(key_list[12], part), 13)
    return {
        "hidden": noise(own_keys[0], (ROWS, D), 1.0, 6.0, ((0, 16),)),
        "ln_gain": jnp.clip(1.0 + 0.18 * jax.random.normal(key_list[1], (D,), jnp.float32), 0.1, 1.9),
        "ln_shift": noise(key_list[2], (D,), 0.4, 2.0, (), jnp.float32),
        "lists": draw_lists(jax.random.fold_in(jax.random.fold_in(key_list[12], part), 71), part),
        "counts": draw_counts(jax.random.fold_in(jax.random.fold_in(key_list[12], part), 71), part),
        "block_slot": jax.random.permutation(key_list[5], NBLOCKS).astype(jnp.int32),
        "w_in": noise(key_list[6], (D, NBLOCKS * BLOCK), D ** -0.5, 0.0546875, ((1, 16),)),
        "b_in": noise(key_list[7], (NBLOCKS * BLOCK,), 0.5, 3.0, ((0, 16),), jnp.float32),
        "w_out": noise(key_list[8], (NBLOCKS * BLOCK, D), (TOPB * BLOCK // 2) ** -0.5, 0.3125, ((0, 16),)),
        "low_in": noise(key_list[9], (D, RANK), D ** -0.5, 0.0546875, ((0, 16),)),
        "low_bias": noise(key_list[10], (RANK,), 0.5, 3.0, (), jnp.float32),
        "low_out": noise(key_list[11], (RANK, D), RANK ** -0.5, 0.25, ((1, 16),)),
    }


def layer_norm(hidden, ln_gain, ln_shift):
    wide = hidden.astype(jnp.float32)
    mean = lax.optimization_barrier(jnp.mean(wide, axis=-1, keepdims=True))
    centred = wide - mean
    variance = lax.optimization_barrier(jnp.mean(centred * centred, axis=-1, keepdims=True))
    return (centred * lax.rsqrt(variance + 1e-05) * ln_gain + ln_shift).astype(jnp.bfloat16)

def reference(hidden, ln_gain, ln_shift, lists, counts, block_slot, w_in, b_in, w_out, low_in, low_bias, low_out):
    normed = layer_norm(hidden, ln_gain, ln_shift)
    lowz = jnp.dot(normed, low_in, preferred_element_type=jnp.float32)
    low_h = jnp.maximum(lowz + low_bias, 0.0).astype(jnp.bfloat16)
    low_y = jnp.dot(low_h, low_out, preferred_element_type=jnp.float32).astype(jnp.bfloat16)
    groups, top = lists.shape
    width = normed.shape[1]
    grouped = normed.reshape(groups, GROUP, width)

    def one_group(items):
        rows, names, count = items

        def one_entry(total, entry):
            slot = block_slot[names[entry]].astype(jnp.int32)
            first = lax.dynamic_slice_in_dim(w_in, slot * BLOCK, BLOCK, 1)
            bias = lax.dynamic_slice_in_dim(b_in, slot * BLOCK, BLOCK, 0)
            second = lax.dynamic_slice_in_dim(w_out, slot * BLOCK, BLOCK, 0)
            act = jnp.maximum(jnp.dot(rows, first, preferred_element_type=jnp.float32) + bias, 0.0).astype(jnp.bfloat16)
            part = jnp.dot(act, second, preferred_element_type=jnp.float32).astype(jnp.bfloat16).astype(jnp.float32)
            return (total + jnp.where(entry < count, part, jnp.zeros_like(part)), None)
        total, unused = lax.scan(one_entry, jnp.zeros((GROUP, width), jnp.float32), jnp.arange(top, dtype=jnp.int32))
        return total
    sparse = lax.map(one_group, (grouped, lists, counts)).reshape(groups * GROUP, width)
    return (low_y.astype(jnp.float32) + sparse).astype(jnp.bfloat16)
```

```python
import jax
import jax.numpy as jnp
from jax import lax
from jax.sharding import PartitionSpec as P

GROUP = 16


def layer_norm(hidden, ln_gain, ln_shift):
    wide = hidden.astype(jnp.float32)
    mean = jnp.mean(wide, axis=-1, keepdims=True)
    centred = wide - mean
    variance = jnp.mean(centred * centred, axis=-1, keepdims=True)
    return (centred * lax.rsqrt(variance + 1e-05) * ln_gain + ln_shift).astype(jnp.bfloat16)


def activity(lists, counts, block_slot):
    groups, top = lists.shape
    nblocks = block_slot.shape[0]
    names = jnp.arange(nblocks, dtype=jnp.int32)
    live = (jnp.arange(top, dtype=jnp.int32)[None, :] < counts[:, None]).astype(jnp.int32)
    hits = (lists[:, :, None] == names[None, None, :]).astype(jnp.int32) * live[:, :, None]
    by_block = jnp.sum(hits, axis=1)
    placed = (block_slot[:, None] == names[None, :]).astype(jnp.int32)
    return jnp.sum(by_block[:, :, None] * placed[None, :, :], axis=1)


def shards(
    hidden,
    ln_gain,
    ln_shift,
    lists,
    counts,
    block_slot,
    w_in,
    b_in,
    w_out,
    low_in,
    low_bias,
    low_out,
):
    f32, bf16 = jnp.float32, jnp.bfloat16
    devices = lax.axis_size("blk")
    position = lax.axis_index("blk")
    row_dev, width = hidden.shape
    groups = lists.shape[0]
    mates = devices // groups
    slots = groups // 2
    share = low_in.shape[0]
    plane = position // mates
    mate = position % mates

    def across(x, k):
        return x if k == 0 else lax.ppermute(x, "blk", [(i, i ^ (mates * k)) for i in range(devices)])

    def within(x, j):
        return x if j == 0 else lax.ppermute(x, "blk", [(i, i ^ j) for i in range(devices)])

    normed = layer_norm(hidden, ln_gain, ln_shift)
    table = activity(lists, counts, block_slot)
    mine = lax.dynamic_slice_in_dim(table, plane * mates, mates, 1)
    order = jnp.arange(mates, dtype=jnp.int32) ^ mate
    mine = mine[:, order]
    rank = jnp.cumsum(mine, axis=0) - mine
    hot = (mine[:, :, None] > 0) & (rank[:, :, None] == jnp.arange(slots)[None, None, :])
    pick = jnp.sum(jnp.where(hot, jnp.arange(groups, dtype=jnp.int32)[:, None, None], 0), axis=0)
    seat = pick ^ plane

    held = jnp.stack([across(normed, k) for k in range(groups)])
    rows, lows = [], []
    for j in range(mates):
        wanted = jnp.stack([lax.dynamic_index_in_dim(held, seat[j, s], 0, False) for s in range(slots)])
        rows.append(within(wanted, j))
        cols = lax.dynamic_slice_in_dim(held, (position ^ j) * share, share, 2)
        lows.append(within(cols, j))
    x = jnp.stack(rows)
    x = x[order].transpose(1, 0, 2, 3).reshape(slots * GROUP, width)
    xl = jnp.stack(lows).reshape(mates * groups * row_dev, share)
    partial = jnp.dot(xl, low_in, preferred_element_type=f32).reshape(mates, groups, row_dev, -1)
    summed = sum(within(partial[j], j) for j in range(mates))
    lowz = 0.0
    for k in range(groups):
        got = across(summed, k)
        lowz = lowz + jnp.stack([got[q ^ k] for q in range(groups)])
    low_h = jnp.maximum(lowz + low_bias, 0.0).astype(bf16)
    all_h = jnp.stack([within(low_h, j) for j in range(mates)])
    low_cols = jnp.dot(
        all_h.reshape(mates * groups * row_dev, -1), low_out, preferred_element_type=f32
    ).astype(bf16).reshape(mates, groups, row_dev, share)

    pre = jnp.dot(x, w_in, preferred_element_type=f32) + b_in
    act = jnp.maximum(pre, 0.0).astype(bf16)
    part = jnp.dot(act, w_out, preferred_element_type=f32).astype(bf16)
    part = part.reshape(slots, mates, row_dev, width)

    back = [within(lax.dynamic_index_in_dim(part, mate ^ j, 1, False), j) for j in range(mates)]
    low_back = jnp.stack([within(low_cols[j], j) for j in range(mates)])[order]
    low_back = low_back.transpose(1, 2, 0, 3).reshape(groups, row_dev, mates * share)
    live = hot.astype(f32)
    total = None
    for k in range(groups):
        group = plane ^ k
        flags = lax.dynamic_index_in_dim(live, group, 0, False)
        partsum = jnp.zeros((row_dev, width), f32)
        for j in range(mates):
            for s in range(slots):
                partsum = partsum + jnp.where(flags[j, s] > 0, back[j][s].astype(f32), 0.0)
        here = lax.dynamic_slice_in_dim(partsum, plane * mates * share, mates * share, 1)
        partsum = lax.dynamic_update_slice_in_dim(
            partsum, here + low_back[k].astype(f32), plane * mates * share, 1
        )
        if k == 0:
            total = partsum
        else:
            total = total + across(partsum.astype(bf16), k).astype(f32)
    return total.astype(bf16)


def solution(mesh):
    return jax.shard_map(
        shards,
        mesh=mesh,
        in_specs=(
            P(("rep", "blk"), None),
            P(),
            P(),
            P("rep", None),
            P("rep"),
            P(),
            P(None, "blk"),
            P("blk"),
            P("blk", None),
            P("blk", None),
            P(),
            P(None, "blk"),
        ),
        out_specs=P(("rep", "blk"), None),
        check_vma=False,
    )
```

```python
import functools

import jax
import jax.numpy as jnp
from jax import lax
from jax.experimental import pallas as pl
from jax.experimental.pallas import tpu as pltpu
from jax.sharding import PartitionSpec as P

GROUP = 16
MIB = 1 << 20
VMEM = pl.BlockSpec(memory_space=pltpu.VMEM)
SMEM = pl.BlockSpec(memory_space=pltpu.SMEM)
f32, bf16 = jnp.float32, jnp.bfloat16


def piece(width, most):
    size = 128
    while size * 2 <= most and width % (size * 2) == 0:
        size *= 2
    return size


def call(body, outs, ins, limit, scratch=(), flops=0, moved=0):
    return pl.pallas_call(
        body,
        out_shape=outs,
        in_specs=ins,
        out_specs=[VMEM] * len(outs),
        scratch_shapes=list(scratch),
        compiler_params=pltpu.CompilerParams(vmem_limit_bytes=limit * MIB),
        cost_estimate=pl.CostEstimate(flops=flops, bytes_accessed=moved, transcendentals=0),
    )


def norm_body(hidden, gain, shift, out):
    wide = hidden[...].astype(f32)
    mean = jnp.mean(wide, axis=-1, keepdims=True)
    centred = wide - mean
    variance = jnp.mean(centred * centred, axis=-1, keepdims=True)
    out[...] = (centred * lax.rsqrt(variance + 1e-05) * gain[...] + shift[...]).astype(bf16)


def window(index, size):
    return pl.ds(pl.multiple_of(index * size, 128), size)


def strip(whole, index, mates, share):
    wide = whole[:, window(index // mates, mates * share)].astype(f32)
    own = [jnp.where(index % mates == a, wide[:, a * share : (a + 1) * share], 0.0) for a in range(mates)]
    return sum(own).astype(bf16)


def pack_body(groups, mates, share, place, pick, *refs):
    held, rows, lows, whole = refs[:groups], refs[groups : groups + mates], refs[groups + mates : -1], refs[-1]
    width = held[0].shape[1]
    each = rows[0].shape[0]
    step = piece(width, 2048)

    @pl.loop(0, width // step)
    def _(i):
        cols = pl.ds(pl.multiple_of(i * step, step), step)
        block = jnp.concatenate([h[:, cols] for h in held], axis=0)
        whole[:, cols] = block
        chosen = jnp.dot(pick[...], block, preferred_element_type=f32).astype(bf16)
        for j in range(mates):
            rows[j][:, cols] = chosen[j * each : (j + 1) * each]

    for j in range(mates):
        lows[j][...] = whole[:, window(place[0] ^ j, share)] if share % 128 == 0 else strip(whole, place[0] ^ j, mates, share)


def block_body(mates, *refs):
    x, w_in, b_in, w_out, outs = refs[:mates], refs[mates], refs[mates + 1], refs[mates + 2], refs[mates + 3 :]
    width = w_in.shape[0]
    each = x[0].shape[0]
    step = piece(width, 2048)

    def add(i, total):
        cols = pl.ds(pl.multiple_of(i * step, step), step)
        rows = jnp.concatenate([r[:, cols] for r in x], axis=0)
        return total + jnp.dot(rows, w_in[cols, :], preferred_element_type=f32)

    pre = lax.fori_loop(0, width // step, add, jnp.zeros((mates * each, w_in.shape[1]), f32))
    act = jnp.maximum(pre + b_in[...], 0.0).astype(bf16)

    @pl.loop(0, width // step)
    def _(i):
        cols = pl.ds(pl.multiple_of(i * step, step), step)
        part = jnp.dot(act, w_out[:, cols], preferred_element_type=f32).astype(bf16)
        for j in range(mates):
            outs[j][:, cols] = part[j * each : (j + 1) * each]


def sum_body(groups, mates, share, place, pick, *refs):
    back, lows, outs, whole = refs[:mates], refs[mates : 2 * mates], refs[2 * mates : -1], refs[-1]
    width = back[0].shape[1]
    row_dev = outs[0].shape[0]
    step = piece(width, 2048)

    @pl.loop(0, width // step)
    def _(i):
        cols = pl.ds(pl.multiple_of(i * step, step), step)
        block = jnp.concatenate([b[:, cols] for b in back], axis=0)
        whole[:, cols] = jnp.dot(pick[...], block, preferred_element_type=f32)

    if share % 128 == 0:
        for j in range(mates):
            whole[:, window(place[0] ^ j, share)] += lows[j][...].astype(f32)
    else:
        mate = place[0] % mates
        ordered = [sum(jnp.where(mate ^ j == a, lows[j][...].astype(f32), 0.0) for j in range(mates)) for a in range(mates)]
        whole[:, window(place[0] // mates, mates * share)] += jnp.concatenate(ordered, axis=1)

    @pl.loop(0, width // step)
    def _(i):
        cols = pl.ds(pl.multiple_of(i * step, step), step)
        for k in range(groups):
            outs[k][:, cols] = whole[k * row_dev : (k + 1) * row_dev, cols].astype(outs[k].dtype)


def activity(lists, counts, block_slot):
    groups, top = lists.shape
    nblocks = block_slot.shape[0]
    names = jnp.arange(nblocks, dtype=jnp.int32)
    live = (jnp.arange(top, dtype=jnp.int32)[None, :] < counts[:, None]).astype(jnp.int32)
    hits = (lists[:, :, None] == names[None, None, :]).astype(jnp.int32) * live[:, :, None]
    by_block = jnp.sum(hits, axis=1)
    placed = (block_slot[:, None] == names[None, :]).astype(jnp.int32)
    return jnp.sum(by_block[:, :, None] * placed[None, :, :], axis=1)


def shards(
    hidden,
    ln_gain,
    ln_shift,
    lists,
    counts,
    block_slot,
    w_in,
    b_in,
    w_out,
    low_in,
    low_bias,
    low_out,
):
    devices = lax.axis_size("blk")
    position = lax.axis_index("blk")
    row_dev, width = hidden.shape
    groups = lists.shape[0]
    mates = devices // groups
    slots = groups // 2
    share = low_in.shape[0]
    rank = low_in.shape[1]
    plane = position // mates
    mate = position % mates
    place = jnp.reshape(position, (1,)).astype(jnp.int32)

    def across(x, k):
        return x if k == 0 else lax.ppermute(x, "blk", [(i, i ^ (mates * k)) for i in range(devices)])

    def within(x, j):
        return x if j == 0 else lax.ppermute(x, "blk", [(i, i ^ j) for i in range(devices)])

    def shape(*dims, dtype=bf16):
        return jax.ShapeDtypeStruct(dims, dtype)

    normed = call(norm_body, [shape(row_dev, width)], [VMEM] * 3, 16)(
        hidden, ln_gain.reshape(1, width), ln_shift.reshape(1, width)
    )[0]

    table = activity(lists, counts, block_slot)
    upto = jnp.sum(
        jnp.where(jnp.arange(groups)[:, None] > jnp.arange(groups)[None, :], 1, 0)[:, :, None] * table[None], axis=1
    )
    at = plane * mates + (mate ^ jnp.arange(mates))
    by = plane ^ jnp.arange(groups)
    choose = (at[:, None] == jnp.arange(devices)[None, :])[:, None, None, :]
    relate = (by[:, None] == jnp.arange(groups)[None, :])[None, :, :, None]
    code = jnp.where(table > 0, upto, -1)
    code = jnp.sum(jnp.where(choose & relate, code[None, None], 0), axis=(2, 3))
    hot = (code[:, None, :] == jnp.arange(slots)[None, :, None]).astype(f32)
    eye = jnp.eye(row_dev, dtype=f32)
    pick = (hot[:, :, None, :, None] * eye[None, None, :, None, :]).reshape(
        mates * slots * row_dev, groups * row_dev
    ).astype(bf16)

    held = [across(normed, k) for k in range(groups)]
    each = slots * row_dev
    packed = call(
        functools.partial(pack_body, groups, mates, share),
        [shape(each, width)] * mates + [shape(groups * row_dev, share)] * mates,
        [SMEM, VMEM] + [VMEM] * groups,
        24,
        [pltpu.VMEM((groups * row_dev, width), bf16)],
    )(place, pick, *held)
    lows = [within(packed[mates + j], j) for j in range(mates)]
    rows = [within(packed[j], j) for j in range(mates)]

    partial = jnp.dot(jnp.concatenate(lows, axis=0), low_in, preferred_element_type=f32)
    partial = partial.reshape(mates, groups * row_dev, rank)
    summed = sum(within(partial[j], j) for j in range(mates))
    lowz = 0.0
    for k in range(groups):
        got = across(summed, k).reshape(groups, row_dev, rank)
        lowz = lowz + jnp.stack([got[q ^ k] for q in range(groups)])
    low_h = jnp.maximum(lowz + low_bias, 0.0).astype(bf16).reshape(groups * row_dev, rank)
    all_h = jnp.concatenate([within(low_h, j) for j in range(mates)], axis=0)
    low_cols = jnp.dot(all_h, low_out, preferred_element_type=f32).astype(bf16)
    low_cols = low_cols.reshape(mates, groups * row_dev, share)
    low_back = [within(low_cols[j], j) for j in range(mates)]

    parts = call(
        functools.partial(block_body, mates),
        [shape(each, width)] * mates,
        [VMEM] * (mates + 3),
        32,
    )(*rows, w_in, b_in.reshape(1, -1), w_out)
    back = [within(parts[j], j) for j in range(mates)]
    sums = call(
        functools.partial(sum_body, groups, mates, share),
        [shape(row_dev, width, dtype=f32)] + [shape(row_dev, width)] * (groups - 1),
        [SMEM, VMEM] + [VMEM] * (2 * mates),
        32,
        [pltpu.VMEM((groups * row_dev, width), f32)],
    )(place, pick.T, *back, *low_back)
    total = sums[0]
    for k in range(1, groups):
        total = total + across(sums[k], k).astype(f32)
    return total.astype(bf16)


def solution(mesh):
    return jax.shard_map(
        shards,
        mesh=mesh,
        in_specs=(
            P(("rep", "blk"), None),
            P(),
            P(),
            P("rep", None),
            P("rep"),
            P(),
            P(None, "blk"),
            P("blk"),
            P("blk", None),
            P("blk", None),
            P(),
            P(None, "blk"),
        ),
        out_specs=P(("rep", "blk"), None),
        check_vma=False,
    )
```

```python
import functools

import jax
import jax.numpy as jnp
from jax import lax
from jax.experimental import pallas as pl
from jax.experimental.pallas import tpu as pltpu
from jax.sharding import PartitionSpec as P

MIB = 1 << 20
VMEM = pl.BlockSpec(memory_space=pltpu.VMEM)
SMEM = pl.BlockSpec(memory_space=pltpu.SMEM)
HBM = pl.BlockSpec(memory_space=pl.ANY)
f32, bf16 = jnp.float32, jnp.bfloat16


def piece(width, most):
    size = 128
    while size * 2 <= most and width % (size * 2) == 0:
        size *= 2
    return size


def window(index, size):
    return pl.ds(pl.multiple_of(index * size, 128), size)


def call(body, outs, ins, limit, scratch=(), flops=0, moved=0):
    return pl.pallas_call(
        body,
        out_shape=outs,
        in_specs=ins,
        out_specs=[VMEM] * len(outs),
        scratch_shapes=list(scratch),
        compiler_params=pltpu.CompilerParams(vmem_limit_bytes=limit * MIB),
        cost_estimate=pl.CostEstimate(flops=flops, bytes_accessed=moved, transcendentals=0),
    )


def norm_body(groups, place, hidden, gain, shift, out, *rest):
    strips, (held, gains, shifts, sems) = rest[:groups], rest[groups:]
    copies = [
        pltpu.make_async_copy(src, dst, sems.at[i])
        for i, (src, dst) in enumerate(((hidden, held), (gain, gains), (shift, shifts)))
    ]
    for copy in copies:
        copy.start()
    copies[0].wait()
    wide = held[...].astype(f32)
    mean = jnp.mean(wide, axis=-1, keepdims=True)
    centred = wide - mean
    variance = jnp.mean(centred * centred, axis=-1, keepdims=True)
    copies[1].wait()
    copies[2].wait()
    out[...] = (centred * lax.rsqrt(variance + 1e-05) * gains[...] + shifts[...]).astype(bf16)
    span = strips[0].shape[1]
    for k in range(groups):
        strips[k][...] = out[:, window((place[0] // 4) ^ k, span)]


def sort_body(groups, place, *refs):
    strips, (keep, send) = refs[:groups], refs[groups:]
    span = keep.shape[1]
    upper = (place[0] // 2) % 2
    rows = jnp.concatenate([s[...].astype(f32) for s in strips], axis=0)
    low, high = rows[:, :span], rows[:, span:]
    keep[...] = jnp.where(upper == 0, low, high).astype(bf16)
    send[...] = jnp.where(upper == 0, high, low).astype(bf16)


def down_body(place, keep, got, own, mate, near, far):
    share = own.shape[0]
    core = place[0] % 2
    rows = jnp.concatenate([keep[...].astype(f32), got[...].astype(f32)], axis=0)
    low, high = rows[:, :share], rows[:, share:]
    mine = jnp.where(core == 0, low, high).astype(bf16)
    other = jnp.where(core == 0, high, low).astype(bf16)
    total = jnp.dot(mine, own[...], preferred_element_type=f32) + jnp.dot(
        other, mate[...], preferred_element_type=f32
    )
    half = near.shape[0]
    near[...] = total[:half]
    far[...] = total[half:]


def relu_body(groups, bias, *refs):
    sums, out = refs[:groups], refs[groups]
    rows = out.shape[0] // groups
    for q in range(groups):
        total = bias[...]
        for k in range(groups):
            p = q ^ k
            total = total + sums[k][p * rows : (p + 1) * rows, :]
        out[q * rows : (q + 1) * rows, :] = jnp.maximum(total, 0.0).astype(bf16)


def fetch(srcs, dsts, sems, step, axis):
    copies = []
    for i in range(srcs[0].shape[axis] // step):
        at = (pl.ds(i * step, step), slice(None)) if axis == 0 else (slice(None), pl.ds(i * step, step))
        pair = [pltpu.make_async_copy(s.at[at], d.at[at], sems.at[n, i]) for n, (s, d) in enumerate(zip(srcs, dsts))]
        for copy in pair:
            copy.start()
        copies.append(pair)
    return copies


def act_body(count, step, *refs):
    x, (w_own, w_mate, b_own, b_mate, mask, out, own, mate, sems) = refs[:count], refs[count:]
    copies = fetch((w_own, w_mate), (own, mate), sems, step, 0)
    total = jnp.zeros(out.shape, f32)
    for i, pair in enumerate(copies):
        rows = jnp.concatenate([r[:, i * step : (i + 1) * step] for r in x], axis=0)
        for copy in pair:
            copy.wait()
        both = jnp.concatenate([own[i * step : (i + 1) * step, :], mate[i * step : (i + 1) * step, :]], axis=1)
        total = total + jnp.dot(rows, both, preferred_element_type=f32)
    bias = jnp.concatenate([b_own[...], b_mate[...]], axis=1)
    out[...] = (jnp.maximum(total + bias, 0.0) * mask[...]).astype(bf16)


def part_body(groups, step, place, *refs):
    act, w_own, w_mate, near_h, far_h, low_own, low_mate = refs[:7]
    outs, (own, mate, whole, sems) = refs[7 : 7 + 2 * groups], refs[7 + 2 * groups :]
    share = low_own.shape[1]
    copies = fetch((w_own, w_mate), (own, mate), sems, step, 1)
    for i, pair in enumerate(copies):
        for copy in pair:
            copy.wait()
        both = jnp.concatenate([own[:, i * step : (i + 1) * step], mate[:, i * step : (i + 1) * step]], axis=0)
        whole[:, i * step : (i + 1) * step] = jnp.dot(act[...], both, preferred_element_type=f32)
    core = place[0] % 2
    hidden = jnp.concatenate([near_h[...], far_h[...]], axis=0)
    mine = jnp.dot(hidden, low_own[...], preferred_element_type=f32)
    other = jnp.dot(hidden, low_mate[...], preferred_element_type=f32)
    low, high = jnp.where(core == 0, mine, other), jnp.where(core == 0, other, mine)
    whole[:, window(place[0] // 2, 2 * share)] += jnp.concatenate([low, high], axis=1)
    rows = outs[0].shape[0]
    for q in range(2 * groups):
        outs[q][...] = whole[q * rows : (q + 1) * rows, :].astype(outs[q].dtype)


def activity(lists, counts, block_slot):
    groups, top = lists.shape
    nblocks = block_slot.shape[0]
    names = jnp.arange(nblocks, dtype=jnp.int32)
    live = (jnp.arange(top, dtype=jnp.int32)[None, :] < counts[:, None]).astype(jnp.int32)
    hits = (lists[:, :, None] == names[None, None, :]).astype(jnp.int32) * live[:, :, None]
    by_block = jnp.sum(hits, axis=1)
    placed = (block_slot[:, None] == names[None, :]).astype(jnp.int32)
    return jnp.sum(by_block[:, :, None] * placed[None, :, :], axis=1)


def shards(
    hidden,
    ln_gain,
    ln_shift,
    lists,
    counts,
    block_slot,
    w_in,
    b_in,
    w_out,
    low_in,
    low_bias,
    low_out,
):
    devices = lax.axis_size("blk")
    position = lax.axis_index("blk")
    row_dev, width = hidden.shape
    groups = lists.shape[0]
    share, rank = low_in.shape
    block = w_in.shape[1]
    assert devices == 4 * groups
    plane = position // 4
    place = jnp.reshape(position, (1,)).astype(jnp.int32)
    some, rows = groups * row_dev, 2 * groups * row_dev

    def across(x, k):
        return lax.ppermute(x, "blk", [(i, i ^ (4 * k)) for i in range(devices)])

    def beside(x):
        return lax.ppermute(x, "blk", [(i, i ^ 2) for i in range(devices)])

    def core(x):
        return lax.ppermute(x, "blk", [(i, i ^ 1) for i in range(devices)])

    def shape(*dims, dtype=bf16):
        return jax.ShapeDtypeStruct(dims, dtype)

    normed, *strips = call(
        functools.partial(norm_body, groups),
        [shape(row_dev, width)] + [shape(row_dev, 4 * share)] * groups,
        [SMEM] + [HBM] * 3,
        16,
        [
            pltpu.VMEM((row_dev, width), bf16),
            pltpu.VMEM((1, width), f32),
            pltpu.VMEM((1, width), f32),
            pltpu.SemaphoreType.DMA((3,)),
        ],
    )(place, hidden, ln_gain.reshape(1, width), ln_shift.reshape(1, width))

    bias = b_in.reshape(1, block)
    low_in_mate, low_out_mate, w_in_mate, w_out_mate, bias_mate = (
        core(low_in),
        core(low_out),
        core(w_in),
        core(w_out),
        core(bias),
    )

    strips = [strips[0]] + [across(strips[k], k) for k in range(1, groups)]
    held = [normed] + [across(normed, k) for k in range(1, groups)]
    keep, send = call(
        functools.partial(sort_body, groups), [shape(some, 2 * share)] * 2, [SMEM] + [VMEM] * groups, 16
    )(place, *strips)
    near, far = call(down_body, [shape(some, rank, dtype=f32)] * 2, [SMEM] + [VMEM] * 4, 16)(
        place, keep, beside(send), low_in, low_in_mate
    )
    summed = near + beside(far)
    low_h = call(functools.partial(relu_body, groups), [shape(some, rank)], [VMEM] * (groups + 1), 16)(
        low_bias.reshape(1, rank), summed, *[across(summed, k) for k in range(1, groups)]
    )[0]
    far_h = beside(low_h)

    table = activity(lists, counts, block_slot)
    by = plane ^ jnp.arange(groups)
    at = position ^ jnp.arange(2)
    relate = (by[:, None] == jnp.arange(groups)[None, :])[:, None, :, None]
    choose = (at[:, None] == jnp.arange(devices)[None, :])[None, :, None, :]
    live = jnp.sum(jnp.where(relate & choose, table[None, None], 0), axis=(2, 3)).astype(f32)
    mask = jnp.broadcast_to(live[None, :, None, :, None], (2, groups, row_dev, 2, block)).reshape(rows, 2 * block)

    held = held + [beside(h) for h in held]
    step = piece(width, 2048)
    act = call(
        functools.partial(act_body, 2 * groups, step),
        [shape(rows, 2 * block)],
        [VMEM] * (2 * groups) + [HBM] * 2 + [VMEM] * 3,
        32,
        [pltpu.VMEM((width, block), bf16)] * 2 + [pltpu.SemaphoreType.DMA((2, width // step))],
    )(*held, w_in, w_in_mate, bias, bias_mate, mask)[0]
    parts = call(
        functools.partial(part_body, groups, step),
        [shape(row_dev, width, dtype=f32)] * groups + [shape(row_dev, width)] * groups,
        [SMEM, VMEM] + [HBM] * 2 + [VMEM] * 4,
        32,
        [pltpu.VMEM((block, width), bf16)] * 2
        + [pltpu.VMEM((rows, width), f32), pltpu.SemaphoreType.DMA((2, width // step))],
    )(place, act, w_out, w_out_mate, low_h, far_h, low_out, low_out_mate)
    total = None
    for k in range(groups - 1, -1, -1):
        here = parts[k] + beside(parts[groups + k]).astype(f32)
        if k:
            here = across(here.astype(bf16), k).astype(f32)
        total = here if total is None else total + here
    return total.astype(bf16)


def solution(mesh):
    return jax.shard_map(
        shards,
        mesh=mesh,
        in_specs=(
            P(("rep", "blk"), None),
            P(),
            P(),
            P("rep", None),
            P("rep"),
            P(),
            P(None, "blk"),
            P("blk"),
            P("blk", None),
            P("blk", None),
            P(),
            P(None, "blk"),
        ),
        out_specs=P(("rep", "blk"), None),
        check_vma=False,
    )
```

```python
import functools

import jax
import jax.numpy as jnp
from jax import lax
from jax.experimental import pallas as pl
from jax.experimental.pallas import tpu as pltpu
from jax.sharding import PartitionSpec as P

MIB = 1 << 20
VMEM = pl.BlockSpec(memory_space=pltpu.VMEM)
SMEM = pl.BlockSpec(memory_space=pltpu.SMEM)
HBM = pl.BlockSpec(memory_space=pl.ANY)
f32, bf16 = jnp.float32, jnp.bfloat16


def piece(width, most):
    size = 128
    while size * 2 <= most and width % (size * 2) == 0:
        size *= 2
    return size


def window(index, size):
    return pl.ds(pl.multiple_of(index * size, 128), size)


def call(body, outs, ins, limit, scratch=(), flops=0, moved=0):
    return pl.pallas_call(
        body,
        out_shape=outs,
        in_specs=ins,
        out_specs=[VMEM] * len(outs),
        scratch_shapes=list(scratch),
        compiler_params=pltpu.CompilerParams(vmem_limit_bytes=limit * MIB),
        cost_estimate=pl.CostEstimate(flops=flops, bytes_accessed=moved, transcendentals=0),
    )


def normal(hidden, gain, shift):
    wide = hidden.astype(f32)
    mean = jnp.mean(wide, axis=-1, keepdims=True)
    centred = wide - mean
    variance = jnp.mean(centred * centred, axis=-1, keepdims=True)
    return (centred * lax.rsqrt(variance + 1e-05) * gain + shift).astype(bf16)


def norm_body(groups, place, *refs):
    held, (gain, shift, out, keep, send) = refs[:groups], refs[groups:]
    rows = held[0].shape[0]
    for k in range(groups):
        out[k * rows : (k + 1) * rows, :] = normal(held[k][...], gain[...], shift[...])
    span = keep.shape[1]
    chip = place[0] // 2
    keep[...] = out[:, window(chip, span)]
    send[...] = out[:, window(chip ^ 1, span)]


def turn(x, groups, bit):
    rows = x.shape[0] // (2 * groups)
    at = [h * groups + (k ^ bit) for h in range(2) for k in range(groups)]
    return jnp.concatenate([x[i * rows : (i + 1) * rows] for i in at], axis=0)


def down_body(place, keep, got, own, mate, total, message):
    share = own.shape[0]
    core = place[0] % 2
    rows = jnp.concatenate([keep[...].astype(f32), got[...].astype(f32)], axis=0)
    low, high = rows[:, :share], rows[:, share:]
    mine = jnp.where(core == 0, low, high).astype(bf16)
    other = jnp.where(core == 0, high, low).astype(bf16)
    sums = jnp.dot(mine, own[...], preferred_element_type=f32) + jnp.dot(
        other, mate[...], preferred_element_type=f32
    )
    half = keep.shape[0]
    total[...] = sums
    message[:half, :] = sums[half:].astype(bf16)
    message[half:, :] = sums[:half].astype(bf16)


def merge_body(groups, bit, total, got, out, message):
    sums = total[...] + got[...].astype(f32)
    out[...] = sums
    message[...] = turn(sums, groups, bit).astype(bf16)


def up_body(place, total, got, bias, own, mate, near, far):
    hidden = jnp.maximum(total[...] + got[...].astype(f32) + bias[...], 0.0).astype(bf16)
    core = place[0] % 2
    mine = jnp.dot(hidden, own[...], preferred_element_type=f32)
    other = jnp.dot(hidden, mate[...], preferred_element_type=f32)
    low, high = jnp.where(core == 0, mine, other), jnp.where(core == 0, other, mine)
    both = jnp.concatenate([low, high], axis=1)
    half = near.shape[0]
    near[...] = both[:half].astype(bf16)
    far[...] = both[half:].astype(bf16)


def strip_body(groups, place, near, got, *outs):
    upper = (place[0] // 2) % 2
    mine, other = near[...].astype(f32), got[...].astype(f32)
    both = jnp.concatenate([jnp.where(upper == 0, mine, other), jnp.where(upper == 0, other, mine)], axis=1)
    rows = outs[0].shape[0]
    for k in range(groups):
        outs[k][...] = both[k * rows : (k + 1) * rows].astype(bf16)


def last_body(groups, place, *refs):
    sums, strips, (out, total) = refs[:groups], refs[groups : 2 * groups], refs[2 * groups :]
    whole = sums[0][...]
    for k in range(1, groups):
        whole = whole + sums[k][...].astype(f32)
    total[...] = whole
    for k in range(groups):
        total[:, window((place[0] // 4) ^ k, strips[k].shape[1])] += strips[k][...].astype(f32)
    out[...] = total[...].astype(bf16)


def fetch(srcs, dsts, sems, step, axis):
    copies = []
    for i in range(srcs[0].shape[axis] // step):
        at = (pl.ds(i * step, step), slice(None)) if axis == 0 else (slice(None), pl.ds(i * step, step))
        pair = [pltpu.make_async_copy(s.at[at], d.at[at], sems.at[n, i]) for n, (s, d) in enumerate(zip(srcs, dsts))]
        for copy in pair:
            copy.start()
        copies.append(pair)
    return copies


def act_body(groups, step, normed, *refs):
    held, (gain, shift, w_own, w_mate, b_own, b_mate, mask, out, own, mate, whole, sems) = refs[:groups], refs[groups:]
    copies = fetch((w_own, w_mate), (own, mate), sems, step, 0)
    some, rows = normed.shape[0], held[0].shape[0]
    whole[:some, :] = normed[...]
    for k in range(groups):
        whole[some + k * rows : some + (k + 1) * rows, :] = normal(held[k][...], gain[...], shift[...])
    total = jnp.zeros(out.shape, f32)
    for i, pair in enumerate(copies):
        for copy in pair:
            copy.wait()
        both = jnp.concatenate([own[i * step : (i + 1) * step, :], mate[i * step : (i + 1) * step, :]], axis=1)
        total = total + jnp.dot(whole[:, i * step : (i + 1) * step], both, preferred_element_type=f32)
    bias = jnp.concatenate([b_own[...], b_mate[...]], axis=1)
    out[...] = (jnp.maximum(total + bias, 0.0) * mask[...]).astype(bf16)


def part_body(groups, step, act, w_own, w_mate, *refs):
    outs, (own, mate, sems) = refs[: 2 * groups], refs[2 * groups :]
    rows = outs[0].shape[0]
    copies = fetch((w_own, w_mate), (own, mate), sems, step, 1)
    for i, pair in enumerate(copies):
        for copy in pair:
            copy.wait()
        cols = slice(i * step, (i + 1) * step)
        both = jnp.concatenate([own[:, cols], mate[:, cols]], axis=0)
        part = jnp.dot(act[...], both, preferred_element_type=f32)
        for q in range(2 * groups):
            outs[q][:, cols] = part[q * rows : (q + 1) * rows].astype(outs[q].dtype)


def activity(lists, counts, block_slot):
    groups, top = lists.shape
    nblocks = block_slot.shape[0]
    names = jnp.arange(nblocks, dtype=jnp.int32)
    live = (jnp.arange(top, dtype=jnp.int32)[None, :] < counts[:, None]).astype(jnp.int32)
    hits = (lists[:, :, None] == names[None, None, :]).astype(jnp.int32) * live[:, :, None]
    by_block = jnp.sum(hits, axis=1)
    placed = (block_slot[:, None] == names[None, :]).astype(jnp.int32)
    return jnp.sum(by_block[:, :, None] * placed[None, :, :], axis=1)


def shards(
    hidden,
    ln_gain,
    ln_shift,
    lists,
    counts,
    block_slot,
    w_in,
    b_in,
    w_out,
    low_in,
    low_bias,
    low_out,
):
    devices = lax.axis_size("blk")
    position = lax.axis_index("blk")
    row_dev, width = hidden.shape
    groups = lists.shape[0]
    share, rank = low_in.shape
    block = w_in.shape[1]
    assert devices == 4 * groups
    plane = position // 4
    place = jnp.reshape(position, (1,)).astype(jnp.int32)
    some, rows = groups * row_dev, 2 * groups * row_dev

    def across(x, k):
        return lax.ppermute(x, "blk", [(i, i ^ (4 * k)) for i in range(devices)])

    def beside(x):
        return lax.ppermute(x, "blk", [(i, i ^ 2) for i in range(devices)])

    def core(x):
        return lax.ppermute(x, "blk", [(i, i ^ 1) for i in range(devices)])

    def shape(*dims, dtype=bf16):
        return jax.ShapeDtypeStruct(dims, dtype)

    gain, shift, bias = ln_gain.reshape(1, width), ln_shift.reshape(1, width), b_in.reshape(1, block)
    span = 2 * share

    held = [hidden] + [across(hidden, k) for k in range(1, groups)]
    beyond = [beside(h) for h in held]

    mates, previous = [], None
    for w in (bias, low_in, w_in, w_out, low_out):
        if previous is not None:
            w, previous = lax.optimization_barrier((w, previous))
            mates.append(previous)
        previous = core(w)
    bias_mate, low_in_mate, w_in_mate, w_out_mate = mates
    low_out_mate = previous

    normed, keep, send = call(
        functools.partial(norm_body, groups),
        [shape(some, width)] + [shape(some, span)] * 2,
        [SMEM] + [VMEM] * (groups + 2),
        16,
    )(place, *held, gain, shift)
    total, message = call(
        down_body, [shape(rows, rank, dtype=f32), shape(rows, rank)], [SMEM] + [VMEM] * 4, 16
    )(place, keep, beside(send), low_in, low_in_mate)
    got = beside(message)
    bit = 1
    while bit < groups:
        total, message = call(
            functools.partial(merge_body, groups, bit),
            [shape(rows, rank, dtype=f32), shape(rows, rank)],
            [VMEM] * 2,
            16,
        )(total, got)
        got = across(message, bit)
        bit *= 2
    near, far = call(up_body, [shape(some, span)] * 2, [SMEM] + [VMEM] * 5, 16)(
        place, total, got, low_bias.reshape(1, rank), low_out, low_out_mate
    )
    strips = call(
        functools.partial(strip_body, groups), [shape(row_dev, 2 * span)] * groups, [SMEM] + [VMEM] * 2, 16
    )(place, near, beside(far))
    strips = [strips[0]] + [across(strips[k], k) for k in range(1, groups)]

    table = activity(lists, counts, block_slot)
    by = plane ^ jnp.arange(groups)
    at = position ^ jnp.arange(2)
    relate = (by[:, None] == jnp.arange(groups)[None, :])[:, None, :, None]
    choose = (at[:, None] == jnp.arange(devices)[None, :])[None, :, None, :]
    live = jnp.sum(jnp.where(relate & choose, table[None, None], 0), axis=(2, 3)).astype(f32)
    mask = jnp.broadcast_to(live[None, :, None, :, None], (2, groups, row_dev, 2, block)).reshape(rows, 2 * block)

    step = piece(width, 2048)
    act = call(
        functools.partial(act_body, groups, step),
        [shape(rows, 2 * block)],
        [VMEM] * (groups + 3) + [HBM] * 2 + [VMEM] * 3,
        56,
        [pltpu.VMEM((width, block), bf16)] * 2
        + [pltpu.VMEM((rows, width), bf16), pltpu.SemaphoreType.DMA((2, width // step))],
    )(normed, *beyond, gain, shift, w_in, w_in_mate, bias, bias_mate, mask)[0]
    parts = call(
        functools.partial(part_body, groups, step),
        [shape(row_dev, width, dtype=f32)] * groups + [shape(row_dev, width)] * groups,
        [VMEM] + [HBM] * 2,
        56,
        [pltpu.VMEM((block, width), bf16)] * 2 + [pltpu.SemaphoreType.DMA((2, width // step))],
    )(act, w_out, w_out_mate)
    sums = []
    for k in range(groups - 1, -1, -1):
        here = parts[k] + beside(parts[groups + k]).astype(f32)
        sums.append(across(here.astype(bf16), k) if k else here)
    return call(
        functools.partial(last_body, groups),
        [shape(row_dev, width)],
        [SMEM] + [VMEM] * (2 * groups),
        16,
        [pltpu.VMEM((row_dev, width), f32)],
    )(place, *sums[::-1], *strips)[0]


def solution(mesh):
    return jax.shard_map(
        shards,
        mesh=mesh,
        in_specs=(
            P(("rep", "blk"), None),
            P(),
            P(),
            P("rep", None),
            P("rep"),
            P(),
            P(None, "blk"),
            P("blk"),
            P("blk", None),
            P("blk", None),
            P(),
            P(None, "blk"),
        ),
        out_specs=P(("rep", "blk"), None),
        check_vma=False,
    )
```

```python
import functools

import jax
import jax.numpy as jnp
from jax import lax
from jax.experimental import pallas as pl
from jax.experimental.pallas import tpu as pltpu
from jax.sharding import PartitionSpec as P

MIB = 1 << 20
VMEM = pl.BlockSpec(memory_space=pltpu.VMEM)
SMEM = pl.BlockSpec(memory_space=pltpu.SMEM)
HBM = pl.BlockSpec(memory_space=pl.ANY)
f32, bf16 = jnp.float32, jnp.bfloat16


def piece(width, most):
    size = 128
    while size * 2 <= most and width % (size * 2) == 0:
        size *= 2
    return size


def window(index, size):
    return pl.ds(pl.multiple_of(index * size, 128), size)


def call(body, outs, ins, limit, scratch=(), moved=2 * MIB):
    return pl.pallas_call(
        body,
        out_shape=outs,
        in_specs=ins,
        out_specs=[VMEM] * len(outs),
        scratch_shapes=list(scratch),
        compiler_params=pltpu.CompilerParams(vmem_limit_bytes=limit * MIB),
        cost_estimate=pl.CostEstimate(flops=0, bytes_accessed=moved, transcendentals=0),
    )


def normal(hidden, gain, shift):
    wide = hidden.astype(f32)
    mean = jnp.mean(wide, axis=-1, keepdims=True)
    centred = wide - mean
    variance = jnp.mean(centred * centred, axis=-1, keepdims=True)
    return (centred * lax.rsqrt(variance + 1e-05) * gain + shift).astype(bf16)


def norm_body(count, place, *refs):
    held, (gain, shift, out, keep, send) = refs[:count], refs[count:]
    rows = held[0].shape[0]
    for k in range(count):
        out[k * rows : (k + 1) * rows, :] = normal(held[k][...], gain[...], shift[...])
    some, span = keep.shape
    chip = place[0] // 2
    keep[...] = out[:some, window(chip, span)]
    send[...] = out[:some, window(chip ^ 1, span)]


def turn(x, groups, bit):
    rows = x.shape[0] // (2 * groups)
    at = [h * groups + (k ^ bit) for h in range(2) for k in range(groups)]
    return jnp.concatenate([x[i * rows : (i + 1) * rows] for i in at], axis=0)


def down_body(place, keep, got, own, mate, total, message):
    share = own.shape[0]
    core = place[0] % 2
    rows = jnp.concatenate([keep[...].astype(f32), got[...].astype(f32)], axis=0)
    low, high = rows[:, :share], rows[:, share:]
    mine = jnp.where(core == 0, low, high).astype(bf16)
    other = jnp.where(core == 0, high, low).astype(bf16)
    sums = jnp.dot(mine, own[...], preferred_element_type=f32) + jnp.dot(
        other, mate[...], preferred_element_type=f32
    )
    half = keep.shape[0]
    total[...] = sums
    message[:half, :] = sums[half:].astype(bf16)
    message[half:, :] = sums[:half].astype(bf16)


def merge_body(groups, bit, total, got, out, message):
    sums = total[...] + got[...].astype(f32)
    out[...] = sums
    message[...] = turn(sums, groups, bit).astype(bf16)


def up_body(place, total, got, bias, own, mate, near, far):
    hidden = jnp.maximum(total[...] + got[...].astype(f32) + bias[...], 0.0).astype(bf16)
    core = place[0] % 2
    mine = jnp.dot(hidden, own[...], preferred_element_type=f32)
    other = jnp.dot(hidden, mate[...], preferred_element_type=f32)
    low, high = jnp.where(core == 0, mine, other), jnp.where(core == 0, other, mine)
    both = jnp.concatenate([low, high], axis=1)
    half = near.shape[0]
    near[...] = both[:half].astype(bf16)
    far[...] = both[half:].astype(bf16)


def strip_body(groups, place, near, got, *outs):
    upper = (place[0] // 2) % 2
    mine, other = near[...].astype(f32), got[...].astype(f32)
    both = jnp.concatenate([jnp.where(upper == 0, mine, other), jnp.where(upper == 0, other, mine)], axis=1)
    rows = outs[0].shape[0]
    for k in range(groups):
        outs[k][...] = both[k * rows : (k + 1) * rows].astype(bf16)


def last_body(groups, place, *refs):
    sums, strips, (out, total) = refs[:groups], refs[groups : 2 * groups], refs[2 * groups :]
    whole = sums[0][...]
    for k in range(1, groups):
        whole = whole + sums[k][...].astype(f32)
    total[...] = whole
    for k in range(groups):
        total[:, window((place[0] // 4) ^ k, strips[k].shape[1])] += strips[k][...].astype(f32)
    out[...] = total[...].astype(bf16)


def fetch(srcs, dsts, sems, step, axis):
    copies = []
    for i in range(srcs[0].shape[axis] // step):
        at = (pl.ds(i * step, step), slice(None)) if axis == 0 else (slice(None), pl.ds(i * step, step))
        pair = [pltpu.make_async_copy(s.at[at], d.at[at], sems.at[n, i]) for n, (s, d) in enumerate(zip(srcs, dsts))]
        for copy in pair:
            copy.start()
        copies.append(pair)
    return copies


def act_body(count, step, normed, *refs):
    held, (gain, shift, w_own, w_mate, b_own, b_mate, mask, out, own, mate, whole, sems) = refs[:count], refs[count:]
    copies = fetch((w_own, w_mate), (own, mate), sems, step, 0)
    some, rows = normed.shape[0], held[0].shape[0]
    whole[:some, :] = normed[...]
    for k in range(count):
        whole[some + k * rows : some + (k + 1) * rows, :] = normal(held[k][...], gain[...], shift[...])
    total = jnp.zeros(out.shape, f32)
    for i, pair in enumerate(copies):
        for copy in pair:
            copy.wait()
        both = jnp.concatenate([own[i * step : (i + 1) * step, :], mate[i * step : (i + 1) * step, :]], axis=1)
        total = total + jnp.dot(whole[:, i * step : (i + 1) * step], both, preferred_element_type=f32)
    bias = jnp.concatenate([b_own[...], b_mate[...]], axis=1)
    out[...] = (jnp.maximum(total + bias, 0.0) * mask[...]).astype(bf16)


def part_body(groups, step, act, w_own, w_mate, *refs):
    outs, (own, mate, sems) = refs[: 2 * groups], refs[2 * groups :]
    rows = outs[0].shape[0]
    copies = fetch((w_own, w_mate), (own, mate), sems, step, 1)
    for i, pair in enumerate(copies):
        for copy in pair:
            copy.wait()
        cols = slice(i * step, (i + 1) * step)
        both = jnp.concatenate([own[:, cols], mate[:, cols]], axis=0)
        part = jnp.dot(act[...], both, preferred_element_type=f32)
        for q in range(2 * groups):
            outs[q][:, cols] = part[q * rows : (q + 1) * rows].astype(outs[q].dtype)


def activity(lists, counts, block_slot):
    groups, top = lists.shape
    nblocks = block_slot.shape[0]
    names = jnp.arange(nblocks, dtype=jnp.int32)
    live = (jnp.arange(top, dtype=jnp.int32)[None, :] < counts[:, None]).astype(jnp.int32)
    hits = (lists[:, :, None] == names[None, None, :]).astype(jnp.int32) * live[:, :, None]
    by_block = jnp.sum(hits, axis=1)
    placed = (block_slot[:, None] == names[None, :]).astype(jnp.int32)
    return jnp.sum(by_block[:, :, None] * placed[None, :, :], axis=1)


def shards(
    hidden,
    ln_gain,
    ln_shift,
    lists,
    counts,
    block_slot,
    w_in,
    b_in,
    w_out,
    low_in,
    low_bias,
    low_out,
):
    devices = lax.axis_size("blk")
    position = lax.axis_index("blk")
    row_dev, width = hidden.shape
    groups = lists.shape[0]
    share, rank = low_in.shape
    block = w_in.shape[1]
    assert devices == 4 * groups
    plane = position // 4
    place = jnp.reshape(position, (1,)).astype(jnp.int32)
    some, rows = groups * row_dev, 2 * groups * row_dev

    def across(x, k):
        return lax.ppermute(x, "blk", [(i, i ^ (4 * k)) for i in range(devices)])

    def beside(x):
        return lax.ppermute(x, "blk", [(i, i ^ 2) for i in range(devices)])

    def core(x):
        return lax.ppermute(x, "blk", [(i, i ^ 1) for i in range(devices)])

    def shape(*dims, dtype=bf16):
        return jax.ShapeDtypeStruct(dims, dtype)

    gain, shift, bias = ln_gain.reshape(1, width), ln_shift.reshape(1, width), b_in.reshape(1, block)
    span = 2 * share

    held = [hidden] + [across(hidden, k) for k in range(1, groups)]
    w_in_mate = core(w_in)
    held[-1], low_in_sent, bias_sent = lax.optimization_barrier((held[-1], low_in, bias))
    low_in_mate, bias_mate = core(low_in_sent), core(bias_sent)
    beyond = [beside(h) for h in held]

    soon = groups // 2
    normed, keep, send = call(
        functools.partial(norm_body, groups + soon),
        [shape(some + soon * row_dev, width)] + [shape(some, span)] * 2,
        [SMEM] + [VMEM] * (groups + soon + 2),
        16,
    )(place, *held, *beyond[:soon], gain, shift)
    send, w_in_mate, w_out_sent = lax.optimization_barrier((send, w_in_mate, w_out))
    w_out_mate = core(w_out_sent)
    total, message = call(
        down_body, [shape(rows, rank, dtype=f32), shape(rows, rank)], [SMEM] + [VMEM] * 4, 16
    )(place, keep, beside(send), low_in, low_in_mate)
    message, normed, low_out_sent = lax.optimization_barrier((message, normed, low_out))
    low_out_mate = core(low_out_sent)
    got = beside(message)
    table = activity(lists, counts, block_slot)
    by = plane ^ jnp.arange(groups)
    at = position ^ jnp.arange(2)
    relate = (by[:, None] == jnp.arange(groups)[None, :])[:, None, :, None]
    choose = (at[:, None] == jnp.arange(devices)[None, :])[None, :, None, :]
    live = jnp.sum(jnp.where(relate & choose, table[None, None], 0), axis=(2, 3)).astype(f32)
    mask = jnp.broadcast_to(live[None, :, None, :, None], (2, groups, row_dev, 2, block)).reshape(rows, 2 * block)

    step = piece(width, 2048)
    act = call(
        functools.partial(act_body, groups - soon, step),
        [shape(rows, 2 * block)],
        [VMEM] * (groups - soon + 3) + [HBM] * 2 + [VMEM] * 3,
        56,
        [pltpu.VMEM((width, block), bf16)] * 2
        + [pltpu.VMEM((rows, width), bf16), pltpu.SemaphoreType.DMA((2, width // step))],
        16 * MIB,
    )(normed, *beyond[soon:], gain, shift, w_in, w_in_mate, bias, bias_mate, mask)[0]
    total, message = call(
        functools.partial(merge_body, groups, 1),
        [shape(rows, rank, dtype=f32), shape(rows, rank)],
        [VMEM] * 2,
        16,
    )(total, got)
    message, act = lax.optimization_barrier((message, act))
    got = across(message, 1)
    bit = 2
    while bit < groups:
        total, message = call(
            functools.partial(merge_body, groups, bit),
            [shape(rows, rank, dtype=f32), shape(rows, rank)],
            [VMEM] * 2,
            16,
        )(total, got)
        got = across(message, bit)
        bit *= 2
    parts = call(
        functools.partial(part_body, groups, step),
        [shape(row_dev, width, dtype=f32)] * groups + [shape(row_dev, width)] * groups,
        [VMEM] + [HBM] * 2,
        56,
        [pltpu.VMEM((block, width), bf16)] * 2 + [pltpu.SemaphoreType.DMA((2, width // step))],
        16 * MIB,
    )(act, w_out, w_out_mate)
    come = [beside(parts[groups + k]) for k in range(1, groups)]

    got, come[-1] = lax.optimization_barrier((got, come[-1]))
    near, far = call(up_body, [shape(some, span)] * 2, [SMEM] + [VMEM] * 5, 16)(
        place, total, got, low_bias.reshape(1, rank), low_out, low_out_mate
    )
    far, come[-2] = lax.optimization_barrier((beside(far), come[-2]))
    strips = call(
        functools.partial(strip_body, groups), [shape(row_dev, 2 * span)] * groups, [SMEM] + [VMEM] * 2, 16
    )(place, near, far)
    strips = [strips[0]] + [across(strips[k], k) for k in range(1, groups)]

    far_part, come[-1] = lax.optimization_barrier((parts[groups], come[-1]))
    sums = []
    for k in range(groups - 1, 0, -1):
        sums.append(across((parts[k] + come[k - 1].astype(f32)).astype(bf16), k))
    sums.append(parts[0] + beside(far_part).astype(f32))
    return call(
        functools.partial(last_body, groups),
        [shape(row_dev, width)],
        [SMEM] + [VMEM] * (2 * groups),
        16,
        [pltpu.VMEM((row_dev, width), f32)],
    )(place, *sums[::-1], *strips)[0]


def solution(mesh):
    return jax.shard_map(
        shards,
        mesh=mesh,
        in_specs=(
            P(("rep", "blk"), None),
            P(),
            P(),
            P("rep", None),
            P("rep"),
            P(),
            P(None, "blk"),
            P("blk"),
            P("blk", None),
            P("blk", None),
            P(),
            P(None, "blk"),
        ),
        out_specs=P(("rep", "blk"), None),
        check_vma=False,
    )
```

```python
import functools

import jax
import jax.numpy as jnp
from jax import lax
from jax.experimental import pallas as pl
from jax.experimental.pallas import tpu as pltpu
from jax.sharding import PartitionSpec as P

MIB = 1 << 20
VMEM = pl.BlockSpec(memory_space=pltpu.VMEM)
HBM = pl.BlockSpec(memory_space=pl.ANY)
SMEM = pl.BlockSpec(memory_space=pltpu.SMEM)
f32, bf16 = jnp.float32, jnp.bfloat16


def piece(width, most):
    size = 128
    while size * 2 <= most and width % (size * 2) == 0:
        size *= 2
    return size


def window(index, size):
    return pl.ds(pl.multiple_of(index * size, 128), size)


def call(body, outs, ins, limit, scratch=(), moved=2 * MIB):
    return pl.pallas_call(
        body,
        out_shape=outs,
        in_specs=ins,
        out_specs=[VMEM] * len(outs),
        scratch_shapes=list(scratch),
        compiler_params=pltpu.CompilerParams(vmem_limit_bytes=limit * MIB),
        cost_estimate=pl.CostEstimate(flops=0, bytes_accessed=moved, transcendentals=0),
    )


def normal(hidden, gain, shift):
    wide = hidden.astype(f32)
    mean = jnp.mean(wide, axis=-1, keepdims=True)
    centred = wide - mean
    variance = jnp.mean(centred * centred, axis=-1, keepdims=True)
    return (centred * lax.rsqrt(variance + 1e-05) * gain + shift).astype(bf16)


def load_body(count, *refs):
    srcs, dsts, sems = refs[:count], refs[count : 2 * count], refs[2 * count]
    copies = [pltpu.make_async_copy(srcs[i], dsts[i], sems.at[i]) for i in range(count)]
    for copy in copies:
        copy.start()
    for copy in copies:
        copy.wait()


def norm_body(groups, place, *refs):
    held, (gain, shift, own, mate, out, total, message) = refs[: 2 * groups], refs[2 * groups :]
    rows = held[0].shape[0]
    for i in range(0, 2 * groups, 2):
        pair = jnp.concatenate([held[i][...], held[i + 1][...]], axis=0)
        out[i * rows : (i + 2) * rows, :] = normal(pair, gain[...], shift[...])
    share = own.shape[0]
    core = place[0] % 2
    columns = out[:, window(place[0] // 2, 2 * share)].astype(f32)
    low, high = columns[:, :share], columns[:, share:]
    mine = jnp.where(core == 0, low, high).astype(bf16)
    other = jnp.where(core == 0, high, low).astype(bf16)
    sums = jnp.dot(mine, own[...], preferred_element_type=f32) + jnp.dot(
        other, mate[...], preferred_element_type=f32
    )
    half = groups * rows
    total[...] = sums
    message[:half, :] = sums[half:].astype(bf16)
    message[half:, :] = sums[:half].astype(bf16)


def turn(x, groups, bit):
    rows = x.shape[0] // (2 * groups)
    at = [h * groups + (k ^ bit) for h in range(2) for k in range(groups)]
    return jnp.concatenate([x[i * rows : (i + 1) * rows] for i in at], axis=0)


def merge_body(groups, bit, total, got, out, message):
    sums = total[...] + got[...].astype(f32)
    out[...] = sums
    message[...] = turn(sums, groups, bit).astype(bf16)


def up_body(groups, place, total, got, bias, own, mate, part, *outs):
    hidden = jnp.maximum(total[...] + got[...].astype(f32) + bias[...], 0.0).astype(bf16)
    core = place[0] % 2
    mine = jnp.dot(hidden, own[...], preferred_element_type=f32)
    other = jnp.dot(hidden, mate[...], preferred_element_type=f32)
    both = jnp.concatenate([jnp.where(core == 0, mine, other), jnp.where(core == 0, other, mine)], axis=1)
    at = window(place[0] // 2, both.shape[1])
    rows = outs[0].shape[0]
    for q in range(2 * groups):
        some = slice(q * rows, (q + 1) * rows)
        outs[q][...] = part[some, :].astype(outs[q].dtype)
        outs[q][:, at] = (part[some, at] + both[some]).astype(outs[q].dtype)


def last_body(groups, *refs):
    sums, out = refs[:groups], refs[groups]
    total = sums[0][...]
    for k in range(1, groups):
        total = total + sums[k][...].astype(f32)
    out[...] = total.astype(bf16)


def act_body(step, normed, w_own, w_mate, b_own, b_mate, mask, out):
    total = jnp.zeros(out.shape, f32)
    for i in range(normed.shape[1] // step):
        at = slice(i * step, (i + 1) * step)
        both = jnp.concatenate([w_own[at, :], w_mate[at, :]], axis=1)
        total = total + jnp.dot(normed[:, at], both, preferred_element_type=f32)
    bias = jnp.concatenate([b_own[...], b_mate[...]], axis=1)
    out[...] = (jnp.maximum(total + bias, 0.0) * mask[...]).astype(bf16)


def part_body(step, act, w_own, w_mate, out):
    for i in range(out.shape[1] // step):
        at = slice(i * step, (i + 1) * step)
        both = jnp.concatenate([w_own[:, at], w_mate[:, at]], axis=0)
        out[:, at] = jnp.dot(act[...], both, preferred_element_type=f32)


def activity(lists, counts, block_slot):
    groups, top = lists.shape
    nblocks = block_slot.shape[0]
    names = jnp.arange(nblocks, dtype=jnp.int32)
    live = (jnp.arange(top, dtype=jnp.int32)[None, :] < counts[:, None]).astype(jnp.int32)
    hits = (lists[:, :, None] == names[None, None, :]).astype(jnp.int32) * live[:, :, None]
    by_block = jnp.sum(hits, axis=1)
    placed = (block_slot[:, None] == names[None, :]).astype(jnp.int32)
    return jnp.sum(by_block[:, :, None] * placed[None, :, :], axis=1)


def shards(
    hidden,
    ln_gain,
    ln_shift,
    lists,
    counts,
    block_slot,
    w_in,
    b_in,
    w_out,
    low_in,
    low_bias,
    low_out,
):
    devices = lax.axis_size("blk")
    position = lax.axis_index("blk")
    row_dev, width = hidden.shape
    groups = lists.shape[0]
    share, rank = low_in.shape
    block = w_in.shape[1]
    assert devices == 4 * groups
    plane = position // 4
    place = jnp.reshape(position, (1,)).astype(jnp.int32)
    some, rows = groups * row_dev, 2 * groups * row_dev

    def across(x, k):
        return lax.ppermute(x, "blk", [(i, i ^ (4 * k)) for i in range(devices)])

    def beside(x):
        return lax.ppermute(x, "blk", [(i, i ^ 2) for i in range(devices)])

    def core(x):
        return lax.ppermute(x, "blk", [(i, i ^ 1) for i in range(devices)])

    def shape(*dims, dtype=bf16):
        return jax.ShapeDtypeStruct(dims, dtype)

    gain, shift, bias = ln_gain.reshape(1, width), ln_shift.reshape(1, width), b_in.reshape(1, block)
    span = 2 * share

    table = activity(lists, counts, block_slot)
    by = plane ^ jnp.arange(groups)
    at = position ^ jnp.arange(2)
    relate = (by[:, None] == jnp.arange(groups)[None, :])[:, None, :, None]
    choose = (at[:, None] == jnp.arange(devices)[None, :])[None, :, None, :]
    live = jnp.sum(jnp.where(relate & choose, table[None, None], 0), axis=(2, 3)).astype(f32)
    mask = jnp.broadcast_to(live[None, :, None, :, None], (2, groups, row_dev, 2, block)).reshape(rows, 2 * block)

    held = [hidden] + [across(hidden, k) for k in range(1, groups)]
    w_in_mate, low_in_mate = core(w_in), core(low_in)
    held[1], low_in_mate, mask = lax.optimization_barrier((held[1], low_in_mate, mask))
    near = (hidden, gain, shift, low_in, w_in, w_out, low_out)
    *near, mask = lax.optimization_barrier((*near, mask))
    near = call(
        functools.partial(load_body, len(near)),
        [shape(*x.shape, dtype=x.dtype) for x in near],
        [HBM] * len(near),
        16,
        [pltpu.SemaphoreType.DMA((len(near),))],
        8 * MIB,
    )(*near)
    held[2], *near = lax.optimization_barrier((held[2], *near))
    hidden_near, gain, shift, low_in, w_in, w_out_near, low_out_near = near
    *_, w_in_mate, w_out_sent, low_out_sent, bias_sent = lax.optimization_barrier(
        (*held, w_in_mate, w_out, low_out, bias)
    )
    bias_mate, w_out_mate, low_out_mate = core(bias_sent), core(w_out_sent), core(low_out_sent)
    beyond = [beside(h) for h in held]
    held = [hidden_near] + held[1:] + beyond

    normed, total, message = call(
        functools.partial(norm_body, groups),
        [shape(rows, width), shape(rows, rank, dtype=f32), shape(rows, rank)],
        [SMEM] + [VMEM] * (2 * groups + 4),
        16,
        (),
        6 * MIB,
    )(place, *held, gain, shift, low_in, low_in_mate)
    got = beside(message)
    step = piece(width, 2048)
    act = call(
        functools.partial(act_body, step),
        [shape(rows, 2 * block)],
        [VMEM] * 6,
        16,
        (),
        6 * MIB,
    )(normed, w_in, w_in_mate, bias, bias_mate, mask)[0]
    bit = 1
    while bit < groups:
        total, message = call(
            functools.partial(merge_body, groups, bit),
            [shape(rows, rank, dtype=f32), shape(rows, rank)],
            [VMEM] * 2,
            16,
        )(total, got)
        if bit == 1:
            message, act = lax.optimization_barrier((message, act))
        got = across(message, bit)
        bit *= 2
    part = call(
        functools.partial(part_body, step),
        [shape(rows, width, dtype=f32)],
        [VMEM] * 3,
        16,
        (),
        6 * MIB,
    )(act, w_out_near, w_out_mate)[0]
    got, part = lax.optimization_barrier((got, part))
    parts = call(
        functools.partial(up_body, groups),
        [shape(row_dev, width, dtype=f32)] * groups + [shape(row_dev, width)] * groups,
        [SMEM] + [VMEM] * 6,
        16,
        (),
        6 * MIB,
    )(place, total, got, low_bias.reshape(1, rank), low_out_near, low_out_mate, part)

    sums = []
    for k in range(groups - 1, -1, -1):
        here = parts[k] + beside(parts[groups + k]).astype(f32)
        sums.append(across(here.astype(bf16), k) if k else here)
    return call(functools.partial(last_body, groups), [shape(row_dev, width)], [VMEM] * groups, 16)(*sums[::-1])[0]


def solution(mesh):
    return jax.shard_map(
        shards,
        mesh=mesh,
        in_specs=(
            P(("rep", "blk"), None),
            P(),
            P(),
            P("rep", None),
            P("rep"),
            P(),
            P(None, "blk"),
            P("blk"),
            P("blk", None),
            P("blk", None),
            P(),
            P(None, "blk"),
        ),
        out_specs=P(("rep", "blk"), None),
        check_vma=False,
    )
```

```python
import functools

import jax
import jax.numpy as jnp
from jax import lax
from jax.experimental import pallas as pl
from jax.experimental.pallas import tpu as pltpu
from jax.sharding import PartitionSpec as P

MIB = 1 << 20
VMEM = pl.BlockSpec(memory_space=pltpu.VMEM)
HBM = pl.BlockSpec(memory_space=pltpu.HBM)
SMEM = pl.BlockSpec(memory_space=pltpu.SMEM)
f32, bf16 = jnp.float32, jnp.bfloat16


def piece(width, most):
    size = 128
    while size * 2 <= most and width % (size * 2) == 0:
        size *= 2
    return size


def window(index, size):
    return pl.ds(pl.multiple_of(index * size, 128), size)


def call(body, outs, ins, limit, scratch=(), moved=2 * MIB):
    return pl.pallas_call(
        body,
        out_shape=outs,
        in_specs=ins,
        out_specs=[VMEM] * len(outs),
        scratch_shapes=list(scratch),
        compiler_params=pltpu.CompilerParams(vmem_limit_bytes=limit * MIB),
        cost_estimate=pl.CostEstimate(flops=0, bytes_accessed=moved, transcendentals=0),
    )


def normal(hidden, gain, shift):
    wide = hidden.astype(f32)
    mean = jnp.mean(wide, axis=-1, keepdims=True)
    centred = wide - mean
    variance = jnp.mean(centred * centred, axis=-1, keepdims=True)
    return (centred * lax.rsqrt(variance + 1e-05) * gain + shift).astype(bf16)


def load_body(count, *refs):
    srcs, dsts, sems = refs[:count], refs[count : 2 * count], refs[2 * count]
    copies = [pltpu.make_async_copy(srcs[i], dsts[i], sems.at[i]) for i in range(count)]
    for copy in copies:
        copy.start()
    for copy in copies:
        copy.wait()


def early_body(groups, soon, *refs):
    held, (gain, shift, near, far) = refs[: groups + soon], refs[groups + soon :]
    rows = held[0].shape[0]
    for out, some in ((near, held[:groups]), (far, held[groups:])):
        for i in range(0, len(some), 2):
            pair = jnp.concatenate([h[...] for h in some[i : i + 2]], axis=0)
            out[i * rows : i * rows + pair.shape[0], :] = normal(pair, gain[...], shift[...])


def norm_body(count, place, *refs):
    held, (near, first, gain, shift, own, mate, far, total, message) = refs[:count], refs[count:]
    rows, done = held[0].shape[0], first.shape[0]
    far[:done, :] = first[...]
    for i in range(0, count, 2):
        pair = jnp.concatenate([h[...] for h in held[i : i + 2]], axis=0)
        far[done + i * rows : done + i * rows + pair.shape[0], :] = normal(pair, gain[...], shift[...])
    share = own.shape[0]
    core = place[0] % 2
    at = window(place[0] // 2, 2 * share)
    columns = jnp.concatenate([near[:, at].astype(f32), far[:, at].astype(f32)], axis=0)
    low, high = columns[:, :share], columns[:, share:]
    mine = jnp.where(core == 0, low, high).astype(bf16)
    other = jnp.where(core == 0, high, low).astype(bf16)
    sums = jnp.dot(mine, own[...], preferred_element_type=f32) + jnp.dot(
        other, mate[...], preferred_element_type=f32
    )
    half = near.shape[0]
    total[...] = sums
    message[:half, :] = sums[half:].astype(bf16)
    message[half:, :] = sums[:half].astype(bf16)


def turn(x, groups, bit):
    rows = x.shape[0] // (2 * groups)
    at = [h * groups + (k ^ bit) for h in range(2) for k in range(groups)]
    return jnp.concatenate([x[i * rows : (i + 1) * rows] for i in at], axis=0)


def merge_body(groups, total, got, out, *messages):
    sums = total[...] + got[...].astype(f32)
    out[...] = sums
    for k in range(1, groups):
        messages[k - 1][...] = turn(sums, groups, k).astype(bf16)


def up_body(groups, place, total, bias, own, mate, part, *refs):
    got, outs = refs[: groups - 1], refs[groups - 1 :]
    sums = total[...]
    for g in got:
        sums = sums + g[...].astype(f32)
    hidden = jnp.maximum(sums + bias[...], 0.0).astype(bf16)
    core = place[0] % 2
    mine = jnp.dot(hidden, own[...], preferred_element_type=f32)
    other = jnp.dot(hidden, mate[...], preferred_element_type=f32)
    both = jnp.concatenate([jnp.where(core == 0, mine, other), jnp.where(core == 0, other, mine)], axis=1)
    at = window(place[0] // 2, both.shape[1])
    rows = outs[0].shape[0]
    for q in range(2 * groups):
        some = slice(q * rows, (q + 1) * rows)
        outs[q][...] = part[some, :].astype(outs[q].dtype)
        outs[q][:, at] = (part[some, at] + both[some]).astype(outs[q].dtype)


def last_body(groups, *refs):
    sums, out = refs[:groups], refs[groups]
    total = sums[0][...]
    for k in range(1, groups):
        total = total + sums[k][...].astype(f32)
    out[...] = total.astype(bf16)


def act_body(step, near, far, w_own, w_mate, b_own, b_mate, mask, out):
    total = jnp.zeros(out.shape, f32)
    for i in range(near.shape[1] // step):
        at = slice(i * step, (i + 1) * step)
        rows = jnp.concatenate([near[:, at], far[:, at]], axis=0)
        both = jnp.concatenate([w_own[at, :], w_mate[at, :]], axis=1)
        total = total + jnp.dot(rows, both, preferred_element_type=f32)
    bias = jnp.concatenate([b_own[...], b_mate[...]], axis=1)
    out[...] = (jnp.maximum(total + bias, 0.0) * mask[...]).astype(bf16)


def part_body(step, act, w_own, w_mate, out):
    for i in range(out.shape[1] // step):
        at = slice(i * step, (i + 1) * step)
        both = jnp.concatenate([w_own[:, at], w_mate[:, at]], axis=0)
        out[:, at] = jnp.dot(act[...], both, preferred_element_type=f32)


def activity(lists, counts, block_slot):
    groups, top = lists.shape
    nblocks = block_slot.shape[0]
    names = jnp.arange(nblocks, dtype=jnp.int32)
    live = (jnp.arange(top, dtype=jnp.int32)[None, :] < counts[:, None]).astype(jnp.int32)
    hits = (lists[:, :, None] == names[None, None, :]).astype(jnp.int32) * live[:, :, None]
    by_block = jnp.sum(hits, axis=1)
    placed = (block_slot[:, None] == names[None, :]).astype(jnp.int32)
    return jnp.sum(by_block[:, :, None] * placed[None, :, :], axis=1)


def shards(
    hidden,
    ln_gain,
    ln_shift,
    lists,
    counts,
    block_slot,
    w_in,
    b_in,
    w_out,
    low_in,
    low_bias,
    low_out,
):
    devices = lax.axis_size("blk")
    position = lax.axis_index("blk")
    row_dev, width = hidden.shape
    groups = lists.shape[0]
    share, rank = low_in.shape
    block = w_in.shape[1]
    assert devices == 4 * groups
    plane = position // 4
    place = jnp.reshape(position, (1,)).astype(jnp.int32)
    some, rows = groups * row_dev, 2 * groups * row_dev

    def across(x, k):
        return lax.ppermute(x, "blk", [(i, i ^ (4 * k)) for i in range(devices)])

    def beside(x):
        return lax.ppermute(x, "blk", [(i, i ^ 2) for i in range(devices)])

    def core(x):
        return lax.ppermute(x, "blk", [(i, i ^ 1) for i in range(devices)])

    def shape(*dims, dtype=bf16):
        return jax.ShapeDtypeStruct(dims, dtype)

    gain, shift, bias = ln_gain.reshape(1, width), ln_shift.reshape(1, width), b_in.reshape(1, block)
    span = 2 * share

    table = activity(lists, counts, block_slot)
    by = plane ^ jnp.arange(groups)
    at = position ^ jnp.arange(2)
    relate = (by[:, None] == jnp.arange(groups)[None, :])[:, None, :, None]
    choose = (at[:, None] == jnp.arange(devices)[None, :])[None, :, None, :]
    live = jnp.sum(jnp.where(relate & choose, table[None, None], 0), axis=(2, 3)).astype(f32)
    mask = jnp.broadcast_to(live[None, :, None, :, None], (2, groups, row_dev, 2, block)).reshape(rows, 2 * block)

    held = [hidden] + [across(hidden, k) for k in range(1, groups)]
    w_in_mate = core(w_in)
    held[1], low_in_sent, mask = lax.optimization_barrier((held[1], low_in, mask))
    low_in_mate = core(low_in_sent)
    beyond = [beside(h) for h in held]
    near = (hidden, gain, shift, low_in, w_in, w_out, low_out)
    *near, mask, beyond[0] = lax.optimization_barrier((*near, mask, beyond[0]))
    near = call(
        functools.partial(load_body, len(near)),
        [shape(*x.shape, dtype=x.dtype) for x in near],
        [HBM] * len(near),
        16,
        [pltpu.SemaphoreType.DMA((len(near),))],
        8 * MIB,
    )(*[pltpu.with_memory_space_constraint(x, pltpu.HBM) for x in near])
    hidden_near, gain, shift, low_in, w_in, w_out_near, low_out_near = near
    *_, w_in_mate, w_out_sent, low_out_sent, bias_sent = lax.optimization_barrier(
        (*held, *beyond[: groups // 2], w_in_mate, w_out, low_out, bias)
    )
    bias_mate, w_out_mate, low_out_mate = core(bias_sent), core(w_out_sent), core(low_out_sent)
    held[0] = hidden_near

    soon = groups // 2
    normed, first = call(
        functools.partial(early_body, groups, soon),
        [shape(some, width), shape(soon * row_dev, width)],
        [VMEM] * (groups + soon + 2),
        16,
        (),
        4 * MIB,
    )(*held, *beyond[:soon], gain, shift)
    far, total, message = call(
        functools.partial(norm_body, groups - soon),
        [shape(some, width), shape(rows, rank, dtype=f32), shape(rows, rank)],
        [SMEM] + [VMEM] * (groups - soon + 6),
        16,
        (),
        4 * MIB,
    )(place, *beyond[soon:], normed, first, gain, shift, low_in, low_in_mate)
    got = beside(message)
    step = piece(width, 2048)
    act = call(
        functools.partial(act_body, step),
        [shape(rows, 2 * block)],
        [VMEM] * 7,
        16,
        (),
        4 * MIB,
    )(normed, far, w_in, w_in_mate, bias, bias_mate, mask)[0]
    total, *messages = call(
        functools.partial(merge_body, groups),
        [shape(rows, rank, dtype=f32)] + [shape(rows, rank)] * (groups - 1),
        [VMEM] * 2,
        16,
    )(total, got)
    got = [across(messages[k - 1], k) for k in range(1, groups)]
    part = call(
        functools.partial(part_body, step),
        [shape(rows, width, dtype=f32)],
        [VMEM] * 3,
        16,
        (),
        6 * MIB,
    )(act, w_out_near, w_out_mate)[0]
    parts = call(
        functools.partial(up_body, groups),
        [shape(row_dev, width, dtype=f32)] * groups + [shape(row_dev, width)] * groups,
        [SMEM] + [VMEM] * (groups + 4),
        16,
        (),
        6 * MIB,
    )(place, total, low_bias.reshape(1, rank), low_out_near, low_out_mate, part, *got)

    sums = []
    for k in range(groups - 1, -1, -1):
        here = parts[k] + beside(parts[groups + k]).astype(f32)
        sums.append(across(here.astype(bf16), k) if k else here)
    return call(functools.partial(last_body, groups), [shape(row_dev, width)], [VMEM] * groups, 16)(*sums[::-1])[0]


def solution(mesh):
    return jax.shard_map(
        shards,
        mesh=mesh,
        in_specs=(
            P(("rep", "blk"), None),
            P(),
            P(),
            P("rep", None),
            P("rep"),
            P(),
            P(None, "blk"),
            P("blk"),
            P("blk", None),
            P("blk", None),
            P(),
            P(None, "blk"),
        ),
        out_specs=P(("rep", "blk"), None),
        check_vma=False,
    )
```

```python
import functools

import jax
import jax.numpy as jnp
from jax import lax
from jax.experimental import pallas as pl
from jax.experimental.pallas import tpu as pltpu
from jax.sharding import PartitionSpec as P

MIB = 1 << 20
VMEM = pl.BlockSpec(memory_space=pltpu.VMEM)
HBM = pl.BlockSpec(memory_space=pltpu.HBM)
SMEM = pl.BlockSpec(memory_space=pltpu.SMEM)
f32, bf16 = jnp.float32, jnp.bfloat16


def piece(width, most):
    size = 128
    while size * 2 <= most and width % (size * 2) == 0:
        size *= 2
    return size


def window(index, size):
    return pl.ds(pl.multiple_of(index * size, 128), size)


def call(body, outs, ins, limit, scratch=(), moved=2 * MIB):
    return pl.pallas_call(
        body,
        out_shape=outs,
        in_specs=ins,
        out_specs=[VMEM] * len(outs),
        scratch_shapes=list(scratch),
        compiler_params=pltpu.CompilerParams(vmem_limit_bytes=limit * MIB),
        cost_estimate=pl.CostEstimate(flops=0, bytes_accessed=moved, transcendentals=0),
    )


def normal(hidden, gain, shift):
    wide = hidden.astype(f32)
    mean = jnp.mean(wide, axis=-1, keepdims=True)
    centred = wide - mean
    variance = jnp.mean(centred * centred, axis=-1, keepdims=True)
    return (centred * lax.rsqrt(variance + 1e-05) * gain + shift).astype(bf16)


def normalise(held, gain, shift, out):
    rows = held[0].shape[0]
    for i in range(0, len(held), 2):
        pair = jnp.concatenate([h[...] for h in held[i : i + 2]], axis=0)
        out[i * rows : (i + 2) * rows, :] = normal(pair, gain[...], shift[...])


def load_body(count, *refs):
    srcs, dsts, sems = refs[:count], refs[count : 2 * count], refs[2 * count]
    copies = [pltpu.make_async_copy(srcs[i], dsts[i], sems.at[i]) for i in range(count)]
    for copy in copies:
        copy.start()
    for copy in copies:
        copy.wait()


def near_body(groups, place, *refs):
    held, (gain, shift, near, keep, send) = refs[:groups], refs[groups:]
    normalise(held, gain, shift, near)
    span = keep.shape[1]
    chip = place[0] // 2
    keep[...] = near[:, window(chip, span)]
    send[...] = near[:, window(chip ^ 1, span)]


def far_body(groups, *refs):
    normalise(refs[:groups], *refs[groups:])


def down_body(place, keep, got, own, mate, total, message):
    share = own.shape[0]
    core = place[0] % 2
    columns = jnp.concatenate([keep[...].astype(f32), got[...].astype(f32)], axis=0)
    low, high = columns[:, :share], columns[:, share:]
    mine = jnp.where(core == 0, low, high).astype(bf16)
    other = jnp.where(core == 0, high, low).astype(bf16)
    sums = jnp.dot(mine, own[...], preferred_element_type=f32) + jnp.dot(
        other, mate[...], preferred_element_type=f32
    )
    half = keep.shape[0]
    total[...] = sums
    message[:half, :] = sums[half:].astype(bf16)
    message[half:, :] = sums[:half].astype(bf16)


def turn(x, groups, bit):
    rows = x.shape[0] // (2 * groups)
    at = [h * groups + (k ^ bit) for h in range(2) for k in range(groups)]
    return jnp.concatenate([x[i * rows : (i + 1) * rows] for i in at], axis=0)


def merge_body(groups, total, got, out, *messages):
    sums = total[...] + got[...].astype(f32)
    out[...] = sums
    for k in range(1, groups):
        messages[k - 1][...] = turn(sums, groups, k).astype(bf16)


def up_body(groups, place, total, bias, own, mate, part, *refs):
    got, outs = refs[: groups - 1], refs[groups - 1 :]
    sums = total[...]
    for g in got:
        sums = sums + g[...].astype(f32)
    hidden = jnp.maximum(sums + bias[...], 0.0).astype(bf16)
    core = place[0] % 2
    mine = jnp.dot(hidden, own[...], preferred_element_type=f32)
    other = jnp.dot(hidden, mate[...], preferred_element_type=f32)
    both = jnp.concatenate([jnp.where(core == 0, mine, other), jnp.where(core == 0, other, mine)], axis=1)
    at = window(place[0] // 2, both.shape[1])
    rows = outs[0].shape[0]
    for q in range(2 * groups):
        some = slice(q * rows, (q + 1) * rows)
        outs[q][...] = part[some, :].astype(outs[q].dtype)
        outs[q][:, at] = (part[some, at] + both[some]).astype(outs[q].dtype)


def last_body(groups, *refs):
    sums, out = refs[:groups], refs[groups]
    total = sums[0][...]
    for k in range(1, groups):
        total = total + sums[k][...].astype(f32)
    out[...] = total.astype(bf16)


def act_body(step, near, far, w_own, w_mate, b_own, b_mate, mask, out):
    total = jnp.zeros(out.shape, f32)
    for i in range(near.shape[1] // step):
        at = slice(i * step, (i + 1) * step)
        rows = jnp.concatenate([near[:, at], far[:, at]], axis=0)
        both = jnp.concatenate([w_own[at, :], w_mate[at, :]], axis=1)
        total = total + jnp.dot(rows, both, preferred_element_type=f32)
    bias = jnp.concatenate([b_own[...], b_mate[...]], axis=1)
    out[...] = (jnp.maximum(total + bias, 0.0) * mask[...]).astype(bf16)


def part_body(step, act, w_own, w_mate, out):
    for i in range(out.shape[1] // step):
        at = slice(i * step, (i + 1) * step)
        both = jnp.concatenate([w_own[:, at], w_mate[:, at]], axis=0)
        out[:, at] = jnp.dot(act[...], both, preferred_element_type=f32)


def activity(lists, counts, block_slot):
    groups, top = lists.shape
    nblocks = block_slot.shape[0]
    names = jnp.arange(nblocks, dtype=jnp.int32)
    live = (jnp.arange(top, dtype=jnp.int32)[None, :] < counts[:, None]).astype(jnp.int32)
    hits = (lists[:, :, None] == names[None, None, :]).astype(jnp.int32) * live[:, :, None]
    by_block = jnp.sum(hits, axis=1)
    placed = (block_slot[:, None] == names[None, :]).astype(jnp.int32)
    return jnp.sum(by_block[:, :, None] * placed[None, :, :], axis=1)


def shards(
    hidden,
    ln_gain,
    ln_shift,
    lists,
    counts,
    block_slot,
    w_in,
    b_in,
    w_out,
    low_in,
    low_bias,
    low_out,
):
    devices = lax.axis_size("blk")
    position = lax.axis_index("blk")
    row_dev, width = hidden.shape
    groups = lists.shape[0]
    share, rank = low_in.shape
    block = w_in.shape[1]
    assert devices == 4 * groups
    plane = position // 4
    place = jnp.reshape(position, (1,)).astype(jnp.int32)
    some, rows = groups * row_dev, 2 * groups * row_dev

    def across(x, k):
        return lax.ppermute(x, "blk", [(i, i ^ (4 * k)) for i in range(devices)])

    def beside(x):
        return lax.ppermute(x, "blk", [(i, i ^ 2) for i in range(devices)])

    def core(x):
        return lax.ppermute(x, "blk", [(i, i ^ 1) for i in range(devices)])

    def shape(*dims, dtype=bf16):
        return jax.ShapeDtypeStruct(dims, dtype)

    gain, shift, bias = ln_gain.reshape(1, width), ln_shift.reshape(1, width), b_in.reshape(1, block)
    span = 2 * share

    table = activity(lists, counts, block_slot)
    by = plane ^ jnp.arange(groups)
    at = position ^ jnp.arange(2)
    relate = (by[:, None] == jnp.arange(groups)[None, :])[:, None, :, None]
    choose = (at[:, None] == jnp.arange(devices)[None, :])[None, :, None, :]
    live = jnp.sum(jnp.where(relate & choose, table[None, None], 0), axis=(2, 3)).astype(f32)
    mask = jnp.broadcast_to(live[None, :, None, :, None], (2, groups, row_dev, 2, block)).reshape(rows, 2 * block)

    held = [hidden] + [across(hidden, k) for k in range(1, groups)]
    w_in_mate = core(w_in)
    near = (hidden, gain, shift, low_in, w_in, w_out, low_out)
    *near, mask = lax.optimization_barrier((*near, mask))
    near = call(
        functools.partial(load_body, len(near)),
        [shape(*x.shape, dtype=x.dtype) for x in near],
        [HBM] * len(near),
        16,
        [pltpu.SemaphoreType.DMA((len(near),))],
        8 * MIB,
    )(*[pltpu.with_memory_space_constraint(x, pltpu.HBM) for x in near])
    held[1], *near = lax.optimization_barrier((held[1], *near))
    hidden_near, gain, shift, low_in_near, w_in, w_out_near, low_out_near = near
    soon = groups // 2
    beyond = [beside(h) for h in held[:soon]]
    *_, w_in_mate, low_in_sent, w_out_sent, low_out_sent, bias_sent = lax.optimization_barrier(
        (*held, *beyond, w_in_mate, low_in, w_out, low_out, bias)
    )
    low_in_mate, bias_mate, w_out_mate, low_out_mate = map(core, (low_in_sent, bias_sent, w_out_sent, low_out_sent))

    hidden_near, *beyond = lax.optimization_barrier((hidden_near, *beyond))
    normed, keep, send = call(
        functools.partial(near_body, groups),
        [shape(some, width), shape(some, span), shape(some, span)],
        [SMEM] + [VMEM] * (groups + 2),
        16,
        (),
        4 * MIB,
    )(place, hidden_near, *held[1:], gain, shift)
    send, *late = lax.optimization_barrier((send, *held[soon:]))
    got = beside(send)
    beyond = beyond + [beside(h) for h in late]
    total, message = call(
        down_body, [shape(rows, rank, dtype=f32), shape(rows, rank)], [SMEM] + [VMEM] * 4, 16
    )(place, keep, got, low_in_near, low_in_mate)
    far = call(
        functools.partial(far_body, groups), [shape(some, width)], [VMEM] * (groups + 2), 16, (), 4 * MIB
    )(*beyond, gain, shift)[0]
    got = beside(message)
    step = piece(width, 2048)
    act = call(
        functools.partial(act_body, step),
        [shape(rows, 2 * block)],
        [VMEM] * 7,
        16,
        (),
        4 * MIB,
    )(normed, far, w_in, w_in_mate, bias, bias_mate, mask)[0]
    total, *messages = call(
        functools.partial(merge_body, groups),
        [shape(rows, rank, dtype=f32)] + [shape(rows, rank)] * (groups - 1),
        [VMEM] * 2,
        16,
    )(total, got)
    got = [across(messages[k - 1], k) for k in range(1, groups)]
    part = call(
        functools.partial(part_body, step),
        [shape(rows, width, dtype=f32)],
        [VMEM] * 3,
        16,
        (),
        6 * MIB,
    )(act, w_out_near, w_out_mate)[0]
    parts = call(
        functools.partial(up_body, groups),
        [shape(row_dev, width, dtype=f32)] * groups + [shape(row_dev, width)] * groups,
        [SMEM] + [VMEM] * (groups + 4),
        16,
        (),
        6 * MIB,
    )(place, total, low_bias.reshape(1, rank), low_out_near, low_out_mate, part, *got)

    sums = []
    for k in range(groups - 1, -1, -1):
        here = parts[k] + beside(parts[groups + k]).astype(f32)
        sums.append(across(here.astype(bf16), k) if k else here)
    return call(functools.partial(last_body, groups), [shape(row_dev, width)], [VMEM] * groups, 16)(*sums[::-1])[0]


def solution(mesh):
    return jax.shard_map(
        shards,
        mesh=mesh,
        in_specs=(
            P(("rep", "blk"), None),
            P(),
            P(),
            P("rep", None),
            P("rep"),
            P(),
            P(None, "blk"),
            P("blk"),
            P("blk", None),
            P("blk", None),
            P(),
            P(None, "blk"),
        ),
        out_specs=P(("rep", "blk"), None),
        check_vma=False,
    )
```

```python
import functools

import jax
import jax.numpy as jnp
from jax import lax
from jax.experimental import pallas as pl
from jax.experimental.pallas import tpu as pltpu
from jax.sharding import PartitionSpec as P

MIB = 1 << 20
VMEM = pl.BlockSpec(memory_space=pltpu.VMEM)
HBM = pl.BlockSpec(memory_space=pltpu.HBM)
SMEM = pl.BlockSpec(memory_space=pltpu.SMEM)
f32, bf16 = jnp.float32, jnp.bfloat16


def piece(width, most):
    size = 128
    while size * 2 <= most and width % (size * 2) == 0:
        size *= 2
    return size


def window(index, size):
    return pl.ds(pl.multiple_of(index * size, 128), size)


def call(body, outs, ins, limit, scratch=(), moved=2 * MIB):
    return pl.pallas_call(
        body,
        out_shape=outs,
        in_specs=ins,
        out_specs=[VMEM] * len(outs),
        scratch_shapes=list(scratch),
        compiler_params=pltpu.CompilerParams(vmem_limit_bytes=limit * MIB),
        cost_estimate=pl.CostEstimate(flops=0, bytes_accessed=moved, transcendentals=0),
    )


def normal(hidden, gain, shift):
    wide = hidden.astype(f32)
    mean = jnp.mean(wide, axis=-1, keepdims=True)
    centred = wide - mean
    variance = jnp.mean(centred * centred, axis=-1, keepdims=True)
    return (centred * lax.rsqrt(variance + 1e-05) * gain + shift).astype(bf16)


def normalise(held, gain, shift, out):
    rows = held[0].shape[0]
    for i in range(0, len(held), 2):
        pair = jnp.concatenate([h[...] for h in held[i : i + 2]], axis=0)
        out[i * rows : (i + 2) * rows, :] = normal(pair, gain[...], shift[...])


def load_body(count, *refs):
    srcs, dsts, sems = refs[:count], refs[count : 2 * count], refs[2 * count]
    copies = [pltpu.make_async_copy(srcs[i], dsts[i], sems.at[i]) for i in range(count)]
    for copy in copies:
        copy.start()
    for copy in copies:
        copy.wait()


def near_body(groups, place, *refs):
    held, (own, gains, shifts, near, keep, send, gain, shift, first, sems) = refs[: groups - 1], refs[groups - 1 :]
    pairs = ((own, first), (gains, gain), (shifts, shift))
    copies = [pltpu.make_async_copy(src, dst, sems.at[i]) for i, (src, dst) in enumerate(pairs)]
    for copy in copies:
        copy.start()
    for copy in copies:
        copy.wait()
    normalise((first, *held), gain, shift, near)
    span = keep.shape[1]
    chip = place[0] // 2
    keep[...] = near[:, window(chip, span)]
    send[...] = near[:, window(chip ^ 1, span)]


def far_body(groups, *refs):
    normalise(refs[:groups], *refs[groups:])


def down_body(place, keep, got, own, mate, total, message):
    share = own.shape[0]
    core = place[0] % 2
    columns = jnp.concatenate([keep[...].astype(f32), got[...].astype(f32)], axis=0)
    low, high = columns[:, :share], columns[:, share:]
    mine = jnp.where(core == 0, low, high).astype(bf16)
    other = jnp.where(core == 0, high, low).astype(bf16)
    sums = jnp.dot(mine, own[...], preferred_element_type=f32) + jnp.dot(
        other, mate[...], preferred_element_type=f32
    )
    half = keep.shape[0]
    total[...] = sums
    message[:half, :] = sums[half:].astype(bf16)
    message[half:, :] = sums[:half].astype(bf16)


def turn(x, groups, bit):
    rows = x.shape[0] // (2 * groups)
    at = [h * groups + (k ^ bit) for h in range(2) for k in range(groups)]
    return jnp.concatenate([x[i * rows : (i + 1) * rows] for i in at], axis=0)


def merge_body(groups, total, got, out, *messages):
    sums = total[...] + got[...].astype(f32)
    out[...] = sums
    for k in range(1, groups):
        messages[k - 1][...] = turn(sums, groups, k).astype(bf16)


def up_body(groups, place, total, bias, own, mate, part, *refs):
    got, outs = refs[: groups - 1], refs[groups - 1 :]
    sums = total[...]
    for g in got:
        sums = sums + g[...].astype(f32)
    hidden = jnp.maximum(sums + bias[...], 0.0).astype(bf16)
    core = place[0] % 2
    mine = jnp.dot(hidden, own[...], preferred_element_type=f32)
    other = jnp.dot(hidden, mate[...], preferred_element_type=f32)
    both = jnp.concatenate([jnp.where(core == 0, mine, other), jnp.where(core == 0, other, mine)], axis=1)
    at = window(place[0] // 2, both.shape[1])
    rows = outs[0].shape[0]
    for q in range(2 * groups):
        some = slice(q * rows, (q + 1) * rows)
        outs[q][...] = part[some, :].astype(outs[q].dtype)
        outs[q][:, at] = (part[some, at] + both[some]).astype(outs[q].dtype)


def last_body(groups, *refs):
    sums, out = refs[:groups], refs[groups]
    total = sums[0][...]
    for k in range(1, groups):
        total = total + sums[k][...].astype(f32)
    out[...] = total.astype(bf16)


def act_body(step, near, far, w_own, w_mate, b_own, b_mate, mask, out):
    total = jnp.zeros(out.shape, f32)
    for i in range(near.shape[1] // step):
        at = slice(i * step, (i + 1) * step)
        rows = jnp.concatenate([near[:, at], far[:, at]], axis=0)
        both = jnp.concatenate([w_own[at, :], w_mate[at, :]], axis=1)
        total = total + jnp.dot(rows, both, preferred_element_type=f32)
    bias = jnp.concatenate([b_own[...], b_mate[...]], axis=1)
    out[...] = (jnp.maximum(total + bias, 0.0) * mask[...]).astype(bf16)


def part_body(step, act, w_own, w_mate, out):
    for i in range(out.shape[1] // step):
        at = slice(i * step, (i + 1) * step)
        both = jnp.concatenate([w_own[:, at], w_mate[:, at]], axis=0)
        out[:, at] = jnp.dot(act[...], both, preferred_element_type=f32)


def activity(lists, counts, block_slot):
    groups, top = lists.shape
    nblocks = block_slot.shape[0]
    names = jnp.arange(nblocks, dtype=jnp.int32)
    live = (jnp.arange(top, dtype=jnp.int32)[None, :] < counts[:, None]).astype(jnp.int32)
    hits = (lists[:, :, None] == names[None, None, :]).astype(jnp.int32) * live[:, :, None]
    by_block = jnp.sum(hits, axis=1)
    placed = (block_slot[:, None] == names[None, :]).astype(jnp.int32)
    return jnp.sum(by_block[:, :, None] * placed[None, :, :], axis=1)


def shards(
    hidden,
    ln_gain,
    ln_shift,
    lists,
    counts,
    block_slot,
    w_in,
    b_in,
    w_out,
    low_in,
    low_bias,
    low_out,
):
    devices = lax.axis_size("blk")
    position = lax.axis_index("blk")
    row_dev, width = hidden.shape
    groups = lists.shape[0]
    share, rank = low_in.shape
    block = w_in.shape[1]
    assert devices == 4 * groups
    plane = position // 4
    place = jnp.reshape(position, (1,)).astype(jnp.int32)
    some, rows = groups * row_dev, 2 * groups * row_dev

    def across(x, k):
        return lax.ppermute(x, "blk", [(i, i ^ (4 * k)) for i in range(devices)])

    def beside(x):
        return lax.ppermute(x, "blk", [(i, i ^ 2) for i in range(devices)])

    def core(x):
        return lax.ppermute(x, "blk", [(i, i ^ 1) for i in range(devices)])

    def shape(*dims, dtype=bf16):
        return jax.ShapeDtypeStruct(dims, dtype)

    gain, shift, bias = ln_gain.reshape(1, width), ln_shift.reshape(1, width), b_in.reshape(1, block)
    span = 2 * share

    table = activity(lists, counts, block_slot)
    by = plane ^ jnp.arange(groups)
    at = position ^ jnp.arange(2)
    relate = (by[:, None] == jnp.arange(groups)[None, :])[:, None, :, None]
    choose = (at[:, None] == jnp.arange(devices)[None, :])[None, :, None, :]
    live = jnp.sum(jnp.where(relate & choose, table[None, None], 0), axis=(2, 3)).astype(f32)
    mask = jnp.broadcast_to(live[None, :, None, :, None], (2, groups, row_dev, 2, block)).reshape(rows, 2 * block)

    held = [hidden] + [across(hidden, k) for k in range(groups - 1, 0, -1)][::-1]
    w_in_mate = core(w_in)
    first, _ = lax.optimization_barrier((hidden, held[1]))
    beyond = [beside(first), beside(held[1])]
    *_, w_in_mate, mask, low_in_sent, w_out_sent, bias_sent = lax.optimization_barrier(
        (*held, *beyond, w_in_mate, mask, low_in, w_out, bias)
    )
    low_in_mate, bias_mate, w_out_mate = map(core, (low_in_sent, bias_sent, w_out_sent))

    own, *beyond = lax.optimization_barrier((hidden, *beyond))
    normed, keep, send, gain, shift = call(
        functools.partial(near_body, groups),
        [shape(some, width), shape(some, span), shape(some, span)] + [shape(1, width, dtype=f32)] * 2,
        [SMEM] + [VMEM] * (groups - 1) + [HBM] * 3,
        16,
        [pltpu.VMEM((row_dev, width), bf16), pltpu.SemaphoreType.DMA((3,))],
        4 * MIB,
    )(place, *held[1:], *[pltpu.with_memory_space_constraint(x, pltpu.HBM) for x in (own, gain, shift)])
    send, *late = lax.optimization_barrier((send, *held[2:]))
    got, bias_mate = lax.optimization_barrier((beside(send), bias_mate))
    beyond = beyond + [beside(h) for h in late]
    near = (low_in, w_in, w_out, low_out)
    *near, keep = lax.optimization_barrier((*near, keep))
    low_in_near, w_in, w_out_near, low_out_near = call(
        functools.partial(load_body, len(near)),
        [shape(*x.shape, dtype=x.dtype) for x in near],
        [HBM] * len(near),
        16,
        [pltpu.SemaphoreType.DMA((len(near),))],
        8 * MIB,
    )(*[pltpu.with_memory_space_constraint(x, pltpu.HBM) for x in near])
    total, message = call(
        down_body, [shape(rows, rank, dtype=f32), shape(rows, rank)], [SMEM] + [VMEM] * 4, 16
    )(place, keep, got, low_in_near, low_in_mate)
    far = call(
        functools.partial(far_body, groups), [shape(some, width)], [VMEM] * (groups + 2), 16, (), 4 * MIB
    )(*beyond, gain, shift)[0]
    got, low_out_sent, w_out_mate = lax.optimization_barrier((beside(message), low_out, w_out_mate))
    low_out_mate = core(low_out_sent)
    step = piece(width, 2048)
    act = call(
        functools.partial(act_body, step),
        [shape(rows, 2 * block)],
        [VMEM] * 7,
        16,
        (),
        4 * MIB,
    )(normed, far, w_in, w_in_mate, bias, bias_mate, mask)[0]
    total, *messages = call(
        functools.partial(merge_body, groups),
        [shape(rows, rank, dtype=f32)] + [shape(rows, rank)] * (groups - 1),
        [VMEM] * 2,
        16,
    )(total, got)
    got = [across(messages[k - 1], k) for k in range(groups - 1, 0, -1)]
    part = call(
        functools.partial(part_body, step),
        [shape(rows, width, dtype=f32)],
        [VMEM] * 3,
        16,
        (),
        6 * MIB,
    )(act, w_out_near, w_out_mate)[0]
    parts = call(
        functools.partial(up_body, groups),
        [shape(row_dev, width, dtype=f32)] * groups + [shape(row_dev, width)] * groups,
        [SMEM] + [VMEM] * (groups + 4),
        16,
        (),
        6 * MIB,
    )(place, total, low_bias.reshape(1, rank), low_out_near, low_out_mate, part, *got)

    sent, half = list(parts[groups:]), groups // 2
    sums = [None] * groups
    for k in range(groups - 1, -1, -1):
        come = beside(sent[k])
        if k == groups - 1:
            come, *sent[:half] = lax.optimization_barrier((come, *sent[:half]))
        here = parts[k] + come.astype(f32)
        sums[k] = across(here.astype(bf16), k) if k else here
    return call(functools.partial(last_body, groups), [shape(row_dev, width)], [VMEM] * groups, 16)(*sums)[0]


def solution(mesh):
    return jax.shard_map(
        shards,
        mesh=mesh,
        in_specs=(
            P(("rep", "blk"), None),
            P(),
            P(),
            P("rep", None),
            P("rep"),
            P(),
            P(None, "blk"),
            P("blk"),
            P("blk", None),
            P("blk", None),
            P(),
            P(None, "blk"),
        ),
        out_specs=P(("rep", "blk"), None),
        check_vma=False,
    )
```

```python
import functools

import jax
import jax.numpy as jnp
from jax import lax
from jax.experimental import pallas as pl
from jax.experimental.pallas import tpu as pltpu
from jax.sharding import PartitionSpec as P

MIB = 1 << 20
VMEM = pl.BlockSpec(memory_space=pltpu.VMEM)
HBM = pl.BlockSpec(memory_space=pltpu.HBM)
SMEM = pl.BlockSpec(memory_space=pltpu.SMEM)
f32, bf16 = jnp.float32, jnp.bfloat16


def piece(width, most):
    size = 128
    while size * 2 <= most and width % (size * 2) == 0:
        size *= 2
    return size


def window(index, size):
    return pl.ds(pl.multiple_of(index * size, 128), size)


def call(body, outs, ins, limit, scratch=(), moved=2 * MIB):
    return pl.pallas_call(
        body,
        out_shape=outs,
        in_specs=ins,
        out_specs=[VMEM] * len(outs),
        scratch_shapes=list(scratch),
        compiler_params=pltpu.CompilerParams(vmem_limit_bytes=limit * MIB),
        cost_estimate=pl.CostEstimate(flops=0, bytes_accessed=moved, transcendentals=0),
    )


def normal(hidden, gain, shift):
    wide = hidden.astype(f32)
    mean = jnp.mean(wide, axis=-1, keepdims=True)
    centred = wide - mean
    variance = jnp.mean(centred * centred, axis=-1, keepdims=True)
    return (centred * lax.rsqrt(variance + 1e-05) * gain + shift).astype(bf16)


def normalise(held, gain, shift, out):
    rows = held[0].shape[0]
    for i in range(0, len(held), 2):
        pair = jnp.concatenate([h[...] for h in held[i : i + 2]], axis=0)
        out[i * rows : (i + 2) * rows, :] = normal(pair, gain[...], shift[...])


def load_body(count, *refs):
    srcs, dsts, sems = refs[:count], refs[count : 2 * count], refs[2 * count]
    copies = [pltpu.make_async_copy(srcs[i], dsts[i], sems.at[i]) for i in range(count)]
    for copy in copies:
        copy.start()
    for copy in copies:
        copy.wait()


def near_body(groups, place, *refs):
    held, (own, gains, shifts, near, keep, send, gain, shift, first, sems) = refs[: groups - 1], refs[groups - 1 :]
    pairs = ((own, first), (gains, gain), (shifts, shift))
    copies = [pltpu.make_async_copy(src, dst, sems.at[i]) for i, (src, dst) in enumerate(pairs)]
    for copy in copies:
        copy.start()
    for copy in copies:
        copy.wait()
    normalise((first, *held), gain, shift, near)
    span = keep.shape[1]
    chip = place[0] // 2
    keep[...] = near[:, window(chip, span)]
    send[...] = near[:, window(chip ^ 1, span)]


def far_body(groups, *refs):
    normalise(refs[:groups], *refs[groups:])


def down_body(place, keep, got, own, mate, total, message):
    share = own.shape[0]
    core = place[0] % 2
    columns = jnp.concatenate([keep[...].astype(f32), got[...].astype(f32)], axis=0)
    low, high = columns[:, :share], columns[:, share:]
    mine = jnp.where(core == 0, low, high).astype(bf16)
    other = jnp.where(core == 0, high, low).astype(bf16)
    sums = jnp.dot(mine, own[...], preferred_element_type=f32) + jnp.dot(
        other, mate[...], preferred_element_type=f32
    )
    half = keep.shape[0]
    total[...] = sums
    message[:half, :] = sums[half:].astype(bf16)
    message[half:, :] = sums[:half].astype(bf16)


def turn(x, groups, bit):
    rows = x.shape[0] // (2 * groups)
    at = [h * groups + (k ^ bit) for h in range(2) for k in range(groups)]
    return jnp.concatenate([x[i * rows : (i + 1) * rows] for i in at], axis=0)


def merge_body(groups, total, got, out, *messages):
    sums = total[...] + got[...].astype(f32)
    out[...] = sums
    for k in range(1, groups):
        messages[k - 1][...] = turn(sums, groups, k).astype(bf16)


def up_body(groups, place, total, bias, own, mate, part, *refs):
    got, outs = refs[: groups - 1], refs[groups - 1 :]
    sums = total[...]
    for g in got:
        sums = sums + g[...].astype(f32)
    hidden = jnp.maximum(sums + bias[...], 0.0).astype(bf16)
    core = place[0] % 2
    mine = jnp.dot(hidden, own[...], preferred_element_type=f32)
    other = jnp.dot(hidden, mate[...], preferred_element_type=f32)
    both = jnp.concatenate([jnp.where(core == 0, mine, other), jnp.where(core == 0, other, mine)], axis=1)
    at = window(place[0] // 2, both.shape[1])
    rows = outs[0].shape[0]
    for q in range(2 * groups):
        some = slice(q * rows, (q + 1) * rows)
        outs[q][...] = part[some, :].astype(outs[q].dtype)
        outs[q][:, at] = (part[some, at] + both[some]).astype(outs[q].dtype)


def last_body(groups, *refs):
    sums, out = refs[:groups], refs[groups]
    total = sums[0][...]
    for k in range(1, groups):
        total = total + sums[k][...].astype(f32)
    out[...] = total.astype(bf16)


def act_body(step, near, far, w_own, w_mate, b_own, b_mate, mask, out):
    total = jnp.zeros(out.shape, f32)
    for i in range(near.shape[1] // step):
        at = slice(i * step, (i + 1) * step)
        rows = jnp.concatenate([near[:, at], far[:, at]], axis=0)
        both = jnp.concatenate([w_own[at, :], w_mate[at, :]], axis=1)
        total = total + jnp.dot(rows, both, preferred_element_type=f32)
    bias = jnp.concatenate([b_own[...], b_mate[...]], axis=1)
    out[...] = (jnp.maximum(total + bias, 0.0) * mask[...]).astype(bf16)


def part_body(step, act, w_own, w_mate, out):
    for i in range(out.shape[1] // step):
        at = slice(i * step, (i + 1) * step)
        both = jnp.concatenate([w_own[:, at], w_mate[:, at]], axis=0)
        out[:, at] = jnp.dot(act[...], both, preferred_element_type=f32)


def activity(lists, counts, block_slot):
    groups, top = lists.shape
    nblocks = block_slot.shape[0]
    names = jnp.arange(nblocks, dtype=jnp.int32)
    live = (jnp.arange(top, dtype=jnp.int32)[None, :] < counts[:, None]).astype(jnp.int32)
    hits = (lists[:, :, None] == names[None, None, :]).astype(jnp.int32) * live[:, :, None]
    by_block = jnp.sum(hits, axis=1)
    placed = (block_slot[:, None] == names[None, :]).astype(jnp.int32)
    return jnp.sum(by_block[:, :, None] * placed[None, :, :], axis=1)


def shards(
    hidden,
    ln_gain,
    ln_shift,
    lists,
    counts,
    block_slot,
    w_in,
    b_in,
    w_out,
    low_in,
    low_bias,
    low_out,
):
    devices = lax.axis_size("blk")
    position = lax.axis_index("blk")
    row_dev, width = hidden.shape
    groups = lists.shape[0]
    share, rank = low_in.shape
    block = w_in.shape[1]
    assert devices == 4 * groups
    plane = position // 4
    place = jnp.reshape(position, (1,)).astype(jnp.int32)
    some, rows = groups * row_dev, 2 * groups * row_dev

    def across(x, k):
        return lax.ppermute(x, "blk", [(i, i ^ (4 * k)) for i in range(devices)])

    def beside(x):
        return lax.ppermute(x, "blk", [(i, i ^ 2) for i in range(devices)])

    def core(x):
        return lax.ppermute(x, "blk", [(i, i ^ 1) for i in range(devices)])

    def shape(*dims, dtype=bf16):
        return jax.ShapeDtypeStruct(dims, dtype)

    gain, shift, bias = ln_gain.reshape(1, width), ln_shift.reshape(1, width), b_in.reshape(1, block)
    span = 2 * share

    table = activity(lists, counts, block_slot)
    by = plane ^ jnp.arange(groups)
    at = position ^ jnp.arange(2)
    relate = (by[:, None] == jnp.arange(groups)[None, :])[:, None, :, None]
    choose = (at[:, None] == jnp.arange(devices)[None, :])[None, :, None, :]
    live = jnp.sum(jnp.where(relate & choose, table[None, None], 0), axis=(2, 3)).astype(f32)
    mask = jnp.broadcast_to(live[None, :, None, :, None], (2, groups, row_dev, 2, block)).reshape(rows, 2 * block)

    held = [hidden] + [across(hidden, k) for k in range(groups - 1, 0, -1)][::-1]
    w_in_mate = core(w_in)
    near = (low_in, w_in, w_out, low_out)
    *near, mask = lax.optimization_barrier((*near, mask))
    loaded = call(
        functools.partial(load_body, len(near)),
        [shape(*x.shape, dtype=x.dtype) for x in near],
        [HBM] * len(near),
        16,
        [pltpu.SemaphoreType.DMA((len(near),))],
        8 * MIB,
    )(*[pltpu.with_memory_space_constraint(x, pltpu.HBM) for x in near])
    first, *loaded = lax.optimization_barrier((hidden, *loaded))
    low_in_near, w_in, w_out_near, low_out_near = loaded
    beyond = [beside(first), beside(held[1])]
    *_, w_in_mate, mask, low_in_sent, w_out_sent = lax.optimization_barrier(
        (*held, *beyond, w_in_mate, mask, low_in, w_out)
    )
    low_in_mate, w_out_mate = core(low_in_sent), core(w_out_sent)

    own, *beyond = lax.optimization_barrier((hidden, *beyond))
    normed, keep, send, gain, shift = call(
        functools.partial(near_body, groups),
        [shape(some, width), shape(some, span), shape(some, span)] + [shape(1, width, dtype=f32)] * 2,
        [SMEM] + [VMEM] * (groups - 1) + [HBM] * 3,
        16,
        [pltpu.VMEM((row_dev, width), bf16), pltpu.SemaphoreType.DMA((3,))],
        4 * MIB,
    )(place, *held[1:], *[pltpu.with_memory_space_constraint(x, pltpu.HBM) for x in (own, gain, shift)])
    send, bias_sent = lax.optimization_barrier((send, bias))
    got, bias_mate, *late = lax.optimization_barrier((beside(send), core(bias_sent), *held[2:]))
    beyond = beyond + [beside(h) for h in late]
    total, message = call(
        down_body, [shape(rows, rank, dtype=f32), shape(rows, rank)], [SMEM] + [VMEM] * 4, 16
    )(place, keep, got, low_in_near, low_in_mate)
    far = call(
        functools.partial(far_body, groups), [shape(some, width)], [VMEM] * (groups + 2), 16, (), 4 * MIB
    )(*beyond, gain, shift)[0]
    got, low_out_sent, w_out_mate, *beyond = lax.optimization_barrier((beside(message), low_out, w_out_mate, *beyond))
    low_out_mate = core(low_out_sent)
    step = piece(width, 2048)
    act = call(
        functools.partial(act_body, step),
        [shape(rows, 2 * block)],
        [VMEM] * 7,
        16,
        (),
        4 * MIB,
    )(normed, far, w_in, w_in_mate, bias, bias_mate, mask)[0]
    total, *messages = call(
        functools.partial(merge_body, groups),
        [shape(rows, rank, dtype=f32)] + [shape(rows, rank)] * (groups - 1),
        [VMEM] * 2,
        16,
    )(total, got)
    got = [across(messages[k - 1], k) for k in range(groups - 1, 0, -1)]
    part = call(
        functools.partial(part_body, step),
        [shape(rows, width, dtype=f32)],
        [VMEM] * 3,
        16,
        (),
        6 * MIB,
    )(act, w_out_near, w_out_mate)[0]
    parts = call(
        functools.partial(up_body, groups),
        [shape(row_dev, width, dtype=f32)] * groups + [shape(row_dev, width)] * groups,
        [SMEM] + [VMEM] * (groups + 4),
        16,
        (),
        6 * MIB,
    )(place, total, low_bias.reshape(1, rank), low_out_near, low_out_mate, part, *got)

    sums, here = [None] * groups, None
    for k in range(groups - 1, -1, -1):
        come = beside(parts[groups + k])
        if here is not None:
            come, here = lax.optimization_barrier((come, here))
            sums[k + 1] = across(here, k + 1)
        here = parts[k] + come.astype(f32)
        here = here.astype(bf16) if k else here
    sums[0] = here
    return call(functools.partial(last_body, groups), [shape(row_dev, width)], [VMEM] * groups, 16)(*sums)[0]


def solution(mesh):
    return jax.shard_map(
        shards,
        mesh=mesh,
        in_specs=(
            P(("rep", "blk"), None),
            P(),
            P(),
            P("rep", None),
            P("rep"),
            P(),
            P(None, "blk"),
            P("blk"),
            P("blk", None),
            P("blk", None),
            P(),
            P(None, "blk"),
        ),
        out_specs=P(("rep", "blk"), None),
        check_vma=False,
    )
```

```python
import functools

import jax
import jax.numpy as jnp
from jax import lax
from jax.experimental import pallas as pl
from jax.experimental.pallas import tpu as pltpu
from jax.sharding import PartitionSpec as P

MIB = 1 << 20
VMEM = pl.BlockSpec(memory_space=pltpu.VMEM)
HBM = pl.BlockSpec(memory_space=pltpu.HBM)
SMEM = pl.BlockSpec(memory_space=pltpu.SMEM)
f32, bf16 = jnp.float32, jnp.bfloat16


def piece(width, most):
    size = 128
    while size * 2 <= most and width % (size * 2) == 0:
        size *= 2
    return size


def window(index, size):
    return pl.ds(pl.multiple_of(index * size, 128), size)


def call(body, outs, ins, limit, scratch=(), moved=2 * MIB):
    return pl.pallas_call(
        body,
        out_shape=outs,
        in_specs=ins,
        out_specs=[VMEM] * len(outs),
        scratch_shapes=list(scratch),
        compiler_params=pltpu.CompilerParams(vmem_limit_bytes=limit * MIB),
        cost_estimate=pl.CostEstimate(flops=0, bytes_accessed=moved, transcendentals=0),
    )


def normal(hidden, gain, shift):
    wide = hidden.astype(f32)
    mean = jnp.mean(wide, axis=-1, keepdims=True)
    centred = wide - mean
    variance = jnp.mean(centred * centred, axis=-1, keepdims=True)
    return (centred * lax.rsqrt(variance + 1e-05) * gain + shift).astype(bf16)


def load_body(count, *refs):
    srcs, dsts, sems = refs[:count], refs[count : 2 * count], refs[2 * count]
    copies = [pltpu.make_async_copy(srcs[i], dsts[i], sems.at[i]) for i in range(count)]
    for copy in copies:
        copy.start()
    for copy in copies:
        copy.wait()


def early_body(groups, soon, *refs):
    held, (gain, shift, near, far) = refs[: groups + soon], refs[groups + soon :]
    rows = held[0].shape[0]
    for out, some in ((near, held[:groups]), (far, held[groups:])):
        for i in range(0, len(some), 2):
            pair = jnp.concatenate([h[...] for h in some[i : i + 2]], axis=0)
            out[i * rows : i * rows + pair.shape[0], :] = normal(pair, gain[...], shift[...])


def norm_body(groups, count, step, place, *refs):
    held, (near, first, gain, shift, own, mate, far, total, *messages) = refs[:count], refs[count:]
    rows, done = held[0].shape[0], first.shape[0]
    far[:done, :] = first[...]
    for i in range(0, count, 2):
        pair = jnp.concatenate([h[...] for h in held[i : i + 2]], axis=0)
        far[done + i * rows : done + i * rows + pair.shape[0], :] = normal(pair, gain[...], shift[...])
    share = own.shape[0]
    core = place[0] % 2
    at = window(place[0] // 2, 2 * share)
    columns = jnp.concatenate([near[:, at].astype(f32), far[:, at].astype(f32)], axis=0)
    low, high = columns[:, :share], columns[:, share:]
    mine = jnp.where(core == 0, low, high).astype(bf16)
    other = jnp.where(core == 0, high, low).astype(bf16)
    sums = jnp.dot(mine, own[...], preferred_element_type=f32) + jnp.dot(
        other, mate[...], preferred_element_type=f32
    )
    write(sums, groups, step, total, messages)


def stages(groups):
    bits = [(1, 0)]
    while 1 << (len(bits) - 1) < groups:
        bits.append((0, 1 << (len(bits) - 1)))
    steps = []
    for i in range(0, len(bits), 2):
        step = list(bits[i : i + 2])
        if len(step) == 2:
            step.append((step[0][0] ^ step[1][0], step[0][1] ^ step[1][1]))
        steps.append(step)
    return steps


def write(sums, groups, step, total, messages):
    total[...] = sums
    rows = sums.shape[0] // (2 * groups)
    for (other, offset), message in zip(step, messages):
        at = [(h ^ other) * groups + (k ^ offset) for h in range(2) for k in range(groups)]
        message[...] = jnp.concatenate([sums[i * rows : (i + 1) * rows] for i in at], axis=0).astype(bf16)


def merge_body(groups, count, step, *refs):
    sums = refs[0][...]
    for got in refs[1 : count + 1]:
        sums = sums + got[...].astype(f32)
    write(sums, groups, step, refs[count + 1], refs[count + 2 :])


def up_body(groups, count, place, total, bias, own, mate, part, *refs):
    got, outs = refs[:count], refs[count:]
    sums = total[...]
    for g in got:
        sums = sums + g[...].astype(f32)
    hidden = jnp.maximum(sums + bias[...], 0.0).astype(bf16)
    core = place[0] % 2
    mine = jnp.dot(hidden, own[...], preferred_element_type=f32)
    other = jnp.dot(hidden, mate[...], preferred_element_type=f32)
    both = jnp.concatenate([jnp.where(core == 0, mine, other), jnp.where(core == 0, other, mine)], axis=1)
    at = window(place[0] // 2, both.shape[1])
    rows = outs[0].shape[0]
    for q in range(2 * groups):
        some = slice(q * rows, (q + 1) * rows)
        outs[q][...] = part[some, :].astype(outs[q].dtype)
        outs[q][:, at] = (part[some, at] + both[some]).astype(outs[q].dtype)


def last_body(groups, *refs):
    sums, out = refs[:groups], refs[groups]
    total = sums[0][...]
    for k in range(1, groups):
        total = total + sums[k][...].astype(f32)
    out[...] = total.astype(bf16)


def act_body(step, near, far, w_own, w_mate, b_own, b_mate, mask, out):
    total = jnp.zeros(out.shape, f32)
    for i in range(near.shape[1] // step):
        at = slice(i * step, (i + 1) * step)
        rows = jnp.concatenate([near[:, at], far[:, at]], axis=0)
        both = jnp.concatenate([w_own[at, :], w_mate[at, :]], axis=1)
        total = total + jnp.dot(rows, both, preferred_element_type=f32)
    bias = jnp.concatenate([b_own[...], b_mate[...]], axis=1)
    out[...] = (jnp.maximum(total + bias, 0.0) * mask[...]).astype(bf16)


def part_body(step, act, w_own, w_mate, out):
    for i in range(out.shape[1] // step):
        at = slice(i * step, (i + 1) * step)
        both = jnp.concatenate([w_own[:, at], w_mate[:, at]], axis=0)
        out[:, at] = jnp.dot(act[...], both, preferred_element_type=f32)


def activity(lists, counts, block_slot):
    groups, top = lists.shape
    nblocks = block_slot.shape[0]
    names = jnp.arange(nblocks, dtype=jnp.int32)
    live = (jnp.arange(top, dtype=jnp.int32)[None, :] < counts[:, None]).astype(jnp.int32)
    hits = (lists[:, :, None] == names[None, None, :]).astype(jnp.int32) * live[:, :, None]
    by_block = jnp.sum(hits, axis=1)
    placed = (block_slot[:, None] == names[None, :]).astype(jnp.int32)
    return jnp.sum(by_block[:, :, None] * placed[None, :, :], axis=1)


def shards(
    hidden,
    ln_gain,
    ln_shift,
    lists,
    counts,
    block_slot,
    w_in,
    b_in,
    w_out,
    low_in,
    low_bias,
    low_out,
):
    devices = lax.axis_size("blk")
    position = lax.axis_index("blk")
    row_dev, width = hidden.shape
    groups = lists.shape[0]
    share, rank = low_in.shape
    block = w_in.shape[1]
    assert devices == 4 * groups
    plane = position // 4
    place = jnp.reshape(position, (1,)).astype(jnp.int32)
    some, rows = groups * row_dev, 2 * groups * row_dev

    def across(x, k):
        return lax.ppermute(x, "blk", [(i, i ^ (4 * k)) for i in range(devices)])

    def beside(x):
        return lax.ppermute(x, "blk", [(i, i ^ 2) for i in range(devices)])

    def core(x):
        return lax.ppermute(x, "blk", [(i, i ^ 1) for i in range(devices)])

    def shape(*dims, dtype=bf16):
        return jax.ShapeDtypeStruct(dims, dtype)

    gain, shift, bias = ln_gain.reshape(1, width), ln_shift.reshape(1, width), b_in.reshape(1, block)
    span = 2 * share

    table = activity(lists, counts, block_slot)
    by = plane ^ jnp.arange(groups)
    at = position ^ jnp.arange(2)
    relate = (by[:, None] == jnp.arange(groups)[None, :])[:, None, :, None]
    choose = (at[:, None] == jnp.arange(devices)[None, :])[None, :, None, :]
    live = jnp.sum(jnp.where(relate & choose, table[None, None], 0), axis=(2, 3)).astype(f32)
    mask = jnp.broadcast_to(live[None, :, None, :, None], (2, groups, row_dev, 2, block)).reshape(rows, 2 * block)

    held = [hidden] + [across(hidden, k) for k in range(groups - 1, 0, -1)][::-1]
    w_in_mate = core(w_in)
    held[1], low_in_sent, mask = lax.optimization_barrier((held[1], low_in, mask))
    low_in_mate = core(low_in_sent)
    beyond = [beside(h) for h in held]
    near = (hidden, gain, shift, low_in, w_in, w_out, low_out)
    *near, mask, beyond[0] = lax.optimization_barrier((*near, mask, beyond[0]))
    near = call(
        functools.partial(load_body, len(near)),
        [shape(*x.shape, dtype=x.dtype) for x in near],
        [HBM] * len(near),
        16,
        [pltpu.SemaphoreType.DMA((len(near),))],
        8 * MIB,
    )(*[pltpu.with_memory_space_constraint(x, pltpu.HBM) for x in near])
    hidden_near, gain, shift, low_in, w_in, w_out_near, low_out_near = near
    *_, w_in_mate, w_out_sent, low_out_sent, bias_sent = lax.optimization_barrier(
        (*held, *beyond[: groups // 2], w_in_mate, w_out, low_out, bias)
    )
    bias_mate, w_out_mate, low_out_mate = core(bias_sent), core(w_out_sent), core(low_out_sent)
    held[0] = hidden_near

    soon = groups // 2
    normed, first = call(
        functools.partial(early_body, groups, soon),
        [shape(some, width), shape(soon * row_dev, width)],
        [VMEM] * (groups + soon + 2),
        16,
        (),
        4 * MIB,
    )(*held, *beyond[:soon], gain, shift)
    steps = stages(groups)
    far, total, *messages = call(
        functools.partial(norm_body, groups, groups - soon, steps[0]),
        [shape(some, width), shape(rows, rank, dtype=f32)] + [shape(rows, rank)] * len(steps[0]),
        [SMEM] + [VMEM] * (groups - soon + 6),
        16,
        (),
        4 * MIB,
    )(place, *beyond[soon:], normed, first, gain, shift, low_in, low_in_mate)

    def swap(xs, step):
        pairs = [[(i, i ^ (2 * other) ^ (4 * offset)) for i in range(devices)] for other, offset in step]
        return [lax.ppermute(x, "blk", p) for x, p in zip(xs, pairs)]

    got = swap(messages, steps[0])
    step = piece(width, 2048)
    act = call(
        functools.partial(act_body, step),
        [shape(rows, 2 * block)],
        [VMEM] * 7,
        16,
        (),
        4 * MIB,
    )(normed, far, w_in, w_in_mate, bias, bias_mate, mask)[0]
    for before, after in zip(steps, steps[1:]):
        total, *messages = call(
            functools.partial(merge_body, groups, len(before), after),
            [shape(rows, rank, dtype=f32)] + [shape(rows, rank)] * len(after),
            [VMEM] * (1 + len(before)),
            16,
        )(total, *got)
        got = swap(messages, after)
    part = call(
        functools.partial(part_body, step),
        [shape(rows, width, dtype=f32)],
        [VMEM] * 3,
        16,
        (),
        6 * MIB,
    )(act, w_out_near, w_out_mate)[0]
    parts = call(
        functools.partial(up_body, groups, len(got)),
        [shape(row_dev, width, dtype=f32)] * groups + [shape(row_dev, width)] * groups,
        [SMEM] + [VMEM] * (len(got) + 5),
        16,
        (),
        6 * MIB,
    )(place, total, low_bias.reshape(1, rank), low_out_near, low_out_mate, part, *got)

    sums = []
    for k in range(groups - 1, -1, -1):
        here = parts[k] + beside(parts[groups + k]).astype(f32)
        sums.append(across(here.astype(bf16), k) if k else here)
    return call(functools.partial(last_body, groups), [shape(row_dev, width)], [VMEM] * groups, 16)(*sums[::-1])[0]


def solution(mesh):
    return jax.shard_map(
        shards,
        mesh=mesh,
        in_specs=(
            P(("rep", "blk"), None),
            P(),
            P(),
            P("rep", None),
            P("rep"),
            P(),
            P(None, "blk"),
            P("blk"),
            P("blk", None),
            P("blk", None),
            P(),
            P(None, "blk"),
        ),
        out_specs=P(("rep", "blk"), None),
        check_vma=False,
    )
```

```python
import functools

import jax
import jax.numpy as jnp
from jax import lax
from jax.experimental import pallas as pl
from jax.experimental.pallas import tpu as pltpu
from jax.sharding import PartitionSpec as P

MIB = 1 << 20
VMEM = pl.BlockSpec(memory_space=pltpu.VMEM)
HBM = pl.BlockSpec(memory_space=pltpu.HBM)
SMEM = pl.BlockSpec(memory_space=pltpu.SMEM)
f32, bf16 = jnp.float32, jnp.bfloat16


def piece(width, most):
    size = 128
    while size * 2 <= most and width % (size * 2) == 0:
        size *= 2
    return size


def window(index, size):
    return pl.ds(pl.multiple_of(index * size, 128), size)


def call(body, outs, ins, limit, scratch=(), moved=2 * MIB):
    return pl.pallas_call(
        body,
        out_shape=outs,
        in_specs=ins,
        out_specs=[VMEM] * len(outs),
        scratch_shapes=list(scratch),
        compiler_params=pltpu.CompilerParams(vmem_limit_bytes=limit * MIB),
        cost_estimate=pl.CostEstimate(flops=0, bytes_accessed=moved, transcendentals=0),
    )


def normal(hidden, gain, shift):
    wide = hidden.astype(f32)
    mean = jnp.mean(wide, axis=-1, keepdims=True)
    centred = wide - mean
    variance = jnp.mean(centred * centred, axis=-1, keepdims=True)
    return (centred * lax.rsqrt(variance + 1e-05) * gain + shift).astype(bf16)


def normalise(held, gain, shift, out):
    rows = held[0].shape[0]
    for i in range(0, len(held), 2):
        pair = jnp.concatenate([h[...] for h in held[i : i + 2]], axis=0)
        out[i * rows : (i + 2) * rows, :] = normal(pair, gain[...], shift[...])


def load_body(count, *refs):
    srcs, dsts, sems = refs[:count], refs[count : 2 * count], refs[2 * count]
    copies = [pltpu.make_async_copy(srcs[i], dsts[i], sems.at[i]) for i in range(count)]
    for copy in copies:
        copy.start()
    for copy in copies:
        copy.wait()


def near_body(groups, place, *refs):
    held, (gain, shift, near, keep, send) = refs[:groups], refs[groups:]
    normalise(held, gain, shift, near)
    span = keep.shape[1]
    chip = place[0] // 2
    keep[...] = near[:, window(chip, span)]
    send[...] = near[:, window(chip ^ 1, span)]


def far_body(groups, *refs):
    normalise(refs[:groups], *refs[groups:])


def down_body(place, keep, got, own, mate, total, message):
    share = own.shape[0]
    core = place[0] % 2
    columns = jnp.concatenate([keep[...].astype(f32), got[...].astype(f32)], axis=0)
    low, high = columns[:, :share], columns[:, share:]
    mine = jnp.where(core == 0, low, high).astype(bf16)
    other = jnp.where(core == 0, high, low).astype(bf16)
    sums = jnp.dot(mine, own[...], preferred_element_type=f32) + jnp.dot(
        other, mate[...], preferred_element_type=f32
    )
    half = keep.shape[0]
    total[...] = sums
    message[:half, :] = sums[half:].astype(bf16)
    message[half:, :] = sums[:half].astype(bf16)


def turn(x, groups, bit):
    rows = x.shape[0] // (2 * groups)
    at = [h * groups + (k ^ bit) for h in range(2) for k in range(groups)]
    return jnp.concatenate([x[i * rows : (i + 1) * rows] for i in at], axis=0)


def merge_body(groups, total, got, out, *messages):
    sums = total[...] + got[...].astype(f32)
    out[...] = sums
    for k in range(1, groups):
        messages[k - 1][...] = turn(sums, groups, k).astype(bf16)


def up_body(groups, place, total, bias, own, mate, part, *refs):
    got, outs = refs[: groups - 1], refs[groups - 1 :]
    sums = total[...]
    for g in got:
        sums = sums + g[...].astype(f32)
    hidden = jnp.maximum(sums + bias[...], 0.0).astype(bf16)
    core = place[0] % 2
    mine = jnp.dot(hidden, own[...], preferred_element_type=f32)
    other = jnp.dot(hidden, mate[...], preferred_element_type=f32)
    both = jnp.concatenate([jnp.where(core == 0, mine, other), jnp.where(core == 0, other, mine)], axis=1)
    at = window(place[0] // 2, both.shape[1])
    rows = outs[0].shape[0]
    for q in range(2 * groups):
        some = slice(q * rows, (q + 1) * rows)
        outs[q][...] = part[some, :].astype(outs[q].dtype)
        outs[q][:, at] = (part[some, at] + both[some]).astype(outs[q].dtype)


def last_body(groups, *refs):
    sums, out = refs[:groups], refs[groups]
    total = sums[0][...]
    for k in range(1, groups):
        total = total + sums[k][...].astype(f32)
    out[...] = total.astype(bf16)


def act_body(step, near, far, w_own, w_mate, b_own, b_mate, mask, out):
    total = jnp.zeros(out.shape, f32)
    for i in range(near.shape[1] // step):
        at = slice(i * step, (i + 1) * step)
        rows = jnp.concatenate([near[:, at], far[:, at]], axis=0)
        both = jnp.concatenate([w_own[at, :], w_mate[at, :]], axis=1)
        total = total + jnp.dot(rows, both, preferred_element_type=f32)
    bias = jnp.concatenate([b_own[...], b_mate[...]], axis=1)
    out[...] = (jnp.maximum(total + bias, 0.0) * mask[...]).astype(bf16)


def part_body(step, act, w_own, w_mate, out):
    for i in range(out.shape[1] // step):
        at = slice(i * step, (i + 1) * step)
        both = jnp.concatenate([w_own[:, at], w_mate[:, at]], axis=0)
        out[:, at] = jnp.dot(act[...], both, preferred_element_type=f32)


def activity(lists, counts, block_slot):
    groups, top = lists.shape
    nblocks = block_slot.shape[0]
    names = jnp.arange(nblocks, dtype=jnp.int32)
    live = (jnp.arange(top, dtype=jnp.int32)[None, :] < counts[:, None]).astype(jnp.int32)
    hits = (lists[:, :, None] == names[None, None, :]).astype(jnp.int32) * live[:, :, None]
    by_block = jnp.sum(hits, axis=1)
    placed = (block_slot[:, None] == names[None, :]).astype(jnp.int32)
    return jnp.sum(by_block[:, :, None] * placed[None, :, :], axis=1)


def shards(
    hidden,
    ln_gain,
    ln_shift,
    lists,
    counts,
    block_slot,
    w_in,
    b_in,
    w_out,
    low_in,
    low_bias,
    low_out,
):
    devices = lax.axis_size("blk")
    position = lax.axis_index("blk")
    row_dev, width = hidden.shape
    groups = lists.shape[0]
    share, rank = low_in.shape
    block = w_in.shape[1]
    assert devices == 4 * groups
    plane = position // 4
    place = jnp.reshape(position, (1,)).astype(jnp.int32)
    some, rows = groups * row_dev, 2 * groups * row_dev

    def across(x, k):
        return lax.ppermute(x, "blk", [(i, i ^ (4 * k)) for i in range(devices)])

    def beside(x):
        return lax.ppermute(x, "blk", [(i, i ^ 2) for i in range(devices)])

    def core(x):
        return lax.ppermute(x, "blk", [(i, i ^ 1) for i in range(devices)])

    def shape(*dims, dtype=bf16):
        return jax.ShapeDtypeStruct(dims, dtype)

    gain, shift, bias = ln_gain.reshape(1, width), ln_shift.reshape(1, width), b_in.reshape(1, block)
    span = 2 * share

    table = activity(lists, counts, block_slot)
    by = plane ^ jnp.arange(groups)
    at = position ^ jnp.arange(2)
    relate = (by[:, None] == jnp.arange(groups)[None, :])[:, None, :, None]
    choose = (at[:, None] == jnp.arange(devices)[None, :])[None, :, None, :]
    live = jnp.sum(jnp.where(relate & choose, table[None, None], 0), axis=(2, 3)).astype(f32)
    mask = jnp.broadcast_to(live[None, :, None, :, None], (2, groups, row_dev, 2, block)).reshape(rows, 2 * block)

    held = [hidden] + [across(hidden, k) for k in range(1, groups)]
    w_in_mate = core(w_in)
    near = (hidden, gain, shift, low_in, w_in, w_out, low_out)
    *near, mask = lax.optimization_barrier((*near, mask))
    near = call(
        functools.partial(load_body, len(near)),
        [shape(*x.shape, dtype=x.dtype) for x in near],
        [HBM] * len(near),
        16,
        [pltpu.SemaphoreType.DMA((len(near),))],
        8 * MIB,
    )(*[pltpu.with_memory_space_constraint(x, pltpu.HBM) for x in near])
    beyond = [beside(hidden)]
    *_, w_in_mate, low_in_sent, w_out_sent = lax.optimization_barrier(
        (*held, *near, *beyond, w_in_mate, low_in, w_out)
    )
    hidden_near, gain, shift, low_in_near, w_in, w_out_near, low_out_near = near
    low_in_mate, w_out_mate = core(low_in_sent), core(w_out_sent)
    hidden_near, *beyond = lax.optimization_barrier((hidden_near, *beyond))
    normed, keep, send = call(
        functools.partial(near_body, groups),
        [shape(some, width), shape(some, span), shape(some, span)],
        [SMEM] + [VMEM] * (groups + 2),
        16,
        (),
        4 * MIB,
    )(place, hidden_near, *held[1:], gain, shift)
    send, bias_sent, *late = lax.optimization_barrier((send, bias, *held[2:]))
    beyond.append(beside(held[1]))
    got, bias_mate, beyond[1] = lax.optimization_barrier((beside(send), core(bias_sent), beyond[1]))
    beyond = beyond + [beside(h) for h in late]
    total, message = call(
        down_body, [shape(rows, rank, dtype=f32), shape(rows, rank)], [SMEM] + [VMEM] * 4, 16
    )(place, keep, got, low_in_near, low_in_mate)
    far = call(
        functools.partial(far_body, groups), [shape(some, width)], [VMEM] * (groups + 2), 16, (), 4 * MIB
    )(*beyond, gain, shift)[0]
    got, w_out_mate, low_out_sent = lax.optimization_barrier((beside(message), w_out_mate, low_out))
    low_out_mate = core(low_out_sent)
    step = piece(width, 2048)
    act = call(
        functools.partial(act_body, step),
        [shape(rows, 2 * block)],
        [VMEM] * 7,
        16,
        (),
        4 * MIB,
    )(normed, far, w_in, w_in_mate, bias, bias_mate, mask)[0]
    total, *messages = call(
        functools.partial(merge_body, groups),
        [shape(rows, rank, dtype=f32)] + [shape(rows, rank)] * (groups - 1),
        [VMEM] * 2,
        16,
    )(total, got)
    got = [across(messages[k - 1], k) for k in range(groups - 1, 0, -1)]
    part = call(
        functools.partial(part_body, step),
        [shape(rows, width, dtype=f32)],
        [VMEM] * 3,
        16,
        (),
        6 * MIB,
    )(act, w_out_near, w_out_mate)[0]
    parts = call(
        functools.partial(up_body, groups),
        [shape(row_dev, width, dtype=f32)] * groups + [shape(row_dev, width)] * groups,
        [SMEM] + [VMEM] * (groups + 4),
        16,
        (),
        6 * MIB,
    )(place, total, low_bias.reshape(1, rank), low_out_near, low_out_mate, part, *got)

    sums, here, mark = [], None, None
    for k in range(groups - 1, -1, -1):
        mine = parts[groups + k]
        if k == 0:
            mine, _ = lax.optimization_barrier((mine, mark))
        come = beside(mine)
        if here is not None:
            come, _ = lax.optimization_barrier((come, here))
        here = parts[k] + come.astype(f32)
        here = here.astype(bf16) if k else here
        mark = here if k == groups // 2 else mark
        sums.append(across(here, k) if k else here)
    return call(functools.partial(last_body, groups), [shape(row_dev, width)], [VMEM] * groups, 16)(*sums[::-1])[0]


def solution(mesh):
    return jax.shard_map(
        shards,
        mesh=mesh,
        in_specs=(
            P(("rep", "blk"), None),
            P(),
            P(),
            P("rep", None),
            P("rep"),
            P(),
            P(None, "blk"),
            P("blk"),
            P("blk", None),
            P("blk", None),
            P(),
            P(None, "blk"),
        ),
        out_specs=P(("rep", "blk"), None),
        check_vma=False,
    )
```

```python
import functools

import jax
import jax.numpy as jnp
from jax import lax
from jax.experimental import pallas as pl
from jax.experimental.pallas import tpu as pltpu
from jax.sharding import PartitionSpec as P

MIB = 1 << 20
VMEM = pl.BlockSpec(memory_space=pltpu.VMEM)
HBM = pl.BlockSpec(memory_space=pltpu.HBM)
SMEM = pl.BlockSpec(memory_space=pltpu.SMEM)
f32, bf16 = jnp.float32, jnp.bfloat16


def piece(width, most):
    size = 128
    while size * 2 <= most and width % (size * 2) == 0:
        size *= 2
    return size


def window(index, size):
    return pl.ds(pl.multiple_of(index * size, 128), size)


def call(body, outs, ins, limit, scratch=(), moved=2 * MIB):
    return pl.pallas_call(
        body,
        out_shape=outs,
        in_specs=ins,
        out_specs=[VMEM] * len(outs),
        scratch_shapes=list(scratch),
        compiler_params=pltpu.CompilerParams(vmem_limit_bytes=limit * MIB),
        cost_estimate=pl.CostEstimate(flops=0, bytes_accessed=moved, transcendentals=0),
    )


def normal(hidden, gain, shift):
    wide = hidden.astype(f32)
    mean = jnp.mean(wide, axis=-1, keepdims=True)
    centred = wide - mean
    variance = jnp.mean(centred * centred, axis=-1, keepdims=True)
    return (centred * lax.rsqrt(variance + 1e-05) * gain + shift).astype(bf16)


def normalise(held, gain, shift, out):
    rows = held[0].shape[0]
    for i in range(0, len(held), 2):
        pair = jnp.concatenate([h[...] for h in held[i : i + 2]], axis=0)
        out[i * rows : (i + 2) * rows, :] = normal(pair, gain[...], shift[...])


def load_body(count, *refs):
    srcs, dsts, sems = refs[:count], refs[count : 2 * count], refs[2 * count]
    copies = [pltpu.make_async_copy(srcs[i], dsts[i], sems.at[i]) for i in range(count)]
    for copy in copies:
        copy.start()
    for copy in copies:
        copy.wait()


def near_body(groups, place, *refs):
    held, (gain, shift, near, keep, send) = refs[:groups], refs[groups:]
    normalise(held, gain, shift, near)
    span = keep.shape[1]
    chip = place[0] // 2
    keep[...] = near[:, window(chip, span)]
    send[...] = near[:, window(chip ^ 1, span)]


def far_body(groups, *refs):
    normalise(refs[:groups], *refs[groups:])


def down_body(place, keep, got, own, mate, total, message):
    share = own.shape[0]
    core = place[0] % 2
    columns = jnp.concatenate([keep[...].astype(f32), got[...].astype(f32)], axis=0)
    low, high = columns[:, :share], columns[:, share:]
    mine = jnp.where(core == 0, low, high).astype(bf16)
    other = jnp.where(core == 0, high, low).astype(bf16)
    sums = jnp.dot(mine, own[...], preferred_element_type=f32) + jnp.dot(
        other, mate[...], preferred_element_type=f32
    )
    half = keep.shape[0]
    total[...] = sums
    message[:half, :] = sums[half:].astype(bf16)
    message[half:, :] = sums[:half].astype(bf16)


def turn(x, groups, bit):
    rows = x.shape[0] // (2 * groups)
    at = [h * groups + (k ^ bit) for h in range(2) for k in range(groups)]
    return jnp.concatenate([x[i * rows : (i + 1) * rows] for i in at], axis=0)


def merge_body(groups, total, got, out, *messages):
    sums = total[...] + got[...].astype(f32)
    out[...] = sums
    for k in range(1, groups):
        messages[k - 1][...] = turn(sums, groups, k).astype(bf16)


def up_body(groups, place, total, bias, own, mate, part, *refs):
    got, outs = refs[: groups - 1], refs[groups - 1 :]
    sums = total[...]
    for g in got:
        sums = sums + g[...].astype(f32)
    hidden = jnp.maximum(sums + bias[...], 0.0).astype(bf16)
    core = place[0] % 2
    mine = jnp.dot(hidden, own[...], preferred_element_type=f32)
    other = jnp.dot(hidden, mate[...], preferred_element_type=f32)
    both = jnp.concatenate([jnp.where(core == 0, mine, other), jnp.where(core == 0, other, mine)], axis=1)
    at = window(place[0] // 2, both.shape[1])
    rows = outs[0].shape[0]
    for q in range(2 * groups):
        some = slice(q * rows, (q + 1) * rows)
        outs[q][...] = part[some, :].astype(outs[q].dtype)
        outs[q][:, at] = (part[some, at] + both[some]).astype(outs[q].dtype)


def last_body(groups, *refs):
    sums, out = refs[:groups], refs[groups]
    total = sums[0][...]
    for k in range(1, groups):
        total = total + sums[k][...].astype(f32)
    out[...] = total.astype(bf16)


def act_body(step, near, far, w_own, w_mate, b_own, b_mate, mask, out):
    total = jnp.zeros(out.shape, f32)
    for i in range(near.shape[1] // step):
        at = slice(i * step, (i + 1) * step)
        rows = jnp.concatenate([near[:, at], far[:, at]], axis=0)
        both = jnp.concatenate([w_own[at, :], w_mate[at, :]], axis=1)
        total = total + jnp.dot(rows, both, preferred_element_type=f32)
    bias = jnp.concatenate([b_own[...], b_mate[...]], axis=1)
    out[...] = (jnp.maximum(total + bias, 0.0) * mask[...]).astype(bf16)


def part_body(step, act, w_own, w_mate, out):
    for i in range(out.shape[1] // step):
        at = slice(i * step, (i + 1) * step)
        both = jnp.concatenate([w_own[:, at], w_mate[:, at]], axis=0)
        out[:, at] = jnp.dot(act[...], both, preferred_element_type=f32)


def activity(lists, counts, block_slot):
    groups, top = lists.shape
    nblocks = block_slot.shape[0]
    names = jnp.arange(nblocks, dtype=jnp.int32)
    live = (jnp.arange(top, dtype=jnp.int32)[None, :] < counts[:, None]).astype(jnp.int32)
    hits = (lists[:, :, None] == names[None, None, :]).astype(jnp.int32) * live[:, :, None]
    by_block = jnp.sum(hits, axis=1)
    placed = (block_slot[:, None] == names[None, :]).astype(jnp.int32)
    return jnp.sum(by_block[:, :, None] * placed[None, :, :], axis=1)


def shards(
    hidden,
    ln_gain,
    ln_shift,
    lists,
    counts,
    block_slot,
    w_in,
    b_in,
    w_out,
    low_in,
    low_bias,
    low_out,
):
    devices = lax.axis_size("blk")
    position = lax.axis_index("blk")
    row_dev, width = hidden.shape
    groups = lists.shape[0]
    share, rank = low_in.shape
    block = w_in.shape[1]
    assert devices == 4 * groups
    plane = position // 4
    place = jnp.reshape(position, (1,)).astype(jnp.int32)
    some, rows = groups * row_dev, 2 * groups * row_dev

    def across(x, k):
        return lax.ppermute(x, "blk", [(i, i ^ (4 * k)) for i in range(devices)])

    def beside(x):
        return lax.ppermute(x, "blk", [(i, i ^ 2) for i in range(devices)])

    def core(x):
        return lax.ppermute(x, "blk", [(i, i ^ 1) for i in range(devices)])

    def shape(*dims, dtype=bf16):
        return jax.ShapeDtypeStruct(dims, dtype)

    gain, shift, bias = ln_gain.reshape(1, width), ln_shift.reshape(1, width), b_in.reshape(1, block)
    span = 2 * share

    table = activity(lists, counts, block_slot)
    by = plane ^ jnp.arange(groups)
    at = position ^ jnp.arange(2)
    relate = (by[:, None] == jnp.arange(groups)[None, :])[:, None, :, None]
    choose = (at[:, None] == jnp.arange(devices)[None, :])[None, :, None, :]
    live = jnp.sum(jnp.where(relate & choose, table[None, None], 0), axis=(2, 3)).astype(f32)
    mask = jnp.broadcast_to(live[None, :, None, :, None], (2, groups, row_dev, 2, block)).reshape(rows, 2 * block)

    held = [hidden] + [across(hidden, k) for k in range(1, groups)]
    w_in_mate = core(w_in)
    near = (hidden, gain, shift, low_in, w_in, w_out, low_out)
    *near, mask = lax.optimization_barrier((*near, mask))
    near = call(
        functools.partial(load_body, len(near)),
        [shape(*x.shape, dtype=x.dtype) for x in near],
        [HBM] * len(near),
        16,
        [pltpu.SemaphoreType.DMA((len(near),))],
        8 * MIB,
    )(*[pltpu.with_memory_space_constraint(x, pltpu.HBM) for x in near])
    early, bias_mate = lax.optimization_barrier((hidden, core(bias)))
    beyond = [beside(early)]
    *_, w_in_mate, low_in_sent, w_out_sent = lax.optimization_barrier(
        (*held, *near, *beyond, w_in_mate, low_in, w_out)
    )
    hidden_near, gain, shift, low_in_near, w_in, w_out_near, low_out_near = near
    low_in_mate, w_out_mate = core(low_in_sent), core(w_out_sent)
    hidden_near, *beyond = lax.optimization_barrier((hidden_near, *beyond))
    normed, keep, send = call(
        functools.partial(near_body, groups),
        [shape(some, width), shape(some, span), shape(some, span)],
        [SMEM] + [VMEM] * (groups + 2),
        16,
        (),
        4 * MIB,
    )(place, hidden_near, *held[1:], gain, shift)
    send, *late = lax.optimization_barrier((send, *held[2:]))
    beyond.append(beside(held[1]))
    got, beyond[1] = lax.optimization_barrier((beside(send), beyond[1]))
    beyond = beyond + [beside(h) for h in late]
    total, message = call(
        down_body, [shape(rows, rank, dtype=f32), shape(rows, rank)], [SMEM] + [VMEM] * 4, 16
    )(place, keep, got, low_in_near, low_in_mate)
    far = call(
        functools.partial(far_body, groups), [shape(some, width)], [VMEM] * (groups + 2), 16, (), 4 * MIB
    )(*beyond, gain, shift)[0]
    got, w_out_mate, low_out_sent = lax.optimization_barrier((beside(message), w_out_mate, low_out))
    low_out_mate = core(low_out_sent)
    step = piece(width, 2048)
    act = call(
        functools.partial(act_body, step),
        [shape(rows, 2 * block)],
        [VMEM] * 7,
        16,
        (),
        4 * MIB,
    )(normed, far, w_in, w_in_mate, bias, bias_mate, mask)[0]
    total, *messages = call(
        functools.partial(merge_body, groups),
        [shape(rows, rank, dtype=f32)] + [shape(rows, rank)] * (groups - 1),
        [VMEM] * 2,
        16,
    )(total, got)
    got = [across(messages[k - 1], k) for k in range(groups - 1, 0, -1)]
    part = call(
        functools.partial(part_body, step),
        [shape(rows, width, dtype=f32)],
        [VMEM] * 3,
        16,
        (),
        6 * MIB,
    )(act, w_out_near, w_out_mate)[0]
    parts = call(
        functools.partial(up_body, groups),
        [shape(row_dev, width, dtype=f32)] * groups + [shape(row_dev, width)] * groups,
        [SMEM] + [VMEM] * (groups + 4),
        16,
        (),
        6 * MIB,
    )(place, total, low_bias.reshape(1, rank), low_out_near, low_out_mate, part, *got)

    sums, here, mark = [], None, None
    for k in range(groups - 1, -1, -1):
        mine = parts[groups + k]
        if k == 0:
            mine, _ = lax.optimization_barrier((mine, mark))
        come = beside(mine)
        if here is not None:
            come, _ = lax.optimization_barrier((come, here))
        here = parts[k] + come.astype(f32)
        here = here.astype(bf16) if k else here
        mark = here if k == groups // 2 else mark
        sums.append(across(here, k) if k else here)
    return call(functools.partial(last_body, groups), [shape(row_dev, width)], [VMEM] * groups, 16)(*sums[::-1])[0]


def solution(mesh):
    return jax.shard_map(
        shards,
        mesh=mesh,
        in_specs=(
            P(("rep", "blk"), None),
            P(),
            P(),
            P("rep", None),
            P("rep"),
            P(),
            P(None, "blk"),
            P("blk"),
            P("blk", None),
            P("blk", None),
            P(),
            P(None, "blk"),
        ),
        out_specs=P(("rep", "blk"), None),
        check_vma=False,
    )
```

```python
import functools

import jax
import jax.numpy as jnp
from jax import lax
from jax.experimental import pallas as pl
from jax.experimental.pallas import tpu as pltpu
from jax.sharding import PartitionSpec as P

MIB = 1 << 20
VMEM = pl.BlockSpec(memory_space=pltpu.VMEM)
HBM = pl.BlockSpec(memory_space=pltpu.HBM)
SMEM = pl.BlockSpec(memory_space=pltpu.SMEM)
f32, bf16 = jnp.float32, jnp.bfloat16


def piece(width, most):
    size = 128
    while size * 2 <= most and width % (size * 2) == 0:
        size *= 2
    return size


def window(index, size):
    return pl.ds(pl.multiple_of(index * size, 128), size)


def call(body, outs, ins, limit, scratch=(), moved=2 * MIB):
    return pl.pallas_call(
        body,
        out_shape=outs,
        in_specs=ins,
        out_specs=[VMEM] * len(outs),
        scratch_shapes=list(scratch),
        compiler_params=pltpu.CompilerParams(vmem_limit_bytes=limit * MIB),
        cost_estimate=pl.CostEstimate(flops=0, bytes_accessed=moved, transcendentals=0),
    )


def normal(hidden, gain, shift):
    wide = hidden.astype(f32)
    mean = jnp.mean(wide, axis=-1, keepdims=True)
    centred = wide - mean
    variance = jnp.mean(centred * centred, axis=-1, keepdims=True)
    return (centred * lax.rsqrt(variance + 1e-05) * gain + shift).astype(bf16)


def load_body(count, *refs):
    srcs, dsts, sems = refs[:count], refs[count : 2 * count], refs[2 * count]
    copies = [pltpu.make_async_copy(srcs[i], dsts[i], sems.at[i]) for i in range(count)]
    for copy in copies:
        copy.start()
    for copy in copies:
        copy.wait()


def head_body(groups, place, hidden, gain, shift, out, *refs):
    strips, (rows, gains, shifts, sems) = refs[:groups], refs[groups:]
    pairs = ((hidden, rows), (gain, gains), (shift, shifts))
    copies = [pltpu.make_async_copy(src, dst, sems.at[i]) for i, (src, dst) in enumerate(pairs)]
    for copy in copies:
        copy.start()
    for copy in copies:
        copy.wait()
    out[...] = normal(rows[...], gains[...], shifts[...])
    span = strips[0].shape[1]
    for k in range(groups):
        strips[k][...] = out[:, window((place[0] // 4) ^ k, span)]


def sort_body(groups, place, *refs):
    strips, (keep, send) = refs[:groups], refs[groups:]
    span = keep.shape[1]
    upper = (place[0] // 2) % 2
    rows = jnp.concatenate([s[...].astype(f32) for s in strips], axis=0)
    low, high = rows[:, :span], rows[:, span:]
    keep[...] = jnp.where(upper == 0, low, high).astype(bf16)
    send[...] = jnp.where(upper == 0, high, low).astype(bf16)


def down_body(place, keep, got, own, mate, total, message):
    share = own.shape[0]
    core = place[0] % 2
    columns = jnp.concatenate([keep[...].astype(f32), got[...].astype(f32)], axis=0)
    low, high = columns[:, :share], columns[:, share:]
    mine = jnp.where(core == 0, low, high).astype(bf16)
    other = jnp.where(core == 0, high, low).astype(bf16)
    sums = jnp.dot(mine, own[...], preferred_element_type=f32) + jnp.dot(
        other, mate[...], preferred_element_type=f32
    )
    half = keep.shape[0]
    total[...] = sums
    message[:half, :] = sums[half:].astype(bf16)
    message[half:, :] = sums[:half].astype(bf16)


def turn(x, groups, bit):
    rows = x.shape[0] // (2 * groups)
    at = [h * groups + (k ^ bit) for h in range(2) for k in range(groups)]
    return jnp.concatenate([x[i * rows : (i + 1) * rows] for i in at], axis=0)


def merge_body(groups, total, got, out, *messages):
    sums = total[...] + got[...].astype(f32)
    out[...] = sums
    for k in range(1, groups):
        messages[k - 1][...] = turn(sums, groups, k).astype(bf16)


def up_body(groups, place, total, bias, own, mate, part, *refs):
    got, outs = refs[: groups - 1], refs[groups - 1 :]
    sums = total[...]
    for g in got:
        sums = sums + g[...].astype(f32)
    hidden = jnp.maximum(sums + bias[...], 0.0).astype(bf16)
    core = place[0] % 2
    mine = jnp.dot(hidden, own[...], preferred_element_type=f32)
    other = jnp.dot(hidden, mate[...], preferred_element_type=f32)
    both = jnp.concatenate([jnp.where(core == 0, mine, other), jnp.where(core == 0, other, mine)], axis=1)
    at = window(place[0] // 2, both.shape[1])
    rows = outs[0].shape[0]
    for q in range(2 * groups):
        some = slice(q * rows, (q + 1) * rows)
        outs[q][...] = part[some, :].astype(outs[q].dtype)
        outs[q][:, at] = (part[some, at] + both[some]).astype(outs[q].dtype)


def last_body(groups, *refs):
    sums, out = refs[:groups], refs[groups]
    total = sums[0][...]
    for k in range(1, groups):
        total = total + sums[k][...].astype(f32)
    out[...] = total.astype(bf16)


def act_body(groups, step, place, lists, counts, block_slot, *refs):
    x, (w_own, w_mate, b_own, b_mate, out) = refs[: 2 * groups], refs[2 * groups :]
    block, row_dev = w_own.shape[1], x[0].shape[0]
    total = jnp.zeros(out.shape, f32)
    for i in range(w_own.shape[0] // step):
        at = slice(i * step, (i + 1) * step)
        rows = jnp.concatenate([r[:, at] for r in x], axis=0)
        both = jnp.concatenate([w_own[at, :], w_mate[at, :]], axis=1)
        total = total + jnp.dot(rows, both, preferred_element_type=f32)
    bias = jnp.concatenate([b_own[...], b_mate[...]], axis=1)
    act = jnp.maximum(total + bias, 0.0)
    row_k = (lax.broadcasted_iota(jnp.int32, out.shape, 0) // row_dev) % groups
    column_b = lax.broadcasted_iota(jnp.int32, out.shape, 1) // block
    uses = jnp.zeros(out.shape, jnp.int32)
    for k in range(groups):
        group = (place[0] // 4) ^ k

        def hit(e, found):
            slot = block_slot[lists[group, e]]
            live = e < counts[group]
            own = jnp.where(live & (slot == place[0]), 1, 0)
            mate = jnp.where(live & (slot == place[0] ^ 1), 1, 0)
            return found[0] + own, found[1] + mate

        own, mate = lax.fori_loop(0, lists.shape[1], hit, (jnp.int32(0), jnp.int32(0)))
        uses = jnp.where(row_k == k, jnp.where(column_b == 0, own, mate), uses)
    out[...] = jnp.where(uses > 0, act, 0.0).astype(bf16)


def part_body(step, act, w_own, w_mate, out):
    for i in range(out.shape[1] // step):
        at = slice(i * step, (i + 1) * step)
        both = jnp.concatenate([w_own[:, at], w_mate[:, at]], axis=0)
        out[:, at] = jnp.dot(act[...], both, preferred_element_type=f32)


def shards(
    hidden,
    ln_gain,
    ln_shift,
    lists,
    counts,
    block_slot,
    w_in,
    b_in,
    w_out,
    low_in,
    low_bias,
    low_out,
):
    devices = lax.axis_size("blk")
    position = lax.axis_index("blk")
    row_dev, width = hidden.shape
    groups = lists.shape[0]
    share, rank = low_in.shape
    block = w_in.shape[1]
    assert devices == 4 * groups
    plane = position // 4
    place = jnp.reshape(position, (1,)).astype(jnp.int32)
    some, rows = groups * row_dev, 2 * groups * row_dev

    def across(x, k):
        return lax.ppermute(x, "blk", [(i, i ^ (4 * k)) for i in range(devices)])

    def beside(x):
        return lax.ppermute(x, "blk", [(i, i ^ 2) for i in range(devices)])

    def core(x):
        return lax.ppermute(x, "blk", [(i, i ^ 1) for i in range(devices)])

    def shape(*dims, dtype=bf16):
        return jax.ShapeDtypeStruct(dims, dtype)

    gain, shift, bias = ln_gain.reshape(1, width), ln_shift.reshape(1, width), b_in.reshape(1, block)
    span = 2 * share

    hbm = lambda *xs: [pltpu.with_memory_space_constraint(x, pltpu.HBM) for x in xs]
    normed, *strips = call(
        functools.partial(head_body, groups),
        [shape(row_dev, width)] + [shape(row_dev, 2 * span)] * groups,
        [SMEM] + [HBM] * 3,
        16,
        [
            pltpu.VMEM((row_dev, width), bf16),
            pltpu.VMEM((1, width), f32),
            pltpu.VMEM((1, width), f32),
            pltpu.SemaphoreType.DMA((3,)),
        ],
        4 * MIB,
    )(place, *hbm(hidden, gain, shift))

    low_in_mate, bias_mate = core(low_in), core(bias)
    *strips, low_in_mate, bias_mate = lax.optimization_barrier((*strips, low_in_mate, bias_mate))
    strips = [strips[0]] + [across(strips[k], k) for k in range(groups - 1, 0, -1)][::-1]
    normed_sent, *strips = lax.optimization_barrier((normed, *strips))
    held = [normed] + [across(normed_sent, k) for k in range(groups - 1, 0, -1)][::-1]
    beyond = [beside(h) for h in held]

    near = (low_in, w_in, w_out, low_out)
    low_in_near, w_in_near, w_out_near, low_out_near = call(
        functools.partial(load_body, len(near)),
        [shape(*x.shape, dtype=x.dtype) for x in near],
        [HBM] * len(near),
        16,
        [pltpu.SemaphoreType.DMA((len(near),))],
        8 * MIB,
    )(*hbm(*near))

    keep, send = call(
        functools.partial(sort_body, groups), [shape(some, span)] * 2, [SMEM] + [VMEM] * groups, 16
    )(place, *strips)
    send, w_in_sent = lax.optimization_barrier((send, w_in))
    w_in_mate = core(w_in_sent)
    got, beyond[0] = lax.optimization_barrier((beside(send), beyond[0]))
    total, message = call(
        down_body, [shape(rows, rank, dtype=f32), shape(rows, rank)], [SMEM] + [VMEM] * 4, 16
    )(place, keep, got, low_in_near, low_in_mate)
    *_, w_out_sent = lax.optimization_barrier((*held, message, w_in_mate, w_out))
    w_out_mate = core(w_out_sent)
    got, low_out_sent, beyond[1] = lax.optimization_barrier((beside(message), low_out, beyond[1]))
    low_out_mate = core(low_out_sent)
    step = piece(width, 2048)
    act = call(
        functools.partial(act_body, groups, step),
        [shape(rows, 2 * block)],
        [SMEM] * 4 + [VMEM] * (2 * groups + 4),
        16,
        (),
        4 * MIB,
    )(place, lists, counts, block_slot, *held, *beyond, w_in_near, w_in_mate, bias, bias_mate)[0]
    total, *messages = call(
        functools.partial(merge_body, groups),
        [shape(rows, rank, dtype=f32)] + [shape(rows, rank)] * (groups - 1),
        [VMEM] * 2,
        16,
    )(total, got)
    got = [across(messages[k - 1], k) for k in range(groups - 1, 0, -1)]
    part = call(
        functools.partial(part_body, step),
        [shape(rows, width, dtype=f32)],
        [VMEM] * 3,
        16,
        (),
        6 * MIB,
    )(act, w_out_near, w_out_mate)[0]
    parts = call(
        functools.partial(up_body, groups),
        [shape(row_dev, width, dtype=f32)] * groups + [shape(row_dev, width)] * groups,
        [SMEM] + [VMEM] * (groups + 4),
        16,
        (),
        6 * MIB,
    )(place, total, low_bias.reshape(1, rank), low_out_near, low_out_mate, part, *got)

    sums, here, mark = [], None, None
    for k in range(groups - 1, -1, -1):
        mine = parts[groups + k]
        if k == 0:
            mine, _ = lax.optimization_barrier((mine, mark))
        come = beside(mine)
        if here is not None:
            come, _ = lax.optimization_barrier((come, here))
        here = parts[k] + come.astype(f32)
        here = here.astype(bf16) if k else here
        mark = here if k == groups // 2 else mark
        sums.append(across(here, k) if k else here)
    return call(functools.partial(last_body, groups), [shape(row_dev, width)], [VMEM] * groups, 16)(*sums[::-1])[0]


def solution(mesh):
    return jax.shard_map(
        shards,
        mesh=mesh,
        in_specs=(
            P(("rep", "blk"), None),
            P(),
            P(),
            P("rep", None),
            P("rep"),
            P(),
            P(None, "blk"),
            P("blk"),
            P("blk", None),
            P("blk", None),
            P(),
            P(None, "blk"),
        ),
        out_specs=P(("rep", "blk"), None),
        check_vma=False,
    )
```

```python
import functools

import jax
import jax.numpy as jnp
from jax import lax
from jax.experimental import pallas as pl
from jax.experimental.pallas import tpu as pltpu
from jax.sharding import PartitionSpec as P

MIB = 1 << 20
VMEM = pl.BlockSpec(memory_space=pltpu.VMEM)
HBM = pl.BlockSpec(memory_space=pltpu.HBM)
SMEM = pl.BlockSpec(memory_space=pltpu.SMEM)
f32, bf16 = jnp.float32, jnp.bfloat16


def piece(width, most):
    size = 128
    while size * 2 <= most and width % (size * 2) == 0:
        size *= 2
    return size


def window(index, size):
    return pl.ds(pl.multiple_of(index * size, 128), size)


def call(body, outs, ins, limit, scratch=(), moved=2 * MIB):
    return pl.pallas_call(
        body,
        out_shape=outs,
        in_specs=ins,
        out_specs=[VMEM] * len(outs),
        scratch_shapes=list(scratch),
        compiler_params=pltpu.CompilerParams(vmem_limit_bytes=limit * MIB),
        cost_estimate=pl.CostEstimate(flops=0, bytes_accessed=moved, transcendentals=0),
    )


def normal(hidden, gain, shift):
    wide = hidden.astype(f32)
    mean = jnp.mean(wide, axis=-1, keepdims=True)
    centred = wide - mean
    variance = jnp.mean(centred * centred, axis=-1, keepdims=True)
    return (centred * lax.rsqrt(variance + 1e-05) * gain + shift).astype(bf16)


def normalise(held, gain, shift, out):
    rows = held[0].shape[0]
    for i in range(0, len(held), 2):
        pair = jnp.concatenate([h[...] for h in held[i : i + 2]], axis=0)
        out[i * rows : (i + 2) * rows, :] = normal(pair, gain[...], shift[...])


def load_body(count, *refs):
    srcs, dsts, sems = refs[:count], refs[count : 2 * count], refs[2 * count]
    copies = [pltpu.make_async_copy(srcs[i], dsts[i], sems.at[i]) for i in range(count)]
    for copy in copies:
        copy.start()
    for copy in copies:
        copy.wait()


def near_body(groups, *refs):
    normalise(refs[:groups], *refs[groups:])


def far_body(groups, place, *refs):
    held, (near, gain, shift, own, mate, far, total, message) = refs[:groups], refs[groups:]
    normalise(held, gain, shift, far)
    share = own.shape[0]
    core = place[0] % 2
    at = window(place[0] // 2, 2 * share)
    columns = jnp.concatenate([near[:, at].astype(f32), far[:, at].astype(f32)], axis=0)
    low, high = columns[:, :share], columns[:, share:]
    mine = jnp.where(core == 0, low, high).astype(bf16)
    other = jnp.where(core == 0, high, low).astype(bf16)
    sums = jnp.dot(mine, own[...], preferred_element_type=f32) + jnp.dot(
        other, mate[...], preferred_element_type=f32
    )
    half = near.shape[0]
    total[...] = sums
    message[:half, :] = sums[half:].astype(bf16)
    message[half:, :] = sums[:half].astype(bf16)


def turn(x, groups, bit):
    rows = x.shape[0] // (2 * groups)
    at = [h * groups + (k ^ bit) for h in range(2) for k in range(groups)]
    return jnp.concatenate([x[i * rows : (i + 1) * rows] for i in at], axis=0)


def merge_body(groups, total, got, out, *messages):
    sums = total[...] + got[...].astype(f32)
    out[...] = sums
    for k in range(1, groups):
        messages[k - 1][...] = turn(sums, groups, k).astype(bf16)


def up_body(groups, place, total, bias, own, mate, part, *refs):
    got, outs = refs[: groups - 1], refs[groups - 1 :]
    sums = total[...]
    for g in got:
        sums = sums + g[...].astype(f32)
    hidden = jnp.maximum(sums + bias[...], 0.0).astype(bf16)
    core = place[0] % 2
    mine = jnp.dot(hidden, own[...], preferred_element_type=f32)
    other = jnp.dot(hidden, mate[...], preferred_element_type=f32)
    both = jnp.concatenate([jnp.where(core == 0, mine, other), jnp.where(core == 0, other, mine)], axis=1)
    at = window(place[0] // 2, both.shape[1])
    rows = outs[0].shape[0]
    for q in range(2 * groups):
        some = slice(q * rows, (q + 1) * rows)
        outs[q][...] = part[some, :].astype(outs[q].dtype)
        outs[q][:, at] = (part[some, at] + both[some]).astype(outs[q].dtype)


def last_body(groups, *refs):
    sums, out = refs[:groups], refs[groups]
    total = sums[0][...]
    for k in range(1, groups):
        total = total + sums[k][...].astype(f32)
    out[...] = total.astype(bf16)


def act_body(step, near, far, w_own, w_mate, b_own, b_mate, mask, out):
    total = jnp.zeros(out.shape, f32)
    for i in range(near.shape[1] // step):
        at = slice(i * step, (i + 1) * step)
        rows = jnp.concatenate([near[:, at], far[:, at]], axis=0)
        both = jnp.concatenate([w_own[at, :], w_mate[at, :]], axis=1)
        total = total + jnp.dot(rows, both, preferred_element_type=f32)
    bias = jnp.concatenate([b_own[...], b_mate[...]], axis=1)
    out[...] = (jnp.maximum(total + bias, 0.0) * mask[...]).astype(bf16)


def part_body(step, act, w_own, w_mate, out):
    for i in range(out.shape[1] // step):
        at = slice(i * step, (i + 1) * step)
        both = jnp.concatenate([w_own[:, at], w_mate[:, at]], axis=0)
        out[:, at] = jnp.dot(act[...], both, preferred_element_type=f32)


def activity(lists, counts, block_slot):
    groups, top = lists.shape
    nblocks = block_slot.shape[0]
    names = jnp.arange(nblocks, dtype=jnp.int32)
    live = (jnp.arange(top, dtype=jnp.int32)[None, :] < counts[:, None]).astype(jnp.int32)
    hits = (lists[:, :, None] == names[None, None, :]).astype(jnp.int32) * live[:, :, None]
    by_block = jnp.sum(hits, axis=1)
    placed = (block_slot[:, None] == names[None, :]).astype(jnp.int32)
    return jnp.sum(by_block[:, :, None] * placed[None, :, :], axis=1)


def shards(
    hidden,
    ln_gain,
    ln_shift,
    lists,
    counts,
    block_slot,
    w_in,
    b_in,
    w_out,
    low_in,
    low_bias,
    low_out,
):
    devices = lax.axis_size("blk")
    position = lax.axis_index("blk")
    row_dev, width = hidden.shape
    groups = lists.shape[0]
    share, rank = low_in.shape
    block = w_in.shape[1]
    assert devices == 4 * groups
    plane = position // 4
    place = jnp.reshape(position, (1,)).astype(jnp.int32)
    some, rows = groups * row_dev, 2 * groups * row_dev

    def across(x, k):
        return lax.ppermute(x, "blk", [(i, i ^ (4 * k)) for i in range(devices)])

    def beside(x):
        return lax.ppermute(x, "blk", [(i, i ^ 2) for i in range(devices)])

    def core(x):
        return lax.ppermute(x, "blk", [(i, i ^ 1) for i in range(devices)])

    def shape(*dims, dtype=bf16):
        return jax.ShapeDtypeStruct(dims, dtype)

    gain, shift, bias = ln_gain.reshape(1, width), ln_shift.reshape(1, width), b_in.reshape(1, block)
    span = 2 * share

    table = activity(lists, counts, block_slot)
    by = plane ^ jnp.arange(groups)
    at = position ^ jnp.arange(2)
    relate = (by[:, None] == jnp.arange(groups)[None, :])[:, None, :, None]
    choose = (at[:, None] == jnp.arange(devices)[None, :])[None, :, None, :]
    live = jnp.sum(jnp.where(relate & choose, table[None, None], 0), axis=(2, 3)).astype(f32)
    mask = jnp.broadcast_to(live[None, :, None, :, None], (2, groups, row_dev, 2, block)).reshape(rows, 2 * block)

    held = [hidden] + [across(hidden, k) for k in range(1, groups)]
    w_in_mate = core(w_in)
    near = (hidden, gain, shift, low_in, w_in, w_out, low_out)
    *near, mask = lax.optimization_barrier((*near, mask))
    near = call(
        functools.partial(load_body, len(near)),
        [shape(*x.shape, dtype=x.dtype) for x in near],
        [HBM] * len(near),
        16,
        [pltpu.SemaphoreType.DMA((len(near),))],
        8 * MIB,
    )(*[pltpu.with_memory_space_constraint(x, pltpu.HBM) for x in near])
    early, bias_mate = lax.optimization_barrier((hidden, core(bias)))
    beyond = [beside(early), beside(held[1])]
    *_, w_in_mate, low_in_sent, w_out_sent = lax.optimization_barrier(
        (*held, *near, *beyond, w_in_mate, low_in, w_out)
    )
    hidden_near, gain, shift, low_in_near, w_in, w_out_near, low_out_near = near
    low_in_mate, w_out_mate = core(low_in_sent), core(w_out_sent)
    normed = call(
        functools.partial(near_body, groups), [shape(some, width)], [VMEM] * (groups + 2), 16, (), 4 * MIB
    )(hidden_near, *held[1:], gain, shift)[0]
    beyond = beyond + [beside(h) for h in held[len(beyond) :]]
    far, total, message = call(
        functools.partial(far_body, groups),
        [shape(some, width), shape(rows, rank, dtype=f32), shape(rows, rank)],
        [SMEM] + [VMEM] * (groups + 5),
        16,
        (),
        4 * MIB,
    )(place, *beyond, normed, gain, shift, low_in_near, low_in_mate)
    got, w_out_mate, low_out_sent = lax.optimization_barrier((beside(message), w_out_mate, low_out))
    low_out_mate = core(low_out_sent)
    step = piece(width, 2048)
    act = call(
        functools.partial(act_body, step),
        [shape(rows, 2 * block)],
        [VMEM] * 7,
        16,
        (),
        4 * MIB,
    )(normed, far, w_in, w_in_mate, bias, bias_mate, mask)[0]
    total, *messages = call(
        functools.partial(merge_body, groups),
        [shape(rows, rank, dtype=f32)] + [shape(rows, rank)] * (groups - 1),
        [VMEM] * 2,
        16,
    )(total, got)
    got = [across(messages[k - 1], k) for k in range(groups - 1, 0, -1)]
    part = call(
        functools.partial(part_body, step),
        [shape(rows, width, dtype=f32)],
        [VMEM] * 3,
        16,
        (),
        6 * MIB,
    )(act, w_out_near, w_out_mate)[0]
    parts = call(
        functools.partial(up_body, groups),
        [shape(row_dev, width, dtype=f32)] * groups + [shape(row_dev, width)] * groups,
        [SMEM] + [VMEM] * (groups + 4),
        16,
        (),
        6 * MIB,
    )(place, total, low_bias.reshape(1, rank), low_out_near, low_out_mate, part, *got)

    sums, here, mark = [], None, None
    for k in range(groups - 1, -1, -1):
        mine = parts[groups + k]
        if k == 0:
            mine, _ = lax.optimization_barrier((mine, mark))
        come = beside(mine)
        if here is not None:
            come, _ = lax.optimization_barrier((come, here))
        here = parts[k] + come.astype(f32)
        here = here.astype(bf16) if k else here
        mark = here if k == groups // 2 else mark
        sums.append(across(here, k) if k else here)
    return call(functools.partial(last_body, groups), [shape(row_dev, width)], [VMEM] * groups, 16)(*sums[::-1])[0]


def solution(mesh):
    return jax.shard_map(
        shards,
        mesh=mesh,
        in_specs=(
            P(("rep", "blk"), None),
            P(),
            P(),
            P("rep", None),
            P("rep"),
            P(),
            P(None, "blk"),
            P("blk"),
            P("blk", None),
            P("blk", None),
            P(),
            P(None, "blk"),
        ),
        out_specs=P(("rep", "blk"), None),
        check_vma=False,
    )
```

```python
import functools

import jax
import jax.numpy as jnp
from jax import lax
from jax.experimental import pallas as pl
from jax.experimental.pallas import tpu as pltpu
from jax.sharding import PartitionSpec as P

MIB = 1 << 20
VMEM = pl.BlockSpec(memory_space=pltpu.VMEM)
HBM = pl.BlockSpec(memory_space=pltpu.HBM)
SMEM = pl.BlockSpec(memory_space=pltpu.SMEM)
f32, bf16 = jnp.float32, jnp.bfloat16


def piece(width, most):
    size = 128
    while size * 2 <= most and width % (size * 2) == 0:
        size *= 2
    return size


def window(index, size):
    return pl.ds(pl.multiple_of(index * size, 128), size)


def call(body, outs, ins, limit, scratch=(), moved=2 * MIB):
    return pl.pallas_call(
        body,
        out_shape=outs,
        in_specs=ins,
        out_specs=[VMEM] * len(outs),
        scratch_shapes=list(scratch),
        compiler_params=pltpu.CompilerParams(vmem_limit_bytes=limit * MIB),
        cost_estimate=pl.CostEstimate(flops=0, bytes_accessed=moved, transcendentals=0),
    )


def normal(hidden, gain, shift):
    wide = hidden.astype(f32)
    mean = jnp.mean(wide, axis=-1, keepdims=True)
    centred = wide - mean
    variance = jnp.mean(centred * centred, axis=-1, keepdims=True)
    return (centred * lax.rsqrt(variance + 1e-05) * gain + shift).astype(bf16)


def normalise(held, gain, shift, out):
    rows = held[0].shape[0]
    for i in range(0, len(held), 2):
        pair = jnp.concatenate([h[...] for h in held[i : i + 2]], axis=0)
        out[i * rows : (i + 2) * rows, :] = normal(pair, gain[...], shift[...])


def load_body(count, *refs):
    srcs, dsts, sems = refs[:count], refs[count : 2 * count], refs[2 * count]
    copies = [pltpu.make_async_copy(srcs[i], dsts[i], sems.at[i]) for i in range(count)]
    for copy in copies:
        copy.start()
    for copy in copies:
        copy.wait()


def near_body(groups, *refs):
    normalise(refs[:groups], *refs[groups:])


def far_body(groups, place, *refs):
    held, (near, gain, shift, own, mate, far, total, message) = refs[:groups], refs[groups:]
    normalise(held, gain, shift, far)
    share = own.shape[0]
    core = place[0] % 2
    at = window(place[0] // 2, 2 * share)
    columns = jnp.concatenate([near[:, at].astype(f32), far[:, at].astype(f32)], axis=0)
    low, high = columns[:, :share], columns[:, share:]
    mine = jnp.where(core == 0, low, high).astype(bf16)
    other = jnp.where(core == 0, high, low).astype(bf16)
    sums = jnp.dot(mine, own[...], preferred_element_type=f32) + jnp.dot(
        other, mate[...], preferred_element_type=f32
    )
    half = near.shape[0]
    total[...] = sums
    message[:half, :] = sums[half:].astype(bf16)
    message[half:, :] = sums[:half].astype(bf16)


def turn(x, groups, bit):
    rows = x.shape[0] // (2 * groups)
    at = [h * groups + (k ^ bit) for h in range(2) for k in range(groups)]
    return jnp.concatenate([x[i * rows : (i + 1) * rows] for i in at], axis=0)


def merge_body(groups, total, got, out, *messages):
    sums = total[...] + got[...].astype(f32)
    out[...] = sums
    for k in range(1, groups):
        messages[k - 1][...] = turn(sums, groups, k).astype(bf16)


def up_body(groups, place, total, bias, own, mate, part, *refs):
    got, outs = refs[: groups - 1], refs[groups - 1 :]
    sums = total[...]
    for g in got:
        sums = sums + g[...].astype(f32)
    hidden = jnp.maximum(sums + bias[...], 0.0).astype(bf16)
    core = place[0] % 2
    mine = jnp.dot(hidden, own[...], preferred_element_type=f32)
    other = jnp.dot(hidden, mate[...], preferred_element_type=f32)
    both = jnp.concatenate([jnp.where(core == 0, mine, other), jnp.where(core == 0, other, mine)], axis=1)
    at = window(place[0] // 2, both.shape[1])
    rows = outs[0].shape[0]
    for q in range(2 * groups):
        some = slice(q * rows, (q + 1) * rows)
        outs[q][...] = part[some, :].astype(outs[q].dtype)
        outs[q][:, at] = (part[some, at] + both[some]).astype(outs[q].dtype)


def last_body(groups, *refs):
    sums, out = refs[:groups], refs[groups]
    total = sums[0][...]
    for k in range(1, groups):
        total = total + sums[k][...].astype(f32)
    out[...] = total.astype(bf16)


def act_body(groups, step, place, lists, counts, block_slot, near, far, w_own, w_mate, b_own, b_mate, out):
    block, row_dev = w_own.shape[1], near.shape[0] // groups
    total = jnp.zeros(out.shape, f32)
    for i in range(w_own.shape[0] // step):
        at = slice(i * step, (i + 1) * step)
        rows = jnp.concatenate([near[:, at], far[:, at]], axis=0)
        both = jnp.concatenate([w_own[at, :], w_mate[at, :]], axis=1)
        total = total + jnp.dot(rows, both, preferred_element_type=f32)
    bias = jnp.concatenate([b_own[...], b_mate[...]], axis=1)
    act = jnp.maximum(total + bias, 0.0)
    row_k = (lax.broadcasted_iota(jnp.int32, out.shape, 0) // row_dev) % groups
    column_b = lax.broadcasted_iota(jnp.int32, out.shape, 1) // block
    uses = jnp.zeros(out.shape, jnp.int32)
    for k in range(groups):
        group = (place[0] // 4) ^ k

        def hit(e, found):
            slot = block_slot[lists[group, e]]
            live = e < counts[group]
            own = jnp.where(live & (slot == place[0]), 1, 0)
            mate = jnp.where(live & (slot == place[0] ^ 1), 1, 0)
            return found[0] + own, found[1] + mate

        own, mate = lax.fori_loop(0, lists.shape[1], hit, (jnp.int32(0), jnp.int32(0)))
        uses = jnp.where(row_k == k, jnp.where(column_b == 0, own, mate), uses)
    out[...] = jnp.where(uses > 0, act, 0.0).astype(bf16)


def part_body(step, act, w_own, w_mate, out):
    for i in range(out.shape[1] // step):
        at = slice(i * step, (i + 1) * step)
        both = jnp.concatenate([w_own[:, at], w_mate[:, at]], axis=0)
        out[:, at] = jnp.dot(act[...], both, preferred_element_type=f32)


def shards(
    hidden,
    ln_gain,
    ln_shift,
    lists,
    counts,
    block_slot,
    w_in,
    b_in,
    w_out,
    low_in,
    low_bias,
    low_out,
):
    devices = lax.axis_size("blk")
    position = lax.axis_index("blk")
    row_dev, width = hidden.shape
    groups = lists.shape[0]
    share, rank = low_in.shape
    block = w_in.shape[1]
    assert devices == 4 * groups
    plane = position // 4
    place = jnp.reshape(position, (1,)).astype(jnp.int32)
    some, rows = groups * row_dev, 2 * groups * row_dev

    def across(x, k):
        return lax.ppermute(x, "blk", [(i, i ^ (4 * k)) for i in range(devices)])

    def beside(x):
        return lax.ppermute(x, "blk", [(i, i ^ 2) for i in range(devices)])

    def core(x):
        return lax.ppermute(x, "blk", [(i, i ^ 1) for i in range(devices)])

    def shape(*dims, dtype=bf16):
        return jax.ShapeDtypeStruct(dims, dtype)

    gain, shift, bias = ln_gain.reshape(1, width), ln_shift.reshape(1, width), b_in.reshape(1, block)
    span = 2 * share

    held = [hidden] + [across(hidden, k) for k in range(1, groups)]
    w_in_mate = core(w_in)
    near = (hidden, gain, shift, low_in, w_in, w_out, low_out)
    near = call(
        functools.partial(load_body, len(near)),
        [shape(*x.shape, dtype=x.dtype) for x in near],
        [HBM] * len(near),
        16,
        [pltpu.SemaphoreType.DMA((len(near),))],
        8 * MIB,
    )(*[pltpu.with_memory_space_constraint(x, pltpu.HBM) for x in near])
    early, bias_mate = lax.optimization_barrier((hidden, core(bias)))
    held[1], *near = lax.optimization_barrier((held[1], *near))
    beyond = [beside(early), beside(held[1])]
    *_, w_in_mate, low_in_sent, w_out_sent = lax.optimization_barrier(
        (*held, *near, *beyond, w_in_mate, low_in, w_out)
    )
    hidden_near, gain, shift, low_in_near, w_in, w_out_near, low_out_near = near
    low_in_mate, w_out_mate = core(low_in_sent), core(w_out_sent)
    normed = call(
        functools.partial(near_body, groups), [shape(some, width)], [VMEM] * (groups + 2), 16, (), 4 * MIB
    )(hidden_near, *held[1:], gain, shift)[0]
    beyond = beyond + [beside(h) for h in held[len(beyond) :]]
    far, total, message = call(
        functools.partial(far_body, groups),
        [shape(some, width), shape(rows, rank, dtype=f32), shape(rows, rank)],
        [SMEM] + [VMEM] * (groups + 5),
        16,
        (),
        4 * MIB,
    )(place, *beyond, normed, gain, shift, low_in_near, low_in_mate)
    got, w_out_mate, low_out_sent = lax.optimization_barrier((beside(message), w_out_mate, low_out))
    low_out_mate = core(low_out_sent)
    step = piece(width, 2048)
    act = call(
        functools.partial(act_body, groups, step),
        [shape(rows, 2 * block)],
        [SMEM] * 4 + [VMEM] * 6,
        16,
        (),
        4 * MIB,
    )(place, lists, counts, block_slot, normed, far, w_in, w_in_mate, bias, bias_mate)[0]
    total, *messages = call(
        functools.partial(merge_body, groups),
        [shape(rows, rank, dtype=f32)] + [shape(rows, rank)] * (groups - 1),
        [VMEM] * 2,
        16,
    )(total, got)
    got = [across(messages[k - 1], k) for k in range(groups - 1, 0, -1)]
    part = call(
        functools.partial(part_body, step),
        [shape(rows, width, dtype=f32)],
        [VMEM] * 3,
        16,
        (),
        6 * MIB,
    )(act, w_out_near, w_out_mate)[0]
    parts = call(
        functools.partial(up_body, groups),
        [shape(row_dev, width, dtype=f32)] * groups + [shape(row_dev, width)] * groups,
        [SMEM] + [VMEM] * (groups + 4),
        16,
        (),
        6 * MIB,
    )(place, total, low_bias.reshape(1, rank), low_out_near, low_out_mate, part, *got)

    sums, here, mark = [], None, None
    for k in range(groups - 1, -1, -1):
        mine = parts[groups + k]
        if k == 0:
            mine, _ = lax.optimization_barrier((mine, mark))
        come = beside(mine)
        if here is not None:
            come, _ = lax.optimization_barrier((come, here))
        here = parts[k] + come.astype(f32)
        here = here.astype(bf16) if k else here
        mark = here if k == groups // 2 else mark
        sums.append(across(here, k) if k else here)
    return call(functools.partial(last_body, groups), [shape(row_dev, width)], [VMEM] * groups, 16)(*sums[::-1])[0]


def solution(mesh):
    return jax.shard_map(
        shards,
        mesh=mesh,
        in_specs=(
            P(("rep", "blk"), None),
            P(),
            P(),
            P("rep", None),
            P("rep"),
            P(),
            P(None, "blk"),
            P("blk"),
            P("blk", None),
            P("blk", None),
            P(),
            P(None, "blk"),
        ),
        out_specs=P(("rep", "blk"), None),
        check_vma=False,
    )
```

```python
import functools

import jax
import jax.numpy as jnp
from jax import lax
from jax.experimental import pallas as pl
from jax.experimental.pallas import tpu as pltpu
from jax.sharding import PartitionSpec as P

MIB = 1 << 20
VMEM = pl.BlockSpec(memory_space=pltpu.VMEM)
HBM = pl.BlockSpec(memory_space=pltpu.HBM)
SMEM = pl.BlockSpec(memory_space=pltpu.SMEM)
f32, bf16 = jnp.float32, jnp.bfloat16


def piece(width, most):
    size = 128
    while size * 2 <= most and width % (size * 2) == 0:
        size *= 2
    return size


def window(index, size):
    return pl.ds(pl.multiple_of(index * size, 128), size)


def call(body, outs, ins, limit, scratch=(), moved=2 * MIB):
    return pl.pallas_call(
        body,
        out_shape=outs,
        in_specs=ins,
        out_specs=[VMEM] * len(outs),
        scratch_shapes=list(scratch),
        compiler_params=pltpu.CompilerParams(vmem_limit_bytes=limit * MIB),
        cost_estimate=pl.CostEstimate(flops=0, bytes_accessed=moved, transcendentals=0),
    )


def normal(hidden, gain, shift):
    wide = hidden.astype(f32)
    mean = jnp.mean(wide, axis=-1, keepdims=True)
    centred = wide - mean
    variance = jnp.mean(centred * centred, axis=-1, keepdims=True)
    return (centred * lax.rsqrt(variance + 1e-05) * gain + shift).astype(bf16)


def normalise(held, gain, shift, out):
    rows = held[0].shape[0]
    for i in range(0, len(held), 2):
        pair = jnp.concatenate([h[...] for h in held[i : i + 2]], axis=0)
        out[i * rows : (i + 2) * rows, :] = normal(pair, gain[...], shift[...])


def load_body(count, *refs):
    srcs, dsts, sems = refs[:count], refs[count : 2 * count], refs[2 * count]
    copies = [pltpu.make_async_copy(srcs[i], dsts[i], sems.at[i]) for i in range(count)]
    for copy in copies:
        copy.start()
    for copy in copies:
        copy.wait()


def near_body(groups, *refs):
    normalise(refs[:groups], *refs[groups:])


def far_body(groups, place, *refs):
    held, (near, gain, shift, own, mate, far, total, message) = refs[:groups], refs[groups:]
    normalise(held, gain, shift, far)
    share = own.shape[0]
    core = place[0] % 2
    at = window(place[0] // 2, 2 * share)
    columns = jnp.concatenate([near[:, at].astype(f32), far[:, at].astype(f32)], axis=0)
    low, high = columns[:, :share], columns[:, share:]
    mine = jnp.where(core == 0, low, high).astype(bf16)
    other = jnp.where(core == 0, high, low).astype(bf16)
    sums = jnp.dot(mine, own[...], preferred_element_type=f32) + jnp.dot(
        other, mate[...], preferred_element_type=f32
    )
    half = near.shape[0]
    total[...] = sums
    message[:half, :] = sums[half:].astype(bf16)
    message[half:, :] = sums[:half].astype(bf16)


def turn(x, groups, bit):
    rows = x.shape[0] // (2 * groups)
    at = [h * groups + (k ^ bit) for h in range(2) for k in range(groups)]
    return jnp.concatenate([x[i * rows : (i + 1) * rows] for i in at], axis=0)


def merge_body(groups, total, got, out, *messages):
    sums = total[...] + got[...].astype(f32)
    out[...] = sums
    for k in range(1, groups):
        messages[k - 1][...] = turn(sums, groups, k).astype(bf16)


def up_body(groups, place, total, bias, own, mate, part, *refs):
    got, outs = refs[: groups - 1], refs[groups - 1 :]
    sums = total[...]
    for g in got:
        sums = sums + g[...].astype(f32)
    hidden = jnp.maximum(sums + bias[...], 0.0).astype(bf16)
    core = place[0] % 2
    mine = jnp.dot(hidden, own[...], preferred_element_type=f32)
    other = jnp.dot(hidden, mate[...], preferred_element_type=f32)
    both = jnp.concatenate([jnp.where(core == 0, mine, other), jnp.where(core == 0, other, mine)], axis=1)
    at = window(place[0] // 2, both.shape[1])
    rows = outs[0].shape[0]
    for q in range(2 * groups):
        some = slice(q * rows, (q + 1) * rows)
        outs[q][...] = part[some, :].astype(outs[q].dtype)
        outs[q][:, at] = (part[some, at] + both[some]).astype(outs[q].dtype)


def last_body(groups, *refs):
    sums, out = refs[:groups], refs[groups]
    total = sums[0][...]
    for k in range(1, groups):
        total = total + sums[k][...].astype(f32)
    out[...] = total.astype(bf16)


def act_body(groups, step, place, lists, counts, block_slot, near, far, w_own, w_mate, b_own, b_mate, out):
    block, row_dev = w_own.shape[1], near.shape[0] // groups
    total = jnp.zeros(out.shape, f32)
    for i in range(w_own.shape[0] // step):
        at = slice(i * step, (i + 1) * step)
        rows = jnp.concatenate([near[:, at], far[:, at]], axis=0)
        both = jnp.concatenate([w_own[at, :], w_mate[at, :]], axis=1)
        total = total + jnp.dot(rows, both, preferred_element_type=f32)
    bias = jnp.concatenate([b_own[...], b_mate[...]], axis=1)
    act = jnp.maximum(total + bias, 0.0)
    row_k = (lax.broadcasted_iota(jnp.int32, out.shape, 0) // row_dev) % groups
    column_b = lax.broadcasted_iota(jnp.int32, out.shape, 1) // block
    uses = jnp.zeros(out.shape, jnp.int32)
    for k in range(groups):
        group = (place[0] // 4) ^ k

        def hit(e, found):
            slot = block_slot[lists[group, e]]
            live = e < counts[group]
            own = jnp.where(live & (slot == place[0]), 1, 0)
            mate = jnp.where(live & (slot == place[0] ^ 1), 1, 0)
            return found[0] + own, found[1] + mate

        own, mate = lax.fori_loop(0, lists.shape[1], hit, (jnp.int32(0), jnp.int32(0)))
        uses = jnp.where(row_k == k, jnp.where(column_b == 0, own, mate), uses)
    out[...] = jnp.where(uses > 0, act, 0.0).astype(bf16)


def part_body(step, act, w_own, w_mate, out):
    for i in range(out.shape[1] // step):
        at = slice(i * step, (i + 1) * step)
        both = jnp.concatenate([w_own[:, at], w_mate[:, at]], axis=0)
        out[:, at] = jnp.dot(act[...], both, preferred_element_type=f32)


def shards(
    hidden,
    ln_gain,
    ln_shift,
    lists,
    counts,
    block_slot,
    w_in,
    b_in,
    w_out,
    low_in,
    low_bias,
    low_out,
):
    devices = lax.axis_size("blk")
    position = lax.axis_index("blk")
    row_dev, width = hidden.shape
    groups = lists.shape[0]
    share, rank = low_in.shape
    block = w_in.shape[1]
    assert devices == 4 * groups
    plane = position // 4
    place = jnp.reshape(position, (1,)).astype(jnp.int32)
    some, rows = groups * row_dev, 2 * groups * row_dev

    def across(x, k):
        return lax.ppermute(x, "blk", [(i, i ^ (4 * k)) for i in range(devices)])

    def beside(x):
        return lax.ppermute(x, "blk", [(i, i ^ 2) for i in range(devices)])

    def core(x):
        return lax.ppermute(x, "blk", [(i, i ^ 1) for i in range(devices)])

    def shape(*dims, dtype=bf16):
        return jax.ShapeDtypeStruct(dims, dtype)

    gain, shift, bias = ln_gain.reshape(1, width), ln_shift.reshape(1, width), b_in.reshape(1, block)
    span = 2 * share

    held = [hidden] + [across(hidden, k) for k in range(1, groups)]
    w_in_mate = core(w_in)
    near = (hidden, gain, shift, low_in, w_in, w_out, low_out)
    place, *near = lax.optimization_barrier((place, *near))
    near = call(
        functools.partial(load_body, len(near)),
        [shape(*x.shape, dtype=x.dtype) for x in near],
        [HBM] * len(near),
        16,
        [pltpu.SemaphoreType.DMA((len(near),))],
        8 * MIB,
    )(*[pltpu.with_memory_space_constraint(x, pltpu.HBM) for x in near])
    early, bias_mate = lax.optimization_barrier((hidden, core(bias)))
    held[1], *near = lax.optimization_barrier((held[1], *near))
    beyond = [beside(early), beside(held[1])]
    *_, w_in_mate, low_in_sent, w_out_sent = lax.optimization_barrier(
        (*held, *near, *beyond, w_in_mate, low_in, w_out)
    )
    hidden_near, gain, shift, low_in_near, w_in, w_out_near, low_out_near = near
    low_in_mate, w_out_mate = core(low_in_sent), core(w_out_sent)
    normed = call(
        functools.partial(near_body, groups), [shape(some, width)], [VMEM] * (groups + 2), 16, (), 4 * MIB
    )(hidden_near, *held[1:], gain, shift)[0]
    beyond = beyond + [beside(h) for h in held[len(beyond) :]]
    far, total, message = call(
        functools.partial(far_body, groups),
        [shape(some, width), shape(rows, rank, dtype=f32), shape(rows, rank)],
        [SMEM] + [VMEM] * (groups + 5),
        16,
        (),
        4 * MIB,
    )(place, *beyond, normed, gain, shift, low_in_near, low_in_mate)
    got, w_out_mate, low_out_sent = lax.optimization_barrier((beside(message), w_out_mate, low_out))
    low_out_mate = core(low_out_sent)
    step = piece(width, 2048)
    act = call(
        functools.partial(act_body, groups, step),
        [shape(rows, 2 * block)],
        [SMEM] * 4 + [VMEM] * 6,
        16,
        (),
        4 * MIB,
    )(place, lists, counts, block_slot, normed, far, w_in, w_in_mate, bias, bias_mate)[0]
    total, *messages = call(
        functools.partial(merge_body, groups),
        [shape(rows, rank, dtype=f32)] + [shape(rows, rank)] * (groups - 1),
        [VMEM] * 2,
        16,
    )(total, got)
    got = [across(messages[k - 1], k) for k in range(groups - 1, 0, -1)]
    part = call(
        functools.partial(part_body, step),
        [shape(rows, width, dtype=f32)],
        [VMEM] * 3,
        16,
        (),
        6 * MIB,
    )(act, w_out_near, w_out_mate)[0]
    parts = call(
        functools.partial(up_body, groups),
        [shape(row_dev, width, dtype=f32)] * groups + [shape(row_dev, width)] * groups,
        [SMEM] + [VMEM] * (groups + 4),
        16,
        (),
        6 * MIB,
    )(place, total, low_bias.reshape(1, rank), low_out_near, low_out_mate, part, *got)

    sums, here, mark = [], None, None
    for k in range(groups - 1, -1, -1):
        mine = parts[groups + k]
        if k == 0:
            mine, _ = lax.optimization_barrier((mine, mark))
        come = beside(mine)
        if here is not None:
            come, _ = lax.optimization_barrier((come, here))
        here = parts[k] + come.astype(f32)
        here = here.astype(bf16) if k else here
        mark = here if k == groups // 2 else mark
        sums.append(across(here, k) if k else here)
    return call(functools.partial(last_body, groups), [shape(row_dev, width)], [VMEM] * groups, 16)(*sums[::-1])[0]


def solution(mesh):
    return jax.shard_map(
        shards,
        mesh=mesh,
        in_specs=(
            P(("rep", "blk"), None),
            P(),
            P(),
            P("rep", None),
            P("rep"),
            P(),
            P(None, "blk"),
            P("blk"),
            P("blk", None),
            P("blk", None),
            P(),
            P(None, "blk"),
        ),
        out_specs=P(("rep", "blk"), None),
        check_vma=False,
    )
```

```python
import functools

import jax
import jax.numpy as jnp
from jax import lax
from jax.experimental import pallas as pl
from jax.experimental.pallas import tpu as pltpu
from jax.sharding import PartitionSpec as P

MIB = 1 << 20
VMEM = pl.BlockSpec(memory_space=pltpu.VMEM)
HBM = pl.BlockSpec(memory_space=pltpu.HBM)
SMEM = pl.BlockSpec(memory_space=pltpu.SMEM)
f32, bf16 = jnp.float32, jnp.bfloat16


def piece(width, most):
    size = 128
    while size * 2 <= most and width % (size * 2) == 0:
        size *= 2
    return size


def window(index, size):
    return pl.ds(pl.multiple_of(index * size, 128), size)


def call(body, outs, ins, limit, scratch=(), moved=2 * MIB):
    return pl.pallas_call(
        body,
        out_shape=outs,
        in_specs=ins,
        out_specs=[VMEM] * len(outs),
        scratch_shapes=list(scratch),
        compiler_params=pltpu.CompilerParams(vmem_limit_bytes=limit * MIB),
        cost_estimate=pl.CostEstimate(flops=0, bytes_accessed=moved, transcendentals=0),
    )


def normal(hidden, gain, shift):
    wide = hidden.astype(f32)
    mean = jnp.mean(wide, axis=-1, keepdims=True)
    centred = wide - mean
    variance = jnp.mean(centred * centred, axis=-1, keepdims=True)
    return (centred * lax.rsqrt(variance + 1e-05) * gain + shift).astype(bf16)


def load_body(count, *refs):
    srcs, dsts, sems = refs[:count], refs[count : 2 * count], refs[2 * count]
    copies = [pltpu.make_async_copy(srcs[i], dsts[i], sems.at[i]) for i in range(count)]
    for copy in copies:
        copy.start()
    for copy in copies:
        copy.wait()


def early_body(groups, soon, *refs):
    held, (gain, shift, near, far) = refs[: groups + soon], refs[groups + soon :]
    rows = held[0].shape[0]
    for out, some in ((near, held[:groups]), (far, held[groups:])):
        for i in range(0, len(some), 2):
            pair = jnp.concatenate([h[...] for h in some[i : i + 2]], axis=0)
            out[i * rows : i * rows + pair.shape[0], :] = normal(pair, gain[...], shift[...])


def norm_body(count, place, *refs):
    held, (near, first, gain, shift, own, mate, far, total, message) = refs[:count], refs[count:]
    rows, done = held[0].shape[0], first.shape[0]
    far[:done, :] = first[...]
    for i in range(0, count, 2):
        pair = jnp.concatenate([h[...] for h in held[i : i + 2]], axis=0)
        far[done + i * rows : done + i * rows + pair.shape[0], :] = normal(pair, gain[...], shift[...])
    share = own.shape[0]
    core = place[0] % 2
    at = window(place[0] // 2, 2 * share)
    columns = jnp.concatenate([near[:, at].astype(f32), far[:, at].astype(f32)], axis=0)
    low, high = columns[:, :share], columns[:, share:]
    mine = jnp.where(core == 0, low, high).astype(bf16)
    other = jnp.where(core == 0, high, low).astype(bf16)
    sums = jnp.dot(mine, own[...], preferred_element_type=f32) + jnp.dot(
        other, mate[...], preferred_element_type=f32
    )
    half = near.shape[0]
    total[...] = sums
    message[:half, :] = sums[half:].astype(bf16)
    message[half:, :] = sums[:half].astype(bf16)


def turn(x, groups, bit):
    rows = x.shape[0] // (2 * groups)
    at = [h * groups + (k ^ bit) for h in range(2) for k in range(groups)]
    return jnp.concatenate([x[i * rows : (i + 1) * rows] for i in at], axis=0)


def merge_body(groups, total, got, out, *messages):
    sums = total[...] + got[...].astype(f32)
    out[...] = sums
    for k in range(1, groups):
        messages[k - 1][...] = turn(sums, groups, k).astype(bf16)


def up_body(groups, place, total, bias, own, mate, part, *refs):
    got, outs = refs[: groups - 1], refs[groups - 1 :]
    sums = total[...]
    for g in got:
        sums = sums + g[...].astype(f32)
    hidden = jnp.maximum(sums + bias[...], 0.0).astype(bf16)
    core = place[0] % 2
    mine = jnp.dot(hidden, own[...], preferred_element_type=f32)
    other = jnp.dot(hidden, mate[...], preferred_element_type=f32)
    both = jnp.concatenate([jnp.where(core == 0, mine, other), jnp.where(core == 0, other, mine)], axis=1)
    at = window(place[0] // 2, both.shape[1])
    rows = outs[0].shape[0]
    for q in range(2 * groups):
        some = slice(q * rows, (q + 1) * rows)
        outs[q][...] = part[some, :].astype(outs[q].dtype)
        outs[q][:, at] = (part[some, at] + both[some]).astype(outs[q].dtype)


def last_body(groups, *refs):
    sums, out = refs[:groups], refs[groups]
    total = sums[0][...]
    for k in range(1, groups):
        total = total + sums[k][...].astype(f32)
    out[...] = total.astype(bf16)


def act_body(step, near, far, w_own, w_mate, b_own, b_mate, mask, out):
    total = jnp.zeros(out.shape, f32)
    for i in range(near.shape[1] // step):
        at = slice(i * step, (i + 1) * step)
        rows = jnp.concatenate([near[:, at], far[:, at]], axis=0)
        both = jnp.concatenate([w_own[at, :], w_mate[at, :]], axis=1)
        total = total + jnp.dot(rows, both, preferred_element_type=f32)
    bias = jnp.concatenate([b_own[...], b_mate[...]], axis=1)
    out[...] = (jnp.maximum(total + bias, 0.0) * mask[...]).astype(bf16)


def part_body(step, act, w_own, w_mate, out):
    for i in range(out.shape[1] // step):
        at = slice(i * step, (i + 1) * step)
        both = jnp.concatenate([w_own[:, at], w_mate[:, at]], axis=0)
        out[:, at] = jnp.dot(act[...], both, preferred_element_type=f32)


def activity(lists, counts, block_slot):
    groups, top = lists.shape
    nblocks = block_slot.shape[0]
    names = jnp.arange(nblocks, dtype=jnp.int32)
    live = (jnp.arange(top, dtype=jnp.int32)[None, :] < counts[:, None]).astype(jnp.int32)
    hits = (lists[:, :, None] == names[None, None, :]).astype(jnp.int32) * live[:, :, None]
    by_block = jnp.sum(hits, axis=1)
    placed = (block_slot[:, None] == names[None, :]).astype(jnp.int32)
    return jnp.sum(by_block[:, :, None] * placed[None, :, :], axis=1)


def shards(
    hidden,
    ln_gain,
    ln_shift,
    lists,
    counts,
    block_slot,
    w_in,
    b_in,
    w_out,
    low_in,
    low_bias,
    low_out,
):
    devices = lax.axis_size("blk")
    position = lax.axis_index("blk")
    row_dev, width = hidden.shape
    groups = lists.shape[0]
    share, rank = low_in.shape
    block = w_in.shape[1]
    assert devices == 4 * groups
    plane = position // 4
    place = jnp.reshape(position, (1,)).astype(jnp.int32)
    some, rows = groups * row_dev, 2 * groups * row_dev

    def across(x, k):
        return lax.ppermute(x, "blk", [(i, i ^ (4 * k)) for i in range(devices)])

    def beside(x):
        return lax.ppermute(x, "blk", [(i, i ^ 2) for i in range(devices)])

    def core(x):
        return lax.ppermute(x, "blk", [(i, i ^ 1) for i in range(devices)])

    def shape(*dims, dtype=bf16):
        return jax.ShapeDtypeStruct(dims, dtype)

    gain, shift, bias = ln_gain.reshape(1, width), ln_shift.reshape(1, width), b_in.reshape(1, block)
    span = 2 * share

    table = activity(lists, counts, block_slot)
    by = plane ^ jnp.arange(groups)
    at = position ^ jnp.arange(2)
    relate = (by[:, None] == jnp.arange(groups)[None, :])[:, None, :, None]
    choose = (at[:, None] == jnp.arange(devices)[None, :])[None, :, None, :]
    live = jnp.sum(jnp.where(relate & choose, table[None, None], 0), axis=(2, 3)).astype(f32)
    mask = jnp.broadcast_to(live[None, :, None, :, None], (2, groups, row_dev, 2, block)).reshape(rows, 2 * block)

    held = [hidden] + [across(hidden, k) for k in range(1, groups)]
    w_in_mate = core(w_in)
    held[1], low_in_sent, mask = lax.optimization_barrier((held[1], low_in, mask))
    low_in_mate = core(low_in_sent)
    early, bias_mate = lax.optimization_barrier((hidden, core(bias)))
    beyond = [beside(h) for h in [early] + held[1:]]
    near = (hidden, gain, shift, low_in, w_in, w_out, low_out)
    *near, mask, beyond[0] = lax.optimization_barrier((*near, mask, beyond[0]))
    near = call(
        functools.partial(load_body, len(near)),
        [shape(*x.shape, dtype=x.dtype) for x in near],
        [HBM] * len(near),
        16,
        [pltpu.SemaphoreType.DMA((len(near),))],
        8 * MIB,
    )(*[pltpu.with_memory_space_constraint(x, pltpu.HBM) for x in near])
    hidden_near, gain, shift, low_in, w_in, w_out_near, low_out_near = near
    *_, w_in_mate, w_out_sent, low_out_sent = lax.optimization_barrier(
        (*held, *beyond[: groups // 2], w_in_mate, w_out, low_out)
    )
    w_out_mate, low_out_mate = core(w_out_sent), core(low_out_sent)
    held[0] = hidden_near

    soon = groups // 2
    normed, first = call(
        functools.partial(early_body, groups, soon),
        [shape(some, width), shape(soon * row_dev, width)],
        [VMEM] * (groups + soon + 2),
        16,
        (),
        4 * MIB,
    )(*held, *beyond[:soon], gain, shift)
    far, total, message = call(
        functools.partial(norm_body, groups - soon),
        [shape(some, width), shape(rows, rank, dtype=f32), shape(rows, rank)],
        [SMEM] + [VMEM] * (groups - soon + 6),
        16,
        (),
        4 * MIB,
    )(place, *beyond[soon:], normed, first, gain, shift, low_in, low_in_mate)
    got = beside(message)
    step = piece(width, 2048)
    act = call(
        functools.partial(act_body, step),
        [shape(rows, 2 * block)],
        [VMEM] * 7,
        16,
        (),
        4 * MIB,
    )(normed, far, w_in, w_in_mate, bias, bias_mate, mask)[0]
    total, *messages = call(
        functools.partial(merge_body, groups),
        [shape(rows, rank, dtype=f32)] + [shape(rows, rank)] * (groups - 1),
        [VMEM] * 2,
        16,
    )(total, got)
    got = [across(messages[k - 1], k) for k in range(groups - 1, 0, -1)]
    part = call(
        functools.partial(part_body, step),
        [shape(rows, width, dtype=f32)],
        [VMEM] * 3,
        16,
        (),
        6 * MIB,
    )(act, w_out_near, w_out_mate)[0]
    parts = call(
        functools.partial(up_body, groups),
        [shape(row_dev, width, dtype=f32)] * groups + [shape(row_dev, width)] * groups,
        [SMEM] + [VMEM] * (groups + 4),
        16,
        (),
        6 * MIB,
    )(place, total, low_bias.reshape(1, rank), low_out_near, low_out_mate, part, *got)

    sums = []
    for k in range(groups - 1, -1, -1):
        here = parts[k] + beside(parts[groups + k]).astype(f32)
        sums.append(across(here.astype(bf16), k) if k else here)
    return call(functools.partial(last_body, groups), [shape(row_dev, width)], [VMEM] * groups, 16)(*sums[::-1])[0]


def solution(mesh):
    return jax.shard_map(
        shards,
        mesh=mesh,
        in_specs=(
            P(("rep", "blk"), None),
            P(),
            P(),
            P("rep", None),
            P("rep"),
            P(),
            P(None, "blk"),
            P("blk"),
            P("blk", None),
            P("blk", None),
            P(),
            P(None, "blk"),
        ),
        out_specs=P(("rep", "blk"), None),
        check_vma=False,
    )
```

```python
import functools

import jax
import jax.numpy as jnp
from jax import lax
from jax.experimental import pallas as pl
from jax.experimental.pallas import tpu as pltpu
from jax.sharding import PartitionSpec as P

MIB = 1 << 20
VMEM = pl.BlockSpec(memory_space=pltpu.VMEM)
HBM = pl.BlockSpec(memory_space=pltpu.HBM)
SMEM = pl.BlockSpec(memory_space=pltpu.SMEM)
f32, bf16 = jnp.float32, jnp.bfloat16


def piece(width, most):
    size = 128
    while size * 2 <= most and width % (size * 2) == 0:
        size *= 2
    return size


def window(index, size):
    return pl.ds(pl.multiple_of(index * size, 128), size)


def call(body, outs, ins, limit, scratch=(), moved=2 * MIB):
    return pl.pallas_call(
        body,
        out_shape=outs,
        in_specs=ins,
        out_specs=[VMEM] * len(outs),
        scratch_shapes=list(scratch),
        compiler_params=pltpu.CompilerParams(vmem_limit_bytes=limit * MIB),
        cost_estimate=pl.CostEstimate(flops=0, bytes_accessed=moved, transcendentals=0),
    )


def normal(hidden, gain, shift):
    wide = hidden.astype(f32)
    mean = jnp.mean(wide, axis=-1, keepdims=True)
    centred = wide - mean
    variance = jnp.mean(centred * centred, axis=-1, keepdims=True)
    return (centred * lax.rsqrt(variance + 1e-05) * gain + shift).astype(bf16)


def load_body(count, *refs):
    srcs, dsts, sems = refs[:count], refs[count : 2 * count], refs[2 * count]
    copies = [pltpu.make_async_copy(srcs[i], dsts[i], sems.at[i]) for i in range(count)]
    for copy in copies:
        copy.start()
    for copy in copies:
        copy.wait()


def early_body(groups, soon, *refs):
    held, (gain, shift, near, far) = refs[: groups + soon], refs[groups + soon :]
    rows = held[0].shape[0]
    for out, some in ((near, held[:groups]), (far, held[groups:])):
        for i in range(0, len(some), 2):
            pair = jnp.concatenate([h[...] for h in some[i : i + 2]], axis=0)
            out[i * rows : i * rows + pair.shape[0], :] = normal(pair, gain[...], shift[...])


def norm_body(count, place, *refs):
    held, (near, first, gain, shift, own, mate, far, total, message) = refs[:count], refs[count:]
    rows, done = held[0].shape[0], first.shape[0]
    far[:done, :] = first[...]
    for i in range(0, count, 2):
        pair = jnp.concatenate([h[...] for h in held[i : i + 2]], axis=0)
        far[done + i * rows : done + i * rows + pair.shape[0], :] = normal(pair, gain[...], shift[...])
    share = own.shape[0]
    core = place[0] % 2
    at = window(place[0] // 2, 2 * share)
    columns = jnp.concatenate([near[:, at].astype(f32), far[:, at].astype(f32)], axis=0)
    low, high = columns[:, :share], columns[:, share:]
    mine = jnp.where(core == 0, low, high).astype(bf16)
    other = jnp.where(core == 0, high, low).astype(bf16)
    sums = jnp.dot(mine, own[...], preferred_element_type=f32) + jnp.dot(
        other, mate[...], preferred_element_type=f32
    )
    half = near.shape[0]
    total[...] = sums
    message[:half, :] = sums[half:].astype(bf16)
    message[half:, :] = sums[:half].astype(bf16)


def turn(x, groups, bit):
    rows = x.shape[0] // (2 * groups)
    at = [h * groups + (k ^ bit) for h in range(2) for k in range(groups)]
    return jnp.concatenate([x[i * rows : (i + 1) * rows] for i in at], axis=0)


def merge_body(groups, total, got, out, *messages):
    sums = total[...] + got[...].astype(f32)
    out[...] = sums
    for k in range(1, groups):
        messages[k - 1][...] = turn(sums, groups, k).astype(bf16)


def up_body(groups, place, total, bias, own, mate, part, *refs):
    got, outs = refs[: groups - 1], refs[groups - 1 :]
    sums = total[...]
    for g in got:
        sums = sums + g[...].astype(f32)
    hidden = jnp.maximum(sums + bias[...], 0.0).astype(bf16)
    core = place[0] % 2
    mine = jnp.dot(hidden, own[...], preferred_element_type=f32)
    other = jnp.dot(hidden, mate[...], preferred_element_type=f32)
    both = jnp.concatenate([jnp.where(core == 0, mine, other), jnp.where(core == 0, other, mine)], axis=1)
    at = window(place[0] // 2, both.shape[1])
    rows = outs[0].shape[0]
    for q in range(2 * groups):
        some = slice(q * rows, (q + 1) * rows)
        outs[q][...] = part[some, :].astype(outs[q].dtype)
        outs[q][:, at] = (part[some, at] + both[some]).astype(outs[q].dtype)


def last_body(groups, *refs):
    sums, out = refs[:groups], refs[groups]
    total = sums[0][...]
    for k in range(1, groups):
        total = total + sums[k][...].astype(f32)
    out[...] = total.astype(bf16)


def act_body(step, near, far, w_own, w_mate, b_own, b_mate, mask, out):
    total = jnp.zeros(out.shape, f32)
    for i in range(near.shape[1] // step):
        at = slice(i * step, (i + 1) * step)
        rows = jnp.concatenate([near[:, at], far[:, at]], axis=0)
        both = jnp.concatenate([w_own[at, :], w_mate[at, :]], axis=1)
        total = total + jnp.dot(rows, both, preferred_element_type=f32)
    bias = jnp.concatenate([b_own[...], b_mate[...]], axis=1)
    out[...] = (jnp.maximum(total + bias, 0.0) * mask[...]).astype(bf16)


def part_body(step, act, w_own, w_mate, out):
    for i in range(out.shape[1] // step):
        at = slice(i * step, (i + 1) * step)
        both = jnp.concatenate([w_own[:, at], w_mate[:, at]], axis=0)
        out[:, at] = jnp.dot(act[...], both, preferred_element_type=f32)


def activity(lists, counts, block_slot):
    groups, top = lists.shape
    nblocks = block_slot.shape[0]
    names = jnp.arange(nblocks, dtype=jnp.int32)
    live = (jnp.arange(top, dtype=jnp.int32)[None, :] < counts[:, None]).astype(jnp.int32)
    hits = (lists[:, :, None] == names[None, None, :]).astype(jnp.int32) * live[:, :, None]
    by_block = jnp.sum(hits, axis=1)
    placed = (block_slot[:, None] == names[None, :]).astype(jnp.int32)
    return jnp.sum(by_block[:, :, None] * placed[None, :, :], axis=1)


def shards(
    hidden,
    ln_gain,
    ln_shift,
    lists,
    counts,
    block_slot,
    w_in,
    b_in,
    w_out,
    low_in,
    low_bias,
    low_out,
):
    devices = lax.axis_size("blk")
    position = lax.axis_index("blk")
    row_dev, width = hidden.shape
    groups = lists.shape[0]
    share, rank = low_in.shape
    block = w_in.shape[1]
    assert devices == 4 * groups
    plane = position // 4
    place = jnp.reshape(position, (1,)).astype(jnp.int32)
    some, rows = groups * row_dev, 2 * groups * row_dev

    def across(x, k):
        return lax.ppermute(x, "blk", [(i, i ^ (4 * k)) for i in range(devices)])

    def beside(x):
        return lax.ppermute(x, "blk", [(i, i ^ 2) for i in range(devices)])

    def core(x):
        return lax.ppermute(x, "blk", [(i, i ^ 1) for i in range(devices)])

    def shape(*dims, dtype=bf16):
        return jax.ShapeDtypeStruct(dims, dtype)

    gain, shift, bias = ln_gain.reshape(1, width), ln_shift.reshape(1, width), b_in.reshape(1, block)
    span = 2 * share

    table = activity(lists, counts, block_slot)
    by = plane ^ jnp.arange(groups)
    at = position ^ jnp.arange(2)
    relate = (by[:, None] == jnp.arange(groups)[None, :])[:, None, :, None]
    choose = (at[:, None] == jnp.arange(devices)[None, :])[None, :, None, :]
    live = jnp.sum(jnp.where(relate & choose, table[None, None], 0), axis=(2, 3)).astype(f32)
    mask = jnp.broadcast_to(live[None, :, None, :, None], (2, groups, row_dev, 2, block)).reshape(rows, 2 * block)

    start, bias_mate = lax.optimization_barrier((hidden, core(bias)))
    held = [hidden] + [across(start, k) for k in range(1, groups)]
    w_in_mate = core(w_in)
    held[1], low_in_sent, mask = lax.optimization_barrier((held[1], low_in, mask))
    low_in_mate = core(low_in_sent)
    beyond = [beside(h) for h in [start] + held[1:]]
    near = (hidden, gain, shift, low_in, w_in, w_out, low_out)
    *near, mask, beyond[0] = lax.optimization_barrier((*near, mask, beyond[0]))
    near = call(
        functools.partial(load_body, len(near)),
        [shape(*x.shape, dtype=x.dtype) for x in near],
        [HBM] * len(near),
        16,
        [pltpu.SemaphoreType.DMA((len(near),))],
        8 * MIB,
    )(*[pltpu.with_memory_space_constraint(x, pltpu.HBM) for x in near])
    hidden_near, gain, shift, low_in, w_in, w_out_near, low_out_near = near
    *_, w_in_mate, w_out_sent, low_out_sent = lax.optimization_barrier(
        (*held, *beyond[: groups // 2], w_in_mate, w_out, low_out)
    )
    w_out_mate, low_out_mate = core(w_out_sent), core(low_out_sent)
    held[0] = hidden_near

    soon = groups // 2
    normed, first = call(
        functools.partial(early_body, groups, soon),
        [shape(some, width), shape(soon * row_dev, width)],
        [VMEM] * (groups + soon + 2),
        16,
        (),
        4 * MIB,
    )(*held, *beyond[:soon], gain, shift)
    far, total, message = call(
        functools.partial(norm_body, groups - soon),
        [shape(some, width), shape(rows, rank, dtype=f32), shape(rows, rank)],
        [SMEM] + [VMEM] * (groups - soon + 6),
        16,
        (),
        4 * MIB,
    )(place, *beyond[soon:], normed, first, gain, shift, low_in, low_in_mate)
    got = beside(message)
    step = piece(width, 2048)
    act = call(
        functools.partial(act_body, step),
        [shape(rows, 2 * block)],
        [VMEM] * 7,
        16,
        (),
        4 * MIB,
    )(normed, far, w_in, w_in_mate, bias, bias_mate, mask)[0]
    total, *messages = call(
        functools.partial(merge_body, groups),
        [shape(rows, rank, dtype=f32)] + [shape(rows, rank)] * (groups - 1),
        [VMEM] * 2,
        16,
    )(total, got)
    got = [across(messages[k - 1], k) for k in range(groups - 1, 0, -1)]
    part = call(
        functools.partial(part_body, step),
        [shape(rows, width, dtype=f32)],
        [VMEM] * 3,
        16,
        (),
        6 * MIB,
    )(act, w_out_near, w_out_mate)[0]
    parts = call(
        functools.partial(up_body, groups),
        [shape(row_dev, width, dtype=f32)] * groups + [shape(row_dev, width)] * groups,
        [SMEM] + [VMEM] * (groups + 4),
        16,
        (),
        6 * MIB,
    )(place, total, low_bias.reshape(1, rank), low_out_near, low_out_mate, part, *got)

    sums = []
    for k in range(groups - 1, -1, -1):
        here = parts[k] + beside(parts[groups + k]).astype(f32)
        sums.append(across(here.astype(bf16), k) if k else here)
    return call(functools.partial(last_body, groups), [shape(row_dev, width)], [VMEM] * groups, 16)(*sums[::-1])[0]


def solution(mesh):
    return jax.shard_map(
        shards,
        mesh=mesh,
        in_specs=(
            P(("rep", "blk"), None),
            P(),
            P(),
            P("rep", None),
            P("rep"),
            P(),
            P(None, "blk"),
            P("blk"),
            P("blk", None),
            P("blk", None),
            P(),
            P(None, "blk"),
        ),
        out_specs=P(("rep", "blk"), None),
        check_vma=False,
    )
```

```python
import functools

import jax
import jax.numpy as jnp
from jax import lax
from jax.experimental import pallas as pl
from jax.experimental.pallas import tpu as pltpu
from jax.sharding import PartitionSpec as P

MIB = 1 << 20
VMEM = pl.BlockSpec(memory_space=pltpu.VMEM)
HBM = pl.BlockSpec(memory_space=pltpu.HBM)
SMEM = pl.BlockSpec(memory_space=pltpu.SMEM)
f32, bf16 = jnp.float32, jnp.bfloat16


def piece(width, most):
    size = 128
    while size * 2 <= most and width % (size * 2) == 0:
        size *= 2
    return size


def window(index, size):
    return pl.ds(pl.multiple_of(index * size, 128), size)


def call(body, outs, ins, limit, scratch=(), moved=2 * MIB):
    return pl.pallas_call(
        body,
        out_shape=outs,
        in_specs=ins,
        out_specs=[VMEM] * len(outs),
        scratch_shapes=list(scratch),
        compiler_params=pltpu.CompilerParams(vmem_limit_bytes=limit * MIB),
        cost_estimate=pl.CostEstimate(flops=0, bytes_accessed=moved, transcendentals=0),
    )


def normal(hidden, gain, shift):
    wide = hidden.astype(f32)
    mean = jnp.mean(wide, axis=-1, keepdims=True)
    centred = wide - mean
    variance = jnp.mean(centred * centred, axis=-1, keepdims=True)
    return (centred * lax.rsqrt(variance + 1e-05) * gain + shift).astype(bf16)


def load_body(count, *refs):
    srcs, dsts, sems = refs[:count], refs[count : 2 * count], refs[2 * count]
    copies = [pltpu.make_async_copy(srcs[i], dsts[i], sems.at[i]) for i in range(count)]
    for copy in copies:
        copy.start()
    for copy in copies:
        copy.wait()


def early_body(groups, soon, *refs):
    held, (gain, shift, near, far) = refs[: groups + soon], refs[groups + soon :]
    rows = held[0].shape[0]
    for out, some in ((near, held[:groups]), (far, held[groups:])):
        for i in range(0, len(some), 2):
            pair = jnp.concatenate([h[...] for h in some[i : i + 2]], axis=0)
            out[i * rows : i * rows + pair.shape[0], :] = normal(pair, gain[...], shift[...])


def norm_body(count, place, *refs):
    held, (near, first, gain, shift, own, mate, far, total, message) = refs[:count], refs[count:]
    rows, done = held[0].shape[0], first.shape[0]
    far[:done, :] = first[...]
    for i in range(0, count, 2):
        pair = jnp.concatenate([h[...] for h in held[i : i + 2]], axis=0)
        far[done + i * rows : done + i * rows + pair.shape[0], :] = normal(pair, gain[...], shift[...])
    share = own.shape[0]
    core = place[0] % 2
    at = window(place[0] // 2, 2 * share)
    columns = jnp.concatenate([near[:, at].astype(f32), far[:, at].astype(f32)], axis=0)
    low, high = columns[:, :share], columns[:, share:]
    mine = jnp.where(core == 0, low, high).astype(bf16)
    other = jnp.where(core == 0, high, low).astype(bf16)
    sums = jnp.dot(mine, own[...], preferred_element_type=f32) + jnp.dot(
        other, mate[...], preferred_element_type=f32
    )
    half = near.shape[0]
    total[...] = sums
    message[:half, :] = sums[half:].astype(bf16)
    message[half:, :] = sums[:half].astype(bf16)


def turn(x, groups, bit):
    rows = x.shape[0] // (2 * groups)
    at = [h * groups + (k ^ bit) for h in range(2) for k in range(groups)]
    return jnp.concatenate([x[i * rows : (i + 1) * rows] for i in at], axis=0)


def merge_body(groups, total, got, out, *messages):
    sums = total[...] + got[...].astype(f32)
    out[...] = sums
    for k in range(1, groups):
        messages[k - 1][...] = turn(sums, groups, k).astype(bf16)


def up_body(groups, place, total, bias, own, mate, part, *refs):
    got, outs = refs[: groups - 1], refs[groups - 1 :]
    sums = total[...]
    for g in got:
        sums = sums + g[...].astype(f32)
    hidden = jnp.maximum(sums + bias[...], 0.0).astype(bf16)
    core = place[0] % 2
    mine = jnp.dot(hidden, own[...], preferred_element_type=f32)
    other = jnp.dot(hidden, mate[...], preferred_element_type=f32)
    both = jnp.concatenate([jnp.where(core == 0, mine, other), jnp.where(core == 0, other, mine)], axis=1)
    at = window(place[0] // 2, both.shape[1])
    rows = outs[0].shape[0]
    for q in range(2 * groups):
        some = slice(q * rows, (q + 1) * rows)
        outs[q][...] = part[some, :].astype(outs[q].dtype)
        outs[q][:, at] = (part[some, at] + both[some]).astype(outs[q].dtype)


def last_body(groups, *refs):
    sums, out = refs[:groups], refs[groups]
    total = sums[0][...]
    for k in range(1, groups):
        total = total + sums[k][...].astype(f32)
    out[...] = total.astype(bf16)


def act_body(step, near, far, w_own, w_mate, b_own, b_mate, mask, out):
    total = jnp.zeros(out.shape, f32)
    for i in range(near.shape[1] // step):
        at = slice(i * step, (i + 1) * step)
        rows = jnp.concatenate([near[:, at], far[:, at]], axis=0)
        both = jnp.concatenate([w_own[at, :], w_mate[at, :]], axis=1)
        total = total + jnp.dot(rows, both, preferred_element_type=f32)
    bias = jnp.concatenate([b_own[...], b_mate[...]], axis=1)
    out[...] = (jnp.maximum(total + bias, 0.0) * mask[...]).astype(bf16)


def part_body(step, act, w_own, w_mate, out):
    for i in range(out.shape[1] // step):
        at = slice(i * step, (i + 1) * step)
        both = jnp.concatenate([w_own[:, at], w_mate[:, at]], axis=0)
        out[:, at] = jnp.dot(act[...], both, preferred_element_type=f32)


def activity(lists, counts, block_slot):
    groups, top = lists.shape
    nblocks = block_slot.shape[0]
    names = jnp.arange(nblocks, dtype=jnp.int32)
    live = (jnp.arange(top, dtype=jnp.int32)[None, :] < counts[:, None]).astype(jnp.int32)
    hits = (lists[:, :, None] == names[None, None, :]).astype(jnp.int32) * live[:, :, None]
    by_block = jnp.sum(hits, axis=1)
    placed = (block_slot[:, None] == names[None, :]).astype(jnp.int32)
    return jnp.sum(by_block[:, :, None] * placed[None, :, :], axis=1)


def shards(
    hidden,
    ln_gain,
    ln_shift,
    lists,
    counts,
    block_slot,
    w_in,
    b_in,
    w_out,
    low_in,
    low_bias,
    low_out,
):
    devices = lax.axis_size("blk")
    position = lax.axis_index("blk")
    row_dev, width = hidden.shape
    groups = lists.shape[0]
    share, rank = low_in.shape
    block = w_in.shape[1]
    assert devices == 4 * groups
    plane = position // 4
    place = jnp.reshape(position, (1,)).astype(jnp.int32)
    some, rows = groups * row_dev, 2 * groups * row_dev

    def across(x, k):
        return lax.ppermute(x, "blk", [(i, i ^ (4 * k)) for i in range(devices)])

    def beside(x):
        return lax.ppermute(x, "blk", [(i, i ^ 2) for i in range(devices)])

    def core(x):
        return lax.ppermute(x, "blk", [(i, i ^ 1) for i in range(devices)])

    def shape(*dims, dtype=bf16):
        return jax.ShapeDtypeStruct(dims, dtype)

    gain, shift, bias = ln_gain.reshape(1, width), ln_shift.reshape(1, width), b_in.reshape(1, block)
    span = 2 * share

    table = activity(lists, counts, block_slot)
    by = plane ^ jnp.arange(groups)
    at = position ^ jnp.arange(2)
    relate = (by[:, None] == jnp.arange(groups)[None, :])[:, None, :, None]
    choose = (at[:, None] == jnp.arange(devices)[None, :])[None, :, None, :]
    live = jnp.sum(jnp.where(relate & choose, table[None, None], 0), axis=(2, 3)).astype(f32)
    mask = jnp.broadcast_to(live[None, :, None, :, None], (2, groups, row_dev, 2, block)).reshape(rows, 2 * block)

    held = [hidden] + [across(hidden, k) for k in range(1, groups)]
    w_in_mate = core(w_in)
    held[1], low_in_sent, mask = lax.optimization_barrier((held[1], low_in, mask))
    low_in_mate = core(low_in_sent)
    beyond = [beside(h) for h in held]
    near = (hidden, gain, shift, low_in, w_in, w_out, low_out)
    *near, mask, beyond[0] = lax.optimization_barrier((*near, mask, beyond[0]))
    near = call(
        functools.partial(load_body, len(near)),
        [shape(*x.shape, dtype=x.dtype) for x in near],
        [HBM] * len(near),
        16,
        [pltpu.SemaphoreType.DMA((len(near),))],
        8 * MIB,
    )(*[pltpu.with_memory_space_constraint(x, pltpu.HBM) for x in near])
    hidden_near, gain, shift, low_in, w_in, w_out_near, low_out_near = near
    *_, w_in_mate, w_out_sent, low_out_sent, bias_sent = lax.optimization_barrier(
        (*held, *beyond[: groups // 2], w_in_mate, w_out, low_out, bias)
    )
    bias_mate, w_out_mate, low_out_mate = core(bias_sent), core(w_out_sent), core(low_out_sent)
    held[0] = hidden_near

    soon = groups // 2
    normed, first = call(
        functools.partial(early_body, groups, soon),
        [shape(some, width), shape(soon * row_dev, width)],
        [VMEM] * (groups + soon + 2),
        16,
        (),
        4 * MIB,
    )(*held, *beyond[:soon], gain, shift)
    far, total, message = call(
        functools.partial(norm_body, groups - soon),
        [shape(some, width), shape(rows, rank, dtype=f32), shape(rows, rank)],
        [SMEM] + [VMEM] * (groups - soon + 6),
        16,
        (),
        4 * MIB,
    )(place, *beyond[soon:], normed, first, gain, shift, low_in, low_in_mate)
    got = beside(message)
    step = piece(width, 2048)
    act = call(
        functools.partial(act_body, step),
        [shape(rows, 2 * block)],
        [VMEM] * 7,
        16,
        (),
        4 * MIB,
    )(normed, far, w_in, w_in_mate, bias, bias_mate, mask)[0]
    total, *messages = call(
        functools.partial(merge_body, groups),
        [shape(rows, rank, dtype=f32)] + [shape(rows, rank)] * (groups - 1),
        [VMEM] * 2,
        16,
    )(total, got)
    got = [across(messages[k - 1], k) for k in range(groups - 1, 0, -1)]
    part = call(
        functools.partial(part_body, step),
        [shape(rows, width, dtype=f32)],
        [VMEM] * 3,
        16,
        (),
        6 * MIB,
    )(act, w_out_near, w_out_mate)[0]
    parts = call(
        functools.partial(up_body, groups),
        [shape(row_dev, width, dtype=f32)] * groups + [shape(row_dev, width)] * groups,
        [SMEM] + [VMEM] * (groups + 4),
        16,
        (),
        6 * MIB,
    )(place, total, low_bias.reshape(1, rank), low_out_near, low_out_mate, part, *got)

    sums = []
    for k in range(groups - 1, -1, -1):
        here = parts[k] + beside(parts[groups + k]).astype(f32)
        sums.append(across(here.astype(bf16), k) if k else here)
    return call(functools.partial(last_body, groups), [shape(row_dev, width)], [VMEM] * groups, 16)(*sums[::-1])[0]


def solution(mesh):
    return jax.shard_map(
        shards,
        mesh=mesh,
        in_specs=(
            P(("rep", "blk"), None),
            P(),
            P(),
            P("rep", None),
            P("rep"),
            P(),
            P(None, "blk"),
            P("blk"),
            P("blk", None),
            P("blk", None),
            P(),
            P(None, "blk"),
        ),
        out_specs=P(("rep", "blk"), None),
        check_vma=False,
    )
```

```python
import functools

import jax
import jax.numpy as jnp
from jax import lax
from jax.experimental import pallas as pl
from jax.experimental.pallas import tpu as pltpu
from jax.sharding import PartitionSpec as P

MIB = 1 << 20
VMEM = pl.BlockSpec(memory_space=pltpu.VMEM)
HBM = pl.BlockSpec(memory_space=pltpu.HBM)
SMEM = pl.BlockSpec(memory_space=pltpu.SMEM)
f32, bf16 = jnp.float32, jnp.bfloat16


def piece(width, most):
    size = 128
    while size * 2 <= most and width % (size * 2) == 0:
        size *= 2
    return size


def window(index, size):
    return pl.ds(pl.multiple_of(index * size, 128), size)


def call(body, outs, ins, limit, scratch=(), moved=2 * MIB):
    return pl.pallas_call(
        body,
        out_shape=outs,
        in_specs=ins,
        out_specs=[VMEM] * len(outs),
        scratch_shapes=list(scratch),
        compiler_params=pltpu.CompilerParams(vmem_limit_bytes=limit * MIB),
        cost_estimate=pl.CostEstimate(flops=0, bytes_accessed=moved, transcendentals=0),
    )


def normal(hidden, gain, shift):
    wide = hidden.astype(f32)
    mean = jnp.mean(wide, axis=-1, keepdims=True)
    centred = wide - mean
    variance = jnp.mean(centred * centred, axis=-1, keepdims=True)
    return (centred * lax.rsqrt(variance + 1e-05) * gain + shift).astype(bf16)


def load_body(count, *refs):
    srcs, dsts, sems = refs[:count], refs[count : 2 * count], refs[2 * count]
    copies = [pltpu.make_async_copy(srcs[i], dsts[i], sems.at[i]) for i in range(count)]
    for copy in copies:
        copy.start()
    for copy in copies:
        copy.wait()


def early_body(groups, soon, *refs):
    held, (gain, shift, near, far) = refs[: groups + soon], refs[groups + soon :]
    rows = held[0].shape[0]
    for out, some in ((near, held[:groups]), (far, held[groups:])):
        for i in range(0, len(some), 2):
            pair = jnp.concatenate([h[...] for h in some[i : i + 2]], axis=0)
            out[i * rows : i * rows + pair.shape[0], :] = normal(pair, gain[...], shift[...])


def norm_body(count, place, *refs):
    held, (near, first, gain, shift, own, mate, far, total, message) = refs[:count], refs[count:]
    rows, done = held[0].shape[0], first.shape[0]
    far[:done, :] = first[...]
    for i in range(0, count, 2):
        pair = jnp.concatenate([h[...] for h in held[i : i + 2]], axis=0)
        far[done + i * rows : done + i * rows + pair.shape[0], :] = normal(pair, gain[...], shift[...])
    share = own.shape[0]
    core = place[0] % 2
    at = window(place[0] // 2, 2 * share)
    columns = jnp.concatenate([near[:, at].astype(f32), far[:, at].astype(f32)], axis=0)
    low, high = columns[:, :share], columns[:, share:]
    mine = jnp.where(core == 0, low, high).astype(bf16)
    other = jnp.where(core == 0, high, low).astype(bf16)
    sums = jnp.dot(mine, own[...], preferred_element_type=f32) + jnp.dot(
        other, mate[...], preferred_element_type=f32
    )
    half = near.shape[0]
    total[...] = sums
    message[:half, :] = sums[half:].astype(bf16)
    message[half:, :] = sums[:half].astype(bf16)


def turn(x, groups, bit):
    rows = x.shape[0] // (2 * groups)
    at = [h * groups + (k ^ bit) for h in range(2) for k in range(groups)]
    return jnp.concatenate([x[i * rows : (i + 1) * rows] for i in at], axis=0)


def merge_body(groups, total, got, out, *messages):
    sums = total[...] + got[...].astype(f32)
    out[...] = sums
    for k in range(1, groups):
        messages[k - 1][...] = turn(sums, groups, k).astype(bf16)


def up_body(groups, place, total, bias, own, mate, part, *refs):
    got, outs = refs[: groups - 1], refs[groups - 1 :]
    sums = total[...]
    for g in got:
        sums = sums + g[...].astype(f32)
    hidden = jnp.maximum(sums + bias[...], 0.0).astype(bf16)
    core = place[0] % 2
    mine = jnp.dot(hidden, own[...], preferred_element_type=f32)
    other = jnp.dot(hidden, mate[...], preferred_element_type=f32)
    both = jnp.concatenate([jnp.where(core == 0, mine, other), jnp.where(core == 0, other, mine)], axis=1)
    at = window(place[0] // 2, both.shape[1])
    rows = outs[0].shape[0]
    for q in range(2 * groups):
        some = slice(q * rows, (q + 1) * rows)
        outs[q][...] = part[some, :].astype(outs[q].dtype)
        outs[q][:, at] = (part[some, at] + both[some]).astype(outs[q].dtype)


def last_body(groups, *refs):
    sums, out = refs[:groups], refs[groups]
    total = sums[0][...]
    for k in range(1, groups):
        total = total + sums[k][...].astype(f32)
    out[...] = total.astype(bf16)


def act_body(step, near, far, w_own, w_mate, b_own, b_mate, mask, out):
    total = jnp.zeros(out.shape, f32)
    for i in range(near.shape[1] // step):
        at = slice(i * step, (i + 1) * step)
        rows = jnp.concatenate([near[:, at], far[:, at]], axis=0)
        both = jnp.concatenate([w_own[at, :], w_mate[at, :]], axis=1)
        total = total + jnp.dot(rows, both, preferred_element_type=f32)
    bias = jnp.concatenate([b_own[...], b_mate[...]], axis=1)
    out[...] = (jnp.maximum(total + bias, 0.0) * mask[...]).astype(bf16)


def part_body(step, act, w_own, w_mate, out):
    for i in range(out.shape[1] // step):
        at = slice(i * step, (i + 1) * step)
        both = jnp.concatenate([w_own[:, at], w_mate[:, at]], axis=0)
        out[:, at] = jnp.dot(act[...], both, preferred_element_type=f32)


def activity(lists, counts, block_slot):
    groups, top = lists.shape
    nblocks = block_slot.shape[0]
    names = jnp.arange(nblocks, dtype=jnp.int32)
    live = (jnp.arange(top, dtype=jnp.int32)[None, :] < counts[:, None]).astype(jnp.int32)
    hits = (lists[:, :, None] == names[None, None, :]).astype(jnp.int32) * live[:, :, None]
    by_block = jnp.sum(hits, axis=1)
    placed = (block_slot[:, None] == names[None, :]).astype(jnp.int32)
    return jnp.sum(by_block[:, :, None] * placed[None, :, :], axis=1)


def shards(
    hidden,
    ln_gain,
    ln_shift,
    lists,
    counts,
    block_slot,
    w_in,
    b_in,
    w_out,
    low_in,
    low_bias,
    low_out,
):
    devices = lax.axis_size("blk")
    position = lax.axis_index("blk")
    row_dev, width = hidden.shape
    groups = lists.shape[0]
    share, rank = low_in.shape
    block = w_in.shape[1]
    assert devices == 4 * groups
    plane = position // 4
    place = jnp.reshape(position, (1,)).astype(jnp.int32)
    some, rows = groups * row_dev, 2 * groups * row_dev

    def across(x, k):
        return lax.ppermute(x, "blk", [(i, i ^ (4 * k)) for i in range(devices)])

    def beside(x):
        return lax.ppermute(x, "blk", [(i, i ^ 2) for i in range(devices)])

    def core(x):
        return lax.ppermute(x, "blk", [(i, i ^ 1) for i in range(devices)])

    def shape(*dims, dtype=bf16):
        return jax.ShapeDtypeStruct(dims, dtype)

    gain, shift, bias = ln_gain.reshape(1, width), ln_shift.reshape(1, width), b_in.reshape(1, block)
    span = 2 * share

    held = [hidden] + [across(hidden, k) for k in range(1, groups)]
    w_in_mate = core(w_in)
    held[1], lists, counts, block_slot = lax.optimization_barrier((held[1], lists, counts, block_slot))

    table = activity(lists, counts, block_slot)
    by = plane ^ jnp.arange(groups)
    at = position ^ jnp.arange(2)
    relate = (by[:, None] == jnp.arange(groups)[None, :])[:, None, :, None]
    choose = (at[:, None] == jnp.arange(devices)[None, :])[None, :, None, :]
    live = jnp.sum(jnp.where(relate & choose, table[None, None], 0), axis=(2, 3)).astype(f32)
    mask = jnp.broadcast_to(live[None, :, None, :, None], (2, groups, row_dev, 2, block)).reshape(rows, 2 * block)

    low_in_sent, mask = lax.optimization_barrier((low_in, mask))
    low_in_mate = core(low_in_sent)
    early, bias_mate = lax.optimization_barrier((hidden, core(bias)))
    beyond = [beside(h) for h in [early] + held[1:]]
    near = (hidden, gain, shift, low_in, w_in, w_out, low_out)
    *near, mask, beyond[0] = lax.optimization_barrier((*near, mask, beyond[0]))
    near = call(
        functools.partial(load_body, len(near)),
        [shape(*x.shape, dtype=x.dtype) for x in near],
        [HBM] * len(near),
        16,
        [pltpu.SemaphoreType.DMA((len(near),))],
        8 * MIB,
    )(*[pltpu.with_memory_space_constraint(x, pltpu.HBM) for x in near])
    hidden_near, gain, shift, low_in, w_in, w_out_near, low_out_near = near
    *_, w_in_mate, w_out_sent, low_out_sent = lax.optimization_barrier(
        (*held, *beyond[: groups // 2], w_in_mate, w_out, low_out)
    )
    w_out_mate, low_out_mate = core(w_out_sent), core(low_out_sent)
    held[0] = hidden_near

    soon = groups // 2
    normed, first = call(
        functools.partial(early_body, groups, soon),
        [shape(some, width), shape(soon * row_dev, width)],
        [VMEM] * (groups + soon + 2),
        16,
        (),
        4 * MIB,
    )(*held, *beyond[:soon], gain, shift)
    far, total, message = call(
        functools.partial(norm_body, groups - soon),
        [shape(some, width), shape(rows, rank, dtype=f32), shape(rows, rank)],
        [SMEM] + [VMEM] * (groups - soon + 6),
        16,
        (),
        4 * MIB,
    )(place, *beyond[soon:], normed, first, gain, shift, low_in, low_in_mate)
    got = beside(message)
    step = piece(width, 2048)
    act = call(
        functools.partial(act_body, step),
        [shape(rows, 2 * block)],
        [VMEM] * 7,
        16,
        (),
        4 * MIB,
    )(normed, far, w_in, w_in_mate, bias, bias_mate, mask)[0]
    total, *messages = call(
        functools.partial(merge_body, groups),
        [shape(rows, rank, dtype=f32)] + [shape(rows, rank)] * (groups - 1),
        [VMEM] * 2,
        16,
    )(total, got)
    got = [across(messages[k - 1], k) for k in range(groups - 1, 0, -1)]
    part = call(
        functools.partial(part_body, step),
        [shape(rows, width, dtype=f32)],
        [VMEM] * 3,
        16,
        (),
        6 * MIB,
    )(act, w_out_near, w_out_mate)[0]
    parts = call(
        functools.partial(up_body, groups),
        [shape(row_dev, width, dtype=f32)] * groups + [shape(row_dev, width)] * groups,
        [SMEM] + [VMEM] * (groups + 4),
        16,
        (),
        6 * MIB,
    )(place, total, low_bias.reshape(1, rank), low_out_near, low_out_mate, part, *got)

    sums = []
    for k in range(groups - 1, -1, -1):
        here = parts[k] + beside(parts[groups + k]).astype(f32)
        sums.append(across(here.astype(bf16), k) if k else here)
    return call(functools.partial(last_body, groups), [shape(row_dev, width)], [VMEM] * groups, 16)(*sums[::-1])[0]


def solution(mesh):
    return jax.shard_map(
        shards,
        mesh=mesh,
        in_specs=(
            P(("rep", "blk"), None),
            P(),
            P(),
            P("rep", None),
            P("rep"),
            P(),
            P(None, "blk"),
            P("blk"),
            P("blk", None),
            P("blk", None),
            P(),
            P(None, "blk"),
        ),
        out_specs=P(("rep", "blk"), None),
        check_vma=False,
    )
```

```python
import functools

import jax
import jax.numpy as jnp
from jax import lax
from jax.experimental import pallas as pl
from jax.experimental.pallas import tpu as pltpu
from jax.sharding import PartitionSpec as P

MIB = 1 << 20
VMEM = pl.BlockSpec(memory_space=pltpu.VMEM)
HBM = pl.BlockSpec(memory_space=pltpu.HBM)
SMEM = pl.BlockSpec(memory_space=pltpu.SMEM)
f32, bf16 = jnp.float32, jnp.bfloat16


def piece(width, most):
    size = 128
    while size * 2 <= most and width % (size * 2) == 0:
        size *= 2
    return size


def window(index, size):
    return pl.ds(pl.multiple_of(index * size, 128), size)


def call(body, outs, ins, limit, scratch=(), moved=2 * MIB):
    return pl.pallas_call(
        body,
        out_shape=outs,
        in_specs=ins,
        out_specs=[VMEM] * len(outs),
        scratch_shapes=list(scratch),
        compiler_params=pltpu.CompilerParams(vmem_limit_bytes=limit * MIB),
        cost_estimate=pl.CostEstimate(flops=0, bytes_accessed=moved, transcendentals=0),
    )


def normal(hidden, gain, shift):
    wide = hidden.astype(f32)
    mean = jnp.mean(wide, axis=-1, keepdims=True)
    centred = wide - mean
    variance = jnp.mean(centred * centred, axis=-1, keepdims=True)
    return (centred * lax.rsqrt(variance + 1e-05) * gain + shift).astype(bf16)


def load_body(count, *refs):
    srcs, dsts, sems = refs[:count], refs[count : 2 * count], refs[2 * count]
    copies = [pltpu.make_async_copy(srcs[i], dsts[i], sems.at[i]) for i in range(count)]
    for copy in copies:
        copy.start()
    for copy in copies:
        copy.wait()


def early_body(groups, soon, *refs):
    held, (gain, shift, near, far) = refs[: groups + soon], refs[groups + soon :]
    rows = held[0].shape[0]
    for out, some in ((near, held[:groups]), (far, held[groups:])):
        for i in range(0, len(some), 2):
            pair = jnp.concatenate([h[...] for h in some[i : i + 2]], axis=0)
            out[i * rows : i * rows + pair.shape[0], :] = normal(pair, gain[...], shift[...])


def norm_body(count, place, *refs):
    held, (near, first, gain, shift, own, mate, far, total, message) = refs[:count], refs[count:]
    rows, done = held[0].shape[0], first.shape[0]
    far[:done, :] = first[...]
    for i in range(0, count, 2):
        pair = jnp.concatenate([h[...] for h in held[i : i + 2]], axis=0)
        far[done + i * rows : done + i * rows + pair.shape[0], :] = normal(pair, gain[...], shift[...])
    share = own.shape[0]
    core = place[0] % 2
    at = window(place[0] // 2, 2 * share)
    columns = jnp.concatenate([near[:, at].astype(f32), far[:, at].astype(f32)], axis=0)
    low, high = columns[:, :share], columns[:, share:]
    mine = jnp.where(core == 0, low, high).astype(bf16)
    other = jnp.where(core == 0, high, low).astype(bf16)
    sums = jnp.dot(mine, own[...], preferred_element_type=f32) + jnp.dot(
        other, mate[...], preferred_element_type=f32
    )
    half = near.shape[0]
    total[...] = sums
    message[:half, :] = sums[half:].astype(bf16)
    message[half:, :] = sums[:half].astype(bf16)


def turn(x, groups, bit):
    rows = x.shape[0] // (2 * groups)
    at = [h * groups + (k ^ bit) for h in range(2) for k in range(groups)]
    return jnp.concatenate([x[i * rows : (i + 1) * rows] for i in at], axis=0)


def merge_body(groups, total, got, out, *messages):
    sums = total[...] + got[...].astype(f32)
    out[...] = sums
    for k in range(1, groups):
        messages[k - 1][...] = turn(sums, groups, k).astype(bf16)


def up_body(groups, place, total, bias, own, mate, part, *refs):
    got, outs = refs[: groups - 1], refs[groups - 1 :]
    sums = total[...]
    for g in got:
        sums = sums + g[...].astype(f32)
    hidden = jnp.maximum(sums + bias[...], 0.0).astype(bf16)
    core = place[0] % 2
    mine = jnp.dot(hidden, own[...], preferred_element_type=f32)
    other = jnp.dot(hidden, mate[...], preferred_element_type=f32)
    both = jnp.concatenate([jnp.where(core == 0, mine, other), jnp.where(core == 0, other, mine)], axis=1)
    at = window(place[0] // 2, both.shape[1])
    rows = outs[0].shape[0]
    for q in range(2 * groups):
        some = slice(q * rows, (q + 1) * rows)
        outs[q][...] = part[some, :].astype(outs[q].dtype)
        outs[q][:, at] = (part[some, at] + both[some]).astype(outs[q].dtype)


def last_body(groups, *refs):
    sums, out = refs[:groups], refs[groups]
    total = sums[0][...]
    for k in range(1, groups):
        total = total + sums[k][...].astype(f32)
    out[...] = total.astype(bf16)


def act_body(step, near, far, w_own, w_mate, b_own, b_mate, mask, out):
    total = jnp.zeros(out.shape, f32)
    for i in range(near.shape[1] // step):
        at = slice(i * step, (i + 1) * step)
        rows = jnp.concatenate([near[:, at], far[:, at]], axis=0)
        both = jnp.concatenate([w_own[at, :], w_mate[at, :]], axis=1)
        total = total + jnp.dot(rows, both, preferred_element_type=f32)
    bias = jnp.concatenate([b_own[...], b_mate[...]], axis=1)
    out[...] = (jnp.maximum(total + bias, 0.0) * mask[...]).astype(bf16)


def part_body(step, act, w_own, w_mate, out):
    for i in range(out.shape[1] // step):
        at = slice(i * step, (i + 1) * step)
        both = jnp.concatenate([w_own[:, at], w_mate[:, at]], axis=0)
        out[:, at] = jnp.dot(act[...], both, preferred_element_type=f32)


def activity(lists, counts, block_slot):
    groups, top = lists.shape
    nblocks = block_slot.shape[0]
    names = jnp.arange(nblocks, dtype=jnp.int32)
    live = (jnp.arange(top, dtype=jnp.int32)[None, :] < counts[:, None]).astype(jnp.int32)
    hits = (lists[:, :, None] == names[None, None, :]).astype(jnp.int32) * live[:, :, None]
    by_block = jnp.sum(hits, axis=1)
    placed = (block_slot[:, None] == names[None, :]).astype(jnp.int32)
    return jnp.sum(by_block[:, :, None] * placed[None, :, :], axis=1)


def shards(
    hidden,
    ln_gain,
    ln_shift,
    lists,
    counts,
    block_slot,
    w_in,
    b_in,
    w_out,
    low_in,
    low_bias,
    low_out,
):
    devices = lax.axis_size("blk")
    position = lax.axis_index("blk")
    row_dev, width = hidden.shape
    groups = lists.shape[0]
    share, rank = low_in.shape
    block = w_in.shape[1]
    assert devices == 4 * groups
    plane = position // 4
    place = jnp.reshape(position, (1,)).astype(jnp.int32)
    some, rows = groups * row_dev, 2 * groups * row_dev

    def across(x, k):
        return lax.ppermute(x, "blk", [(i, i ^ (4 * k)) for i in range(devices)])

    def beside(x):
        return lax.ppermute(x, "blk", [(i, i ^ 2) for i in range(devices)])

    def core(x):
        return lax.ppermute(x, "blk", [(i, i ^ 1) for i in range(devices)])

    def shape(*dims, dtype=bf16):
        return jax.ShapeDtypeStruct(dims, dtype)

    gain, shift, bias = ln_gain.reshape(1, width), ln_shift.reshape(1, width), b_in.reshape(1, block)
    span = 2 * share

    held = [hidden] + [across(hidden, k) for k in range(1, groups)]
    w_in_mate = core(w_in)
    held[1], lists, counts, block_slot, w_in_mate = lax.optimization_barrier(
        (held[1], lists, counts, block_slot, w_in_mate)
    )

    table = activity(lists, counts, block_slot)
    by = plane ^ jnp.arange(groups)
    at = position ^ jnp.arange(2)
    relate = (by[:, None] == jnp.arange(groups)[None, :])[:, None, :, None]
    choose = (at[:, None] == jnp.arange(devices)[None, :])[None, :, None, :]
    live = jnp.sum(jnp.where(relate & choose, table[None, None], 0), axis=(2, 3)).astype(f32)
    mask = jnp.broadcast_to(live[None, :, None, :, None], (2, groups, row_dev, 2, block)).reshape(rows, 2 * block)

    low_in_sent, mask = lax.optimization_barrier((low_in, mask))
    low_in_mate = core(low_in_sent)
    early, bias_mate = lax.optimization_barrier((hidden, core(bias)))
    beyond = [beside(h) for h in [early] + held[1:]]
    near = (hidden, gain, shift, low_in, w_in, w_out, low_out)
    *near, mask, beyond[0] = lax.optimization_barrier((*near, mask, beyond[0]))
    near = call(
        functools.partial(load_body, len(near)),
        [shape(*x.shape, dtype=x.dtype) for x in near],
        [HBM] * len(near),
        16,
        [pltpu.SemaphoreType.DMA((len(near),))],
        8 * MIB,
    )(*[pltpu.with_memory_space_constraint(x, pltpu.HBM) for x in near])
    hidden_near, gain, shift, low_in, w_in, w_out_near, low_out_near = near
    *_, w_in_mate, w_out_sent, low_out_sent = lax.optimization_barrier(
        (*held, *beyond[: groups // 2], w_in_mate, w_out, low_out)
    )
    w_out_mate, low_out_mate = core(w_out_sent), core(low_out_sent)
    held[0] = hidden_near

    soon = groups // 2
    normed, first = call(
        functools.partial(early_body, groups, soon),
        [shape(some, width), shape(soon * row_dev, width)],
        [VMEM] * (groups + soon + 2),
        16,
        (),
        4 * MIB,
    )(*held, *beyond[:soon], gain, shift)
    far, total, message = call(
        functools.partial(norm_body, groups - soon),
        [shape(some, width), shape(rows, rank, dtype=f32), shape(rows, rank)],
        [SMEM] + [VMEM] * (groups - soon + 6),
        16,
        (),
        4 * MIB,
    )(place, *beyond[soon:], normed, first, gain, shift, low_in, low_in_mate)
    got = beside(message)
    step = piece(width, 2048)
    act = call(
        functools.partial(act_body, step),
        [shape(rows, 2 * block)],
        [VMEM] * 7,
        16,
        (),
        4 * MIB,
    )(normed, far, w_in, w_in_mate, bias, bias_mate, mask)[0]
    total, *messages = call(
        functools.partial(merge_body, groups),
        [shape(rows, rank, dtype=f32)] + [shape(rows, rank)] * (groups - 1),
        [VMEM] * 2,
        16,
    )(total, got)
    got = [across(messages[k - 1], k) for k in range(groups - 1, 0, -1)]
    part = call(
        functools.partial(part_body, step),
        [shape(rows, width, dtype=f32)],
        [VMEM] * 3,
        16,
        (),
        6 * MIB,
    )(act, w_out_near, w_out_mate)[0]
    parts = call(
        functools.partial(up_body, groups),
        [shape(row_dev, width, dtype=f32)] * groups + [shape(row_dev, width)] * groups,
        [SMEM] + [VMEM] * (groups + 4),
        16,
        (),
        6 * MIB,
    )(place, total, low_bias.reshape(1, rank), low_out_near, low_out_mate, part, *got)

    sums = []
    for k in range(groups - 1, -1, -1):
        here = parts[k] + beside(parts[groups + k]).astype(f32)
        sums.append(across(here.astype(bf16), k) if k else here)
    return call(functools.partial(last_body, groups), [shape(row_dev, width)], [VMEM] * groups, 16)(*sums[::-1])[0]


def solution(mesh):
    return jax.shard_map(
        shards,
        mesh=mesh,
        in_specs=(
            P(("rep", "blk"), None),
            P(),
            P(),
            P("rep", None),
            P("rep"),
            P(),
            P(None, "blk"),
            P("blk"),
            P("blk", None),
            P("blk", None),
            P(),
            P(None, "blk"),
        ),
        out_specs=P(("rep", "blk"), None),
        check_vma=False,
    )
```

```python
import functools

import jax
import jax.numpy as jnp
from jax import lax
from jax.experimental import pallas as pl
from jax.experimental.pallas import tpu as pltpu
from jax.sharding import PartitionSpec as P

MIB = 1 << 20
VMEM = pl.BlockSpec(memory_space=pltpu.VMEM)
HBM = pl.BlockSpec(memory_space=pltpu.HBM)
SMEM = pl.BlockSpec(memory_space=pltpu.SMEM)
f32, bf16 = jnp.float32, jnp.bfloat16


def piece(width, most):
    size = 128
    while size * 2 <= most and width % (size * 2) == 0:
        size *= 2
    return size


def window(index, size):
    return pl.ds(pl.multiple_of(index * size, 128), size)


def call(body, outs, ins, limit, scratch=(), moved=2 * MIB):
    return pl.pallas_call(
        body,
        out_shape=outs,
        in_specs=ins,
        out_specs=[VMEM] * len(outs),
        scratch_shapes=list(scratch),
        compiler_params=pltpu.CompilerParams(vmem_limit_bytes=limit * MIB),
        cost_estimate=pl.CostEstimate(flops=0, bytes_accessed=moved, transcendentals=0),
    )


def normal(hidden, gain, shift):
    wide = hidden.astype(f32)
    mean = jnp.mean(wide, axis=-1, keepdims=True)
    centred = wide - mean
    variance = jnp.mean(centred * centred, axis=-1, keepdims=True)
    return (centred * lax.rsqrt(variance + 1e-05) * gain + shift).astype(bf16)


def load_body(count, *refs):
    srcs, dsts, sems = refs[:count], refs[count : 2 * count], refs[2 * count]
    copies = [pltpu.make_async_copy(srcs[i], dsts[i], sems.at[i]) for i in range(count)]
    for copy in copies:
        copy.start()
    for copy in copies:
        copy.wait()


def early_body(groups, soon, *refs):
    held, (gain, shift, near, far) = refs[: groups + soon], refs[groups + soon :]
    rows = held[0].shape[0]
    for out, some in ((near, held[:groups]), (far, held[groups:])):
        for i in range(0, len(some), 2):
            pair = jnp.concatenate([h[...] for h in some[i : i + 2]], axis=0)
            out[i * rows : i * rows + pair.shape[0], :] = normal(pair, gain[...], shift[...])


def norm_body(count, place, *refs):
    held, (near, first, gain, shift, own, mate, far, total, *messages) = refs[:count], refs[count:]
    rows, done = held[0].shape[0], first.shape[0]
    far[:done, :] = first[...]
    for i in range(0, count, 2):
        pair = jnp.concatenate([h[...] for h in held[i : i + 2]], axis=0)
        far[done + i * rows : done + i * rows + pair.shape[0], :] = normal(pair, gain[...], shift[...])
    share = own.shape[0]
    core = place[0] % 2
    at = window(place[0] // 2, 2 * share)
    columns = jnp.concatenate([near[:, at].astype(f32), far[:, at].astype(f32)], axis=0)
    low, high = columns[:, :share], columns[:, share:]
    mine = jnp.where(core == 0, low, high).astype(bf16)
    other = jnp.where(core == 0, high, low).astype(bf16)
    sums = jnp.dot(mine, own[...], preferred_element_type=f32) + jnp.dot(
        other, mate[...], preferred_element_type=f32
    )
    total[...] = sums
    for k, message in enumerate(messages, 1):
        message[...] = turn(sums, len(messages) + 1, k).astype(bf16)


def turn(x, groups, bit):
    rows = x.shape[0] // (2 * groups)
    at = [h * groups + (k ^ bit) for h in range(2) for k in range(groups)]
    return jnp.concatenate([x[i * rows : (i + 1) * rows] for i in at], axis=0)


def merge_body(groups, total, *refs):
    got, (out, message) = refs[: groups - 1], refs[groups - 1 :]
    sums = total[...]
    for g in got:
        sums = sums + g[...].astype(f32)
    out[...] = sums
    half = sums.shape[0] // 2
    message[:half, :] = sums[half:].astype(bf16)
    message[half:, :] = sums[:half].astype(bf16)


def up_body(groups, place, total, bias, own, mate, part, got, *outs):
    sums = total[...] + got[...].astype(f32)
    hidden = jnp.maximum(sums + bias[...], 0.0).astype(bf16)
    core = place[0] % 2
    mine = jnp.dot(hidden, own[...], preferred_element_type=f32)
    other = jnp.dot(hidden, mate[...], preferred_element_type=f32)
    both = jnp.concatenate([jnp.where(core == 0, mine, other), jnp.where(core == 0, other, mine)], axis=1)
    at = window(place[0] // 2, both.shape[1])
    rows = outs[0].shape[0]
    for q in range(2 * groups):
        some = slice(q * rows, (q + 1) * rows)
        outs[q][...] = part[some, :].astype(outs[q].dtype)
        outs[q][:, at] = (part[some, at] + both[some]).astype(outs[q].dtype)


def last_body(groups, *refs):
    sums, out = refs[:groups], refs[groups]
    total = sums[0][...]
    for k in range(1, groups):
        total = total + sums[k][...].astype(f32)
    out[...] = total.astype(bf16)


def act_body(step, near, far, w_own, w_mate, b_own, b_mate, mask, out):
    total = jnp.zeros(out.shape, f32)
    for i in range(near.shape[1] // step):
        at = slice(i * step, (i + 1) * step)
        rows = jnp.concatenate([near[:, at], far[:, at]], axis=0)
        both = jnp.concatenate([w_own[at, :], w_mate[at, :]], axis=1)
        total = total + jnp.dot(rows, both, preferred_element_type=f32)
    bias = jnp.concatenate([b_own[...], b_mate[...]], axis=1)
    out[...] = (jnp.maximum(total + bias, 0.0) * mask[...]).astype(bf16)


def part_body(step, act, w_own, w_mate, out):
    for i in range(out.shape[1] // step):
        at = slice(i * step, (i + 1) * step)
        both = jnp.concatenate([w_own[:, at], w_mate[:, at]], axis=0)
        out[:, at] = jnp.dot(act[...], both, preferred_element_type=f32)


def activity(lists, counts, block_slot):
    groups, top = lists.shape
    nblocks = block_slot.shape[0]
    names = jnp.arange(nblocks, dtype=jnp.int32)
    live = (jnp.arange(top, dtype=jnp.int32)[None, :] < counts[:, None]).astype(jnp.int32)
    hits = (lists[:, :, None] == names[None, None, :]).astype(jnp.int32) * live[:, :, None]
    by_block = jnp.sum(hits, axis=1)
    placed = (block_slot[:, None] == names[None, :]).astype(jnp.int32)
    return jnp.sum(by_block[:, :, None] * placed[None, :, :], axis=1)


def shards(
    hidden,
    ln_gain,
    ln_shift,
    lists,
    counts,
    block_slot,
    w_in,
    b_in,
    w_out,
    low_in,
    low_bias,
    low_out,
):
    devices = lax.axis_size("blk")
    position = lax.axis_index("blk")
    row_dev, width = hidden.shape
    groups = lists.shape[0]
    share, rank = low_in.shape
    block = w_in.shape[1]
    assert devices == 4 * groups
    plane = position // 4
    place = jnp.reshape(position, (1,)).astype(jnp.int32)
    some, rows = groups * row_dev, 2 * groups * row_dev

    def across(x, k):
        return lax.ppermute(x, "blk", [(i, i ^ (4 * k)) for i in range(devices)])

    def beside(x):
        return lax.ppermute(x, "blk", [(i, i ^ 2) for i in range(devices)])

    def core(x):
        return lax.ppermute(x, "blk", [(i, i ^ 1) for i in range(devices)])

    def shape(*dims, dtype=bf16):
        return jax.ShapeDtypeStruct(dims, dtype)

    gain, shift, bias = ln_gain.reshape(1, width), ln_shift.reshape(1, width), b_in.reshape(1, block)
    span = 2 * share

    held = [hidden] + [across(hidden, k) for k in range(1, groups)]
    w_in_mate = core(w_in)
    held[1], lists, counts, block_slot = lax.optimization_barrier((held[1], lists, counts, block_slot))

    table = activity(lists, counts, block_slot)
    by = plane ^ jnp.arange(groups)
    at = position ^ jnp.arange(2)
    relate = (by[:, None] == jnp.arange(groups)[None, :])[:, None, :, None]
    choose = (at[:, None] == jnp.arange(devices)[None, :])[None, :, None, :]
    live = jnp.sum(jnp.where(relate & choose, table[None, None], 0), axis=(2, 3)).astype(f32)
    mask = jnp.broadcast_to(live[None, :, None, :, None], (2, groups, row_dev, 2, block)).reshape(rows, 2 * block)

    low_in_sent, mask = lax.optimization_barrier((low_in, mask))
    low_in_mate = core(low_in_sent)
    early, bias_mate = lax.optimization_barrier((hidden, core(bias)))
    beyond = [beside(h) for h in [early] + held[1:]]
    near = (hidden, gain, shift, low_in, w_in, w_out, low_out)
    *near, mask, beyond[0] = lax.optimization_barrier((*near, mask, beyond[0]))
    near = call(
        functools.partial(load_body, len(near)),
        [shape(*x.shape, dtype=x.dtype) for x in near],
        [HBM] * len(near),
        16,
        [pltpu.SemaphoreType.DMA((len(near),))],
        8 * MIB,
    )(*[pltpu.with_memory_space_constraint(x, pltpu.HBM) for x in near])
    hidden_near, gain, shift, low_in, w_in, w_out_near, low_out_near = near
    *_, w_in_mate, w_out_sent, low_out_sent = lax.optimization_barrier(
        (*held, *beyond[: groups // 2], w_in_mate, w_out, low_out)
    )
    w_out_mate, low_out_mate = core(w_out_sent), core(low_out_sent)
    held[0] = hidden_near

    soon = groups // 2
    normed, first = call(
        functools.partial(early_body, groups, soon),
        [shape(some, width), shape(soon * row_dev, width)],
        [VMEM] * (groups + soon + 2),
        16,
        (),
        4 * MIB,
    )(*held, *beyond[:soon], gain, shift)
    far, total, *messages = call(
        functools.partial(norm_body, groups - soon),
        [shape(some, width), shape(rows, rank, dtype=f32)] + [shape(rows, rank)] * (groups - 1),
        [SMEM] + [VMEM] * (groups - soon + 6),
        16,
        (),
        4 * MIB,
    )(place, *beyond[soon:], normed, first, gain, shift, low_in, low_in_mate)
    got = [across(messages[k - 1], k) for k in (1, *range(groups - 1, 1, -1))]
    step = piece(width, 2048)
    act = call(
        functools.partial(act_body, step),
        [shape(rows, 2 * block)],
        [VMEM] * 7,
        16,
        (),
        4 * MIB,
    )(normed, far, w_in, w_in_mate, bias, bias_mate, mask)[0]
    total, message = call(
        functools.partial(merge_body, groups),
        [shape(rows, rank, dtype=f32), shape(rows, rank)],
        [VMEM] * groups,
        16,
    )(total, *got)
    got = beside(message)
    part = call(
        functools.partial(part_body, step),
        [shape(rows, width, dtype=f32)],
        [VMEM] * 3,
        16,
        (),
        6 * MIB,
    )(act, w_out_near, w_out_mate)[0]
    parts = call(
        functools.partial(up_body, groups),
        [shape(row_dev, width, dtype=f32)] * groups + [shape(row_dev, width)] * groups,
        [SMEM] + [VMEM] * 6,
        16,
        (),
        6 * MIB,
    )(place, total, low_bias.reshape(1, rank), low_out_near, low_out_mate, part, got)

    sums = []
    for k in range(groups - 1, -1, -1):
        here = parts[k] + beside(parts[groups + k]).astype(f32)
        sums.append(across(here.astype(bf16), k) if k else here)
    return call(functools.partial(last_body, groups), [shape(row_dev, width)], [VMEM] * groups, 16)(*sums[::-1])[0]


def solution(mesh):
    return jax.shard_map(
        shards,
        mesh=mesh,
        in_specs=(
            P(("rep", "blk"), None),
            P(),
            P(),
            P("rep", None),
            P("rep"),
            P(),
            P(None, "blk"),
            P("blk"),
            P("blk", None),
            P("blk", None),
            P(),
            P(None, "blk"),
        ),
        out_specs=P(("rep", "blk"), None),
        check_vma=False,
    )
```

```python
import functools

import jax
import jax.numpy as jnp
from jax import lax
from jax.experimental import pallas as pl
from jax.experimental.pallas import tpu as pltpu
from jax.sharding import PartitionSpec as P

MIB = 1 << 20
VMEM = pl.BlockSpec(memory_space=pltpu.VMEM)
HBM = pl.BlockSpec(memory_space=pltpu.HBM)
SMEM = pl.BlockSpec(memory_space=pltpu.SMEM)
f32, bf16 = jnp.float32, jnp.bfloat16


def piece(width, most):
    size = 128
    while size * 2 <= most and width % (size * 2) == 0:
        size *= 2
    return size


def window(index, size):
    return pl.ds(pl.multiple_of(index * size, 128), size)


def call(body, outs, ins, limit, scratch=(), moved=2 * MIB):
    return pl.pallas_call(
        body,
        out_shape=outs,
        in_specs=ins,
        out_specs=[VMEM] * len(outs),
        scratch_shapes=list(scratch),
        compiler_params=pltpu.CompilerParams(vmem_limit_bytes=limit * MIB),
        cost_estimate=pl.CostEstimate(flops=0, bytes_accessed=moved, transcendentals=0),
    )


def normal(hidden, gain, shift):
    wide = hidden.astype(f32)
    mean = jnp.mean(wide, axis=-1, keepdims=True)
    centred = wide - mean
    variance = jnp.mean(centred * centred, axis=-1, keepdims=True)
    return (centred * lax.rsqrt(variance + 1e-05) * gain + shift).astype(bf16)


def load_body(count, *refs):
    srcs, dsts, sems = refs[:count], refs[count : 2 * count], refs[2 * count]
    copies = [pltpu.make_async_copy(srcs[i], dsts[i], sems.at[i]) for i in range(count)]
    for copy in copies:
        copy.start()
    for copy in copies:
        copy.wait()


def early_body(groups, soon, *refs):
    held, (gain, shift, near, far) = refs[: groups + soon], refs[groups + soon :]
    rows = held[0].shape[0]
    for out, some in ((near, held[:groups]), (far, held[groups:])):
        for i in range(0, len(some), 2):
            pair = jnp.concatenate([h[...] for h in some[i : i + 2]], axis=0)
            out[i * rows : i * rows + pair.shape[0], :] = normal(pair, gain[...], shift[...])


def norm_body(count, place, *refs):
    held, (near, first, gain, shift, own, mate, far, total, message) = refs[:count], refs[count:]
    rows, done = held[0].shape[0], first.shape[0]
    far[:done, :] = first[...]
    for i in range(0, count, 2):
        pair = jnp.concatenate([h[...] for h in held[i : i + 2]], axis=0)
        far[done + i * rows : done + i * rows + pair.shape[0], :] = normal(pair, gain[...], shift[...])
    share = own.shape[0]
    core = place[0] % 2
    at = window(place[0] // 2, 2 * share)
    columns = jnp.concatenate([near[:, at].astype(f32), far[:, at].astype(f32)], axis=0)
    low, high = columns[:, :share], columns[:, share:]
    mine = jnp.where(core == 0, low, high).astype(bf16)
    other = jnp.where(core == 0, high, low).astype(bf16)
    sums = jnp.dot(mine, own[...], preferred_element_type=f32) + jnp.dot(
        other, mate[...], preferred_element_type=f32
    )
    half = near.shape[0]
    total[...] = sums
    message[:half, :] = sums[half:]
    message[half:, :] = sums[:half]


def turn(x, groups, bit):
    rows = x.shape[0] // (2 * groups)
    at = [h * groups + (k ^ bit) for h in range(2) for k in range(groups)]
    return jnp.concatenate([x[i * rows : (i + 1) * rows] for i in at], axis=0)


def merge_body(groups, total, got, out, *messages):
    sums = total[...] + got[...]
    out[...] = sums
    for k in range(1, groups):
        messages[k - 1][...] = turn(sums, groups, k)


def up_body(groups, place, total, bias, own, mate, part, *refs):
    got, outs = refs[: groups - 1], refs[groups - 1 :]
    sums = total[...]
    for g in got:
        sums = sums + g[...]
    hidden = jnp.maximum(sums + bias[...], 0.0).astype(bf16)
    core = place[0] % 2
    mine = jnp.dot(hidden, own[...], preferred_element_type=f32)
    other = jnp.dot(hidden, mate[...], preferred_element_type=f32)
    both = jnp.concatenate([jnp.where(core == 0, mine, other), jnp.where(core == 0, other, mine)], axis=1)
    at = window(place[0] // 2, both.shape[1])
    rows = outs[0].shape[0]
    for q in range(2 * groups):
        some = slice(q * rows, (q + 1) * rows)
        outs[q][...] = part[some, :].astype(outs[q].dtype)
        outs[q][:, at] = (part[some, at] + both[some]).astype(outs[q].dtype)


def last_body(groups, *refs):
    sums, out = refs[:groups], refs[groups]
    total = sums[0][...]
    for k in range(1, groups):
        total = total + sums[k][...].astype(f32)
    out[...] = total.astype(bf16)


def act_body(step, near, far, w_own, w_mate, b_own, b_mate, mask, out):
    total = jnp.zeros(out.shape, f32)
    for i in range(near.shape[1] // step):
        at = slice(i * step, (i + 1) * step)
        rows = jnp.concatenate([near[:, at], far[:, at]], axis=0)
        both = jnp.concatenate([w_own[at, :], w_mate[at, :]], axis=1)
        total = total + jnp.dot(rows, both, preferred_element_type=f32)
    bias = jnp.concatenate([b_own[...], b_mate[...]], axis=1)
    out[...] = (jnp.maximum(total + bias, 0.0) * mask[...]).astype(bf16)


def part_body(step, act, w_own, w_mate, out):
    for i in range(out.shape[1] // step):
        at = slice(i * step, (i + 1) * step)
        both = jnp.concatenate([w_own[:, at], w_mate[:, at]], axis=0)
        out[:, at] = jnp.dot(act[...], both, preferred_element_type=f32)


def activity(lists, counts, block_slot):
    groups, top = lists.shape
    nblocks = block_slot.shape[0]
    names = jnp.arange(nblocks, dtype=jnp.int32)
    live = (jnp.arange(top, dtype=jnp.int32)[None, :] < counts[:, None]).astype(jnp.int32)
    hits = (lists[:, :, None] == names[None, None, :]).astype(jnp.int32) * live[:, :, None]
    by_block = jnp.sum(hits, axis=1)
    placed = (block_slot[:, None] == names[None, :]).astype(jnp.int32)
    return jnp.sum(by_block[:, :, None] * placed[None, :, :], axis=1)


def shards(
    hidden,
    ln_gain,
    ln_shift,
    lists,
    counts,
    block_slot,
    w_in,
    b_in,
    w_out,
    low_in,
    low_bias,
    low_out,
):
    devices = lax.axis_size("blk")
    position = lax.axis_index("blk")
    row_dev, width = hidden.shape
    groups = lists.shape[0]
    share, rank = low_in.shape
    block = w_in.shape[1]
    assert devices == 4 * groups
    plane = position // 4
    place = jnp.reshape(position, (1,)).astype(jnp.int32)
    some, rows = groups * row_dev, 2 * groups * row_dev

    def across(x, k):
        return lax.ppermute(x, "blk", [(i, i ^ (4 * k)) for i in range(devices)])

    def beside(x):
        return lax.ppermute(x, "blk", [(i, i ^ 2) for i in range(devices)])

    def core(x):
        return lax.ppermute(x, "blk", [(i, i ^ 1) for i in range(devices)])

    def shape(*dims, dtype=bf16):
        return jax.ShapeDtypeStruct(dims, dtype)

    gain, shift, bias = ln_gain.reshape(1, width), ln_shift.reshape(1, width), b_in.reshape(1, block)
    span = 2 * share

    held = [hidden] + [across(hidden, k) for k in range(1, groups)]
    w_in_mate = core(w_in)
    held[1], lists, counts, block_slot = lax.optimization_barrier((held[1], lists, counts, block_slot))

    table = activity(lists, counts, block_slot)
    by = plane ^ jnp.arange(groups)
    at = position ^ jnp.arange(2)
    relate = (by[:, None] == jnp.arange(groups)[None, :])[:, None, :, None]
    choose = (at[:, None] == jnp.arange(devices)[None, :])[None, :, None, :]
    live = jnp.sum(jnp.where(relate & choose, table[None, None], 0), axis=(2, 3)).astype(f32)
    mask = jnp.broadcast_to(live[None, :, None, :, None], (2, groups, row_dev, 2, block)).reshape(rows, 2 * block)

    low_in_sent, mask = lax.optimization_barrier((low_in, mask))
    low_in_mate = core(low_in_sent)
    early, bias_mate = lax.optimization_barrier((hidden, core(bias)))
    beyond = [beside(h) for h in [early] + held[1:]]
    near = (hidden, gain, shift, low_in, w_in, w_out, low_out)
    *near, mask, beyond[0] = lax.optimization_barrier((*near, mask, beyond[0]))
    near = call(
        functools.partial(load_body, len(near)),
        [shape(*x.shape, dtype=x.dtype) for x in near],
        [HBM] * len(near),
        16,
        [pltpu.SemaphoreType.DMA((len(near),))],
        8 * MIB,
    )(*[pltpu.with_memory_space_constraint(x, pltpu.HBM) for x in near])
    hidden_near, gain, shift, low_in, w_in, w_out_near, low_out_near = near
    *_, w_in_mate, w_out_sent, low_out_sent = lax.optimization_barrier(
        (*held, *beyond[: groups // 2], w_in_mate, w_out, low_out)
    )
    w_out_mate, low_out_mate = core(w_out_sent), core(low_out_sent)
    held[0] = hidden_near

    soon = groups // 2
    normed, first = call(
        functools.partial(early_body, groups, soon),
        [shape(some, width), shape(soon * row_dev, width)],
        [VMEM] * (groups + soon + 2),
        16,
        (),
        4 * MIB,
    )(*held, *beyond[:soon], gain, shift)
    far, total, message = call(
        functools.partial(norm_body, groups - soon),
        [shape(some, width), shape(rows, rank, dtype=f32), shape(rows, rank, dtype=f32)],
        [SMEM] + [VMEM] * (groups - soon + 6),
        16,
        (),
        4 * MIB,
    )(place, *beyond[soon:], normed, first, gain, shift, low_in, low_in_mate)
    got = beside(message)
    step = piece(width, 2048)
    act = call(
        functools.partial(act_body, step),
        [shape(rows, 2 * block)],
        [VMEM] * 7,
        16,
        (),
        4 * MIB,
    )(normed, far, w_in, w_in_mate, bias, bias_mate, mask)[0]
    total, *messages = call(
        functools.partial(merge_body, groups),
        [shape(rows, rank, dtype=f32)] * groups,
        [VMEM] * 2,
        16,
    )(total, got)
    got = [across(messages[k - 1], k) for k in range(groups - 1, 0, -1)]
    part = call(
        functools.partial(part_body, step),
        [shape(rows, width, dtype=f32)],
        [VMEM] * 3,
        16,
        (),
        6 * MIB,
    )(act, w_out_near, w_out_mate)[0]
    parts = call(
        functools.partial(up_body, groups),
        [shape(row_dev, width, dtype=f32)] * groups + [shape(row_dev, width)] * groups,
        [SMEM] + [VMEM] * (groups + 4),
        16,
        (),
        6 * MIB,
    )(place, total, low_bias.reshape(1, rank), low_out_near, low_out_mate, part, *got)

    sums = []
    for k in range(groups - 1, -1, -1):
        here = parts[k] + beside(parts[groups + k]).astype(f32)
        sums.append(across(here.astype(bf16), k) if k else here)
    return call(functools.partial(last_body, groups), [shape(row_dev, width)], [VMEM] * groups, 16)(*sums[::-1])[0]


def solution(mesh):
    return jax.shard_map(
        shards,
        mesh=mesh,
        in_specs=(
            P(("rep", "blk"), None),
            P(),
            P(),
            P("rep", None),
            P("rep"),
            P(),
            P(None, "blk"),
            P("blk"),
            P("blk", None),
            P("blk", None),
            P(),
            P(None, "blk"),
        ),
        out_specs=P(("rep", "blk"), None),
        check_vma=False,
    )
```

```python
import functools

import jax
import jax.numpy as jnp
from jax import lax
from jax.experimental import pallas as pl
from jax.experimental.pallas import tpu as pltpu
from jax.sharding import PartitionSpec as P

MIB = 1 << 20
VMEM = pl.BlockSpec(memory_space=pltpu.VMEM)
HBM = pl.BlockSpec(memory_space=pltpu.HBM)
SMEM = pl.BlockSpec(memory_space=pltpu.SMEM)
f32, bf16 = jnp.float32, jnp.bfloat16


def piece(width, most):
    size = 128
    while size * 2 <= most and width % (size * 2) == 0:
        size *= 2
    return size


def window(index, size):
    return pl.ds(pl.multiple_of(index * size, 128), size)


def call(body, outs, ins, limit, scratch=(), moved=2 * MIB):
    return pl.pallas_call(
        body,
        out_shape=outs,
        in_specs=ins,
        out_specs=[VMEM] * len(outs),
        scratch_shapes=list(scratch),
        compiler_params=pltpu.CompilerParams(vmem_limit_bytes=limit * MIB),
        cost_estimate=pl.CostEstimate(flops=0, bytes_accessed=moved, transcendentals=0),
    )


def normal(hidden, gain, shift):
    wide = hidden.astype(f32)
    mean = jnp.mean(wide, axis=-1, keepdims=True)
    centred = wide - mean
    variance = jnp.mean(centred * centred, axis=-1, keepdims=True)
    return (centred * lax.rsqrt(variance + 1e-05) * gain + shift).astype(bf16)


def load_body(count, *refs):
    srcs, dsts, sems = refs[:count], refs[count : 2 * count], refs[2 * count]
    copies = [pltpu.make_async_copy(srcs[i], dsts[i], sems.at[i]) for i in range(count)]
    for copy in copies:
        copy.start()
    for copy in copies:
        copy.wait()


def early_body(groups, soon, *refs):
    held, (gain, shift, near, far) = refs[: groups + soon], refs[groups + soon :]
    rows = held[0].shape[0]
    for out, some in ((near, held[:groups]), (far, held[groups:])):
        for i in range(0, len(some), 2):
            pair = jnp.concatenate([h[...] for h in some[i : i + 2]], axis=0)
            out[i * rows : i * rows + pair.shape[0], :] = normal(pair, gain[...], shift[...])


def norm_body(count, place, *refs):
    held, (near, first, gain, shift, own, mate, far, total, message) = refs[:count], refs[count:]
    rows, done = held[0].shape[0], first.shape[0]
    far[:done, :] = first[...]
    for i in range(0, count, 2):
        pair = jnp.concatenate([h[...] for h in held[i : i + 2]], axis=0)
        far[done + i * rows : done + i * rows + pair.shape[0], :] = normal(pair, gain[...], shift[...])
    share = own.shape[0]
    core = place[0] % 2
    at = window(place[0] // 2, 2 * share)
    columns = jnp.concatenate([near[:, at].astype(f32), far[:, at].astype(f32)], axis=0)
    low, high = columns[:, :share], columns[:, share:]
    mine = jnp.where(core == 0, low, high).astype(bf16)
    other = jnp.where(core == 0, high, low).astype(bf16)
    sums = jnp.dot(mine, own[...], preferred_element_type=f32) + jnp.dot(
        other, mate[...], preferred_element_type=f32
    )
    half = near.shape[0]
    total[...] = sums
    message[:half, :] = sums[half:]
    message[half:, :] = sums[:half]


def turn(x, groups, bit):
    rows = x.shape[0] // (2 * groups)
    at = [h * groups + (k ^ bit) for h in range(2) for k in range(groups)]
    return jnp.concatenate([x[i * rows : (i + 1) * rows] for i in at], axis=0)


def merge_body(groups, total, got, out, *messages):
    sums = total[...] + got[...]
    out[...] = sums
    for k in range(1, groups):
        messages[k - 1][...] = turn(sums, groups, k)


def up_body(groups, place, total, bias, own, mate, part, *refs):
    got, outs = refs[: groups - 1], refs[groups - 1 :]
    sums = total[...]
    for g in got:
        sums = sums + g[...]
    hidden = jnp.maximum(sums + bias[...], 0.0).astype(bf16)
    core = place[0] % 2
    mine = jnp.dot(hidden, own[...], preferred_element_type=f32)
    other = jnp.dot(hidden, mate[...], preferred_element_type=f32)
    both = jnp.concatenate([jnp.where(core == 0, mine, other), jnp.where(core == 0, other, mine)], axis=1)
    at = window(place[0] // 2, both.shape[1])
    rows = outs[0].shape[0]
    for q in range(2 * groups):
        some = slice(q * rows, (q + 1) * rows)
        outs[q][...] = part[some, :].astype(outs[q].dtype)
        outs[q][:, at] = (part[some, at] + both[some]).astype(outs[q].dtype)


def last_body(groups, *refs):
    sums, out = refs[:groups], refs[groups]
    total = sums[0][...]
    for k in range(1, groups):
        total = total + sums[k][...].astype(f32)
    out[...] = total.astype(bf16)


def act_body(step, near, far, w_own, w_mate, b_own, b_mate, mask, out):
    total = jnp.zeros(out.shape, f32)
    for i in range(near.shape[1] // step):
        at = slice(i * step, (i + 1) * step)
        rows = jnp.concatenate([near[:, at], far[:, at]], axis=0)
        both = jnp.concatenate([w_own[at, :], w_mate[at, :]], axis=1)
        total = total + jnp.dot(rows, both, preferred_element_type=f32)
    bias = jnp.concatenate([b_own[...], b_mate[...]], axis=1)
    out[...] = (jnp.maximum(total + bias, 0.0) * mask[...]).astype(bf16)


def part_body(step, act, w_own, w_mate, out):
    for i in range(out.shape[1] // step):
        at = slice(i * step, (i + 1) * step)
        both = jnp.concatenate([w_own[:, at], w_mate[:, at]], axis=0)
        out[:, at] = jnp.dot(act[...], both, preferred_element_type=f32)


def activity(lists, counts, block_slot):
    groups, top = lists.shape
    nblocks = block_slot.shape[0]
    names = jnp.arange(nblocks, dtype=jnp.int32)
    live = (jnp.arange(top, dtype=jnp.int32)[None, :] < counts[:, None]).astype(jnp.int32)
    hits = (lists[:, :, None] == names[None, None, :]).astype(jnp.int32) * live[:, :, None]
    by_block = jnp.sum(hits, axis=1)
    placed = (block_slot[:, None] == names[None, :]).astype(jnp.int32)
    return jnp.sum(by_block[:, :, None] * placed[None, :, :], axis=1)


def shards(
    hidden,
    ln_gain,
    ln_shift,
    lists,
    counts,
    block_slot,
    w_in,
    b_in,
    w_out,
    low_in,
    low_bias,
    low_out,
):
    devices = lax.axis_size("blk")
    position = lax.axis_index("blk")
    row_dev, width = hidden.shape
    groups = lists.shape[0]
    share, rank = low_in.shape
    block = w_in.shape[1]
    assert devices == 4 * groups
    plane = position // 4
    place = jnp.reshape(position, (1,)).astype(jnp.int32)
    some, rows = groups * row_dev, 2 * groups * row_dev

    def across(x, k):
        return lax.ppermute(x, "blk", [(i, i ^ (4 * k)) for i in range(devices)])

    def beside(x):
        return lax.ppermute(x, "blk", [(i, i ^ 2) for i in range(devices)])

    def core(x):
        return lax.ppermute(x, "blk", [(i, i ^ 1) for i in range(devices)])

    def shape(*dims, dtype=bf16):
        return jax.ShapeDtypeStruct(dims, dtype)

    gain, shift, bias = ln_gain.reshape(1, width), ln_shift.reshape(1, width), b_in.reshape(1, block)
    span = 2 * share

    held = [hidden] + [across(hidden, k) for k in range(1, groups)]
    held[1], lists, counts, block_slot = lax.optimization_barrier((held[1], lists, counts, block_slot))

    table = activity(lists, counts, block_slot)
    by = plane ^ jnp.arange(groups)
    at = position ^ jnp.arange(2)
    relate = (by[:, None] == jnp.arange(groups)[None, :])[:, None, :, None]
    choose = (at[:, None] == jnp.arange(devices)[None, :])[None, :, None, :]
    live = jnp.sum(jnp.where(relate & choose, table[None, None], 0), axis=(2, 3)).astype(f32)
    mask = jnp.broadcast_to(live[None, :, None, :, None], (2, groups, row_dev, 2, block)).reshape(rows, 2 * block)

    low_in_sent, mask = lax.optimization_barrier((low_in, mask))
    low_in_mate = core(low_in_sent)
    early, bias_mate = lax.optimization_barrier((hidden, core(bias)))
    beyond = [beside(h) for h in [early] + held[1:]]
    near = (hidden, gain, shift, low_in, w_in, w_out, low_out)
    *near, mask, beyond[0] = lax.optimization_barrier((*near, mask, beyond[0]))
    near = call(
        functools.partial(load_body, len(near)),
        [shape(*x.shape, dtype=x.dtype) for x in near],
        [HBM] * len(near),
        16,
        [pltpu.SemaphoreType.DMA((len(near),))],
        8 * MIB,
    )(*[pltpu.with_memory_space_constraint(x, pltpu.HBM) for x in near])
    w_in_first = w_in
    hidden_near, gain, shift, low_in, w_in, w_out_near, low_out_near = near
    *_, w_in_sent, w_out_sent = lax.optimization_barrier(
        (*held, *beyond[: groups // 2], w_in_first, w_out)
    )
    w_in_mate, w_out_mate = core(w_in_sent), core(w_out_sent)
    held[0] = hidden_near

    soon = groups // 2
    normed, first = call(
        functools.partial(early_body, groups, soon),
        [shape(some, width), shape(soon * row_dev, width)],
        [VMEM] * (groups + soon + 2),
        16,
        (),
        4 * MIB,
    )(*held, *beyond[:soon], gain, shift)
    far, total, message = call(
        functools.partial(norm_body, groups - soon),
        [shape(some, width), shape(rows, rank, dtype=f32), shape(rows, rank, dtype=f32)],
        [SMEM] + [VMEM] * (groups - soon + 6),
        16,
        (),
        4 * MIB,
    )(place, *beyond[soon:], normed, first, gain, shift, low_in, low_in_mate)
    message, low_out_sent = lax.optimization_barrier((message, low_out))
    got, low_out_mate = beside(message), core(low_out_sent)
    step = piece(width, 2048)
    act = call(
        functools.partial(act_body, step),
        [shape(rows, 2 * block)],
        [VMEM] * 7,
        16,
        (),
        4 * MIB,
    )(normed, far, w_in, w_in_mate, bias, bias_mate, mask)[0]
    total, *messages = call(
        functools.partial(merge_body, groups),
        [shape(rows, rank, dtype=f32)] * groups,
        [VMEM] * 2,
        16,
    )(total, got)
    got = [across(messages[k - 1], k) for k in range(groups - 1, 0, -1)]
    part = call(
        functools.partial(part_body, step),
        [shape(rows, width, dtype=f32)],
        [VMEM] * 3,
        16,
        (),
        6 * MIB,
    )(act, w_out_near, w_out_mate)[0]
    parts = call(
        functools.partial(up_body, groups),
        [shape(row_dev, width, dtype=f32)] * groups + [shape(row_dev, width)] * groups,
        [SMEM] + [VMEM] * (groups + 4),
        16,
        (),
        6 * MIB,
    )(place, total, low_bias.reshape(1, rank), low_out_near, low_out_mate, part, *got)

    sums = []
    for k in range(groups - 1, -1, -1):
        here = parts[k] + beside(parts[groups + k]).astype(f32)
        sums.append(across(here.astype(bf16), k) if k else here)
    return call(functools.partial(last_body, groups), [shape(row_dev, width)], [VMEM] * groups, 16)(*sums[::-1])[0]


def solution(mesh):
    return jax.shard_map(
        shards,
        mesh=mesh,
        in_specs=(
            P(("rep", "blk"), None),
            P(),
            P(),
            P("rep", None),
            P("rep"),
            P(),
            P(None, "blk"),
            P("blk"),
            P("blk", None),
            P("blk", None),
            P(),
            P(None, "blk"),
        ),
        out_specs=P(("rep", "blk"), None),
        check_vma=False,
    )
```

```python
import functools

import jax
import jax.numpy as jnp
from jax import lax
from jax.experimental import pallas as pl
from jax.experimental.pallas import tpu as pltpu
from jax.sharding import PartitionSpec as P

MIB = 1 << 20
VMEM = pl.BlockSpec(memory_space=pltpu.VMEM)
HBM = pl.BlockSpec(memory_space=pltpu.HBM)
SMEM = pl.BlockSpec(memory_space=pltpu.SMEM)
f32, bf16 = jnp.float32, jnp.bfloat16


def piece(width, most):
    size = 128
    while size * 2 <= most and width % (size * 2) == 0:
        size *= 2
    return size


def window(index, size):
    return pl.ds(pl.multiple_of(index * size, 128), size)


def call(body, outs, ins, limit, scratch=(), moved=2 * MIB):
    return pl.pallas_call(
        body,
        out_shape=outs,
        in_specs=ins,
        out_specs=[VMEM] * len(outs),
        scratch_shapes=list(scratch),
        compiler_params=pltpu.CompilerParams(vmem_limit_bytes=limit * MIB),
        cost_estimate=pl.CostEstimate(flops=0, bytes_accessed=moved, transcendentals=0),
    )


def normal(hidden, gain, shift):
    wide = hidden.astype(f32)
    mean = jnp.mean(wide, axis=-1, keepdims=True)
    centred = wide - mean
    variance = jnp.mean(centred * centred, axis=-1, keepdims=True)
    return (centred * lax.rsqrt(variance + 1e-05) * gain + shift).astype(bf16)


def load_body(count, *refs):
    srcs, dsts, sems = refs[:count], refs[count : 2 * count], refs[2 * count]
    copies = [pltpu.make_async_copy(srcs[i], dsts[i], sems.at[i]) for i in range(count)]
    for copy in copies:
        copy.start()
    for copy in copies:
        copy.wait()


def early_body(groups, soon, *refs):
    held, (gain, shift, near, far) = refs[: groups + soon], refs[groups + soon :]
    rows = held[0].shape[0]
    for out, some in ((near, held[:groups]), (far, held[groups:])):
        for i in range(0, len(some), 2):
            pair = jnp.concatenate([h[...] for h in some[i : i + 2]], axis=0)
            out[i * rows : i * rows + pair.shape[0], :] = normal(pair, gain[...], shift[...])


def norm_body(count, place, *refs):
    held, (near, first, gain, shift, own, mate, far, total, message) = refs[:count], refs[count:]
    rows, done = held[0].shape[0], first.shape[0]
    far[:done, :] = first[...]
    for i in range(0, count, 2):
        pair = jnp.concatenate([h[...] for h in held[i : i + 2]], axis=0)
        far[done + i * rows : done + i * rows + pair.shape[0], :] = normal(pair, gain[...], shift[...])
    share = own.shape[0]
    core = place[0] % 2
    at = window(place[0] // 2, 2 * share)
    columns = jnp.concatenate([near[:, at].astype(f32), far[:, at].astype(f32)], axis=0)
    low, high = columns[:, :share], columns[:, share:]
    mine = jnp.where(core == 0, low, high).astype(bf16)
    other = jnp.where(core == 0, high, low).astype(bf16)
    sums = jnp.dot(mine, own[...], preferred_element_type=f32) + jnp.dot(
        other, mate[...], preferred_element_type=f32
    )
    half = near.shape[0]
    total[...] = sums
    message[:half, :] = sums[half:].astype(bf16)
    message[half:, :] = sums[:half].astype(bf16)


def turn(x, groups, bit):
    rows = x.shape[0] // (2 * groups)
    at = [h * groups + (k ^ bit) for h in range(2) for k in range(groups)]
    return jnp.concatenate([x[i * rows : (i + 1) * rows] for i in at], axis=0)


def merge_body(groups, total, got, out, *messages):
    sums = total[...] + got[...].astype(f32)
    out[...] = sums
    for k in range(1, groups):
        messages[k - 1][...] = turn(sums, groups, k).astype(bf16)


def up_body(groups, place, total, bias, own, mate, part, *refs):
    got, outs = refs[: groups - 1], refs[groups - 1 :]
    sums = total[...]
    for g in got:
        sums = sums + g[...].astype(f32)
    hidden = jnp.maximum(sums + bias[...], 0.0).astype(bf16)
    core = place[0] % 2
    mine = jnp.dot(hidden, own[...], preferred_element_type=f32)
    other = jnp.dot(hidden, mate[...], preferred_element_type=f32)
    both = jnp.concatenate([jnp.where(core == 0, mine, other), jnp.where(core == 0, other, mine)], axis=1)
    at = window(place[0] // 2, both.shape[1])
    rows = outs[0].shape[0]
    for q in range(2 * groups):
        some = slice(q * rows, (q + 1) * rows)
        outs[q][...] = part[some, :].astype(outs[q].dtype)
        outs[q][:, at] = (part[some, at] + both[some]).astype(outs[q].dtype)


def last_body(groups, *refs):
    sums, out = refs[:groups], refs[groups]
    total = sums[0][...]
    for k in range(1, groups):
        total = total + sums[k][...].astype(f32)
    out[...] = total.astype(bf16)


def act_body(step, near, far, w_own, w_mate, b_own, b_mate, mask, out):
    total = jnp.zeros(out.shape, f32)
    for i in range(near.shape[1] // step):
        at = slice(i * step, (i + 1) * step)
        rows = jnp.concatenate([near[:, at], far[:, at]], axis=0)
        both = jnp.concatenate([w_own[at, :], w_mate[at, :]], axis=1)
        total = total + jnp.dot(rows, both, preferred_element_type=f32)
    bias = jnp.concatenate([b_own[...], b_mate[...]], axis=1)
    out[...] = (jnp.maximum(total + bias, 0.0) * mask[...]).astype(bf16)


def part_body(step, act, w_own, w_mate, out):
    for i in range(out.shape[1] // step):
        at = slice(i * step, (i + 1) * step)
        both = jnp.concatenate([w_own[:, at], w_mate[:, at]], axis=0)
        out[:, at] = jnp.dot(act[...], both, preferred_element_type=f32)


def activity(lists, counts, block_slot):
    groups, top = lists.shape
    nblocks = block_slot.shape[0]
    names = jnp.arange(nblocks, dtype=jnp.int32)
    live = (jnp.arange(top, dtype=jnp.int32)[None, :] < counts[:, None]).astype(jnp.int32)
    hits = (lists[:, :, None] == names[None, None, :]).astype(jnp.int32) * live[:, :, None]
    by_block = jnp.sum(hits, axis=1)
    placed = (block_slot[:, None] == names[None, :]).astype(jnp.int32)
    return jnp.sum(by_block[:, :, None] * placed[None, :, :], axis=1)


def shards(
    hidden,
    ln_gain,
    ln_shift,
    lists,
    counts,
    block_slot,
    w_in,
    b_in,
    w_out,
    low_in,
    low_bias,
    low_out,
):
    devices = lax.axis_size("blk")
    position = lax.axis_index("blk")
    row_dev, width = hidden.shape
    groups = lists.shape[0]
    share, rank = low_in.shape
    block = w_in.shape[1]
    assert devices == 4 * groups
    plane = position // 4
    place = jnp.reshape(position, (1,)).astype(jnp.int32)
    some, rows = groups * row_dev, 2 * groups * row_dev

    def across(x, k):
        return lax.ppermute(x, "blk", [(i, i ^ (4 * k)) for i in range(devices)])

    def beside(x):
        return lax.ppermute(x, "blk", [(i, i ^ 2) for i in range(devices)])

    def core(x):
        return lax.ppermute(x, "blk", [(i, i ^ 1) for i in range(devices)])

    def shape(*dims, dtype=bf16):
        return jax.ShapeDtypeStruct(dims, dtype)

    gain, shift, bias = ln_gain.reshape(1, width), ln_shift.reshape(1, width), b_in.reshape(1, block)
    span = 2 * share

    held = [hidden] + [across(hidden, k) for k in range(1, groups)]
    w_in_mate = core(w_in)
    held[1], lists, counts, block_slot = lax.optimization_barrier((held[1], lists, counts, block_slot))

    table = activity(lists, counts, block_slot)
    by = plane ^ jnp.arange(groups)
    at = position ^ jnp.arange(2)
    relate = (by[:, None] == jnp.arange(groups)[None, :])[:, None, :, None]
    choose = (at[:, None] == jnp.arange(devices)[None, :])[None, :, None, :]
    live = jnp.sum(jnp.where(relate & choose, table[None, None], 0), axis=(2, 3)).astype(f32)
    mask = jnp.broadcast_to(live[None, :, None, :, None], (2, groups, row_dev, 2, block)).reshape(rows, 2 * block)

    low_in_sent, mask = lax.optimization_barrier((low_in, mask))
    low_in_mate = core(low_in_sent)
    early, bias_mate = lax.optimization_barrier((hidden, core(bias)))
    beyond = [beside(h) for h in [early] + held[1:]]
    near = (hidden, gain, shift, low_in, w_in, w_out, low_out)
    *near, mask, beyond[0] = lax.optimization_barrier((*near, mask, beyond[0]))
    near = call(
        functools.partial(load_body, len(near)),
        [shape(*x.shape, dtype=x.dtype) for x in near],
        [HBM] * len(near),
        16,
        [pltpu.SemaphoreType.DMA((len(near),))],
        8 * MIB,
    )(*[pltpu.with_memory_space_constraint(x, pltpu.HBM) for x in near])
    hidden_near, gain, shift, low_in, w_in, w_out_near, low_out_near = near
    *_, w_in_mate, w_out_sent, low_out_sent = lax.optimization_barrier(
        (*held, *beyond[: groups // 2], w_in_mate, w_out, low_out)
    )
    w_out_mate, low_out_mate = core(w_out_sent), core(low_out_sent)
    held[0] = hidden_near

    soon = groups // 2
    normed, first = call(
        functools.partial(early_body, groups, soon),
        [shape(some, width), shape(soon * row_dev, width)],
        [VMEM] * (groups + soon + 2),
        16,
        (),
        4 * MIB,
    )(*held, *beyond[:soon], gain, shift)
    far, total, message = call(
        functools.partial(norm_body, groups - soon),
        [shape(some, width), shape(rows, rank, dtype=f32), shape(rows, rank)],
        [SMEM] + [VMEM] * (groups - soon + 6),
        16,
        (),
        4 * MIB,
    )(place, *beyond[soon:], normed, first, gain, shift, low_in, low_in_mate)
    got = beside(message)
    step = piece(width, 2048)
    act = call(
        functools.partial(act_body, step),
        [shape(rows, 2 * block)],
        [VMEM] * 7,
        16,
        (),
        4 * MIB,
    )(normed, far, w_in, w_in_mate, bias, bias_mate, mask)[0]
    total, *messages = call(
        functools.partial(merge_body, groups),
        [shape(rows, rank, dtype=f32)] + [shape(rows, rank)] * (groups - 1),
        [VMEM] * 2,
        16,
    )(total, got)
    got = [across(messages[k - 1], k) for k in range(groups - 1, 0, -1)]
    part = call(
        functools.partial(part_body, step),
        [shape(rows, width, dtype=f32)],
        [VMEM] * 3,
        16,
        (),
        6 * MIB,
    )(act, w_out_near, w_out_mate)[0]
    parts = call(
        functools.partial(up_body, groups),
        [shape(row_dev, width, dtype=f32)] * groups + [shape(row_dev, width)] * groups,
        [SMEM] + [VMEM] * (groups + 4),
        16,
        (),
        6 * MIB,
    )(place, total, low_bias.reshape(1, rank), low_out_near, low_out_mate, part, *got)

    sums, here, mark = [], None, None
    for k in range(groups - 1, -1, -1):
        mine = parts[groups + k]
        if k == 0:
            mine, _ = lax.optimization_barrier((mine, mark))
        come = beside(mine)
        if here is not None:
            come, _ = lax.optimization_barrier((come, here))
        here = parts[k] + come.astype(f32)
        here = here.astype(bf16) if k else here
        mark = here if k == groups // 2 else mark
        sums.append(across(here, k) if k else here)
    return call(functools.partial(last_body, groups), [shape(row_dev, width)], [VMEM] * groups, 16)(*sums[::-1])[0]


def solution(mesh):
    return jax.shard_map(
        shards,
        mesh=mesh,
        in_specs=(
            P(("rep", "blk"), None),
            P(),
            P(),
            P("rep", None),
            P("rep"),
            P(),
            P(None, "blk"),
            P("blk"),
            P("blk", None),
            P("blk", None),
            P(),
            P(None, "blk"),
        ),
        out_specs=P(("rep", "blk"), None),
        check_vma=False,
    )
```

```python
import functools

import jax
import jax.numpy as jnp
from jax import lax
from jax.experimental import pallas as pl
from jax.experimental.pallas import tpu as pltpu
from jax.sharding import PartitionSpec as P

MIB = 1 << 20
VMEM = pl.BlockSpec(memory_space=pltpu.VMEM)
HBM = pl.BlockSpec(memory_space=pltpu.HBM)
SMEM = pl.BlockSpec(memory_space=pltpu.SMEM)
f32, bf16 = jnp.float32, jnp.bfloat16


def piece(width, most):
    size = 128
    while size * 2 <= most and width % (size * 2) == 0:
        size *= 2
    return size


def window(index, size):
    return pl.ds(pl.multiple_of(index * size, 128), size)


def call(body, outs, ins, limit, scratch=(), moved=2 * MIB):
    return pl.pallas_call(
        body,
        out_shape=outs,
        in_specs=ins,
        out_specs=[VMEM] * len(outs),
        scratch_shapes=list(scratch),
        compiler_params=pltpu.CompilerParams(vmem_limit_bytes=limit * MIB),
        cost_estimate=pl.CostEstimate(flops=0, bytes_accessed=moved, transcendentals=0),
    )


def normal(hidden, gain, shift):
    wide = hidden.astype(f32)
    mean = jnp.mean(wide, axis=-1, keepdims=True)
    centred = wide - mean
    variance = jnp.mean(centred * centred, axis=-1, keepdims=True)
    return (centred * lax.rsqrt(variance + 1e-05) * gain + shift).astype(bf16)


def load_body(count, *refs):
    srcs, dsts, sems = refs[:count], refs[count : 2 * count], refs[2 * count]
    copies = [pltpu.make_async_copy(srcs[i], dsts[i], sems.at[i]) for i in range(count)]
    for copy in copies:
        copy.start()
    for copy in copies:
        copy.wait()


def early_body(groups, soon, *refs):
    held, (gain, shift, near, far) = refs[: groups + soon], refs[groups + soon :]
    rows = held[0].shape[0]
    for out, some in ((near, held[:groups]), (far, held[groups:])):
        for i in range(0, len(some), 2):
            pair = jnp.concatenate([h[...] for h in some[i : i + 2]], axis=0)
            out[i * rows : i * rows + pair.shape[0], :] = normal(pair, gain[...], shift[...])


def norm_body(count, place, *refs):
    held, (near, first, gain, shift, own, mate, far, total, message) = refs[:count], refs[count:]
    rows, done = held[0].shape[0], first.shape[0]
    far[:done, :] = first[...]
    for i in range(0, count, 2):
        pair = jnp.concatenate([h[...] for h in held[i : i + 2]], axis=0)
        far[done + i * rows : done + i * rows + pair.shape[0], :] = normal(pair, gain[...], shift[...])
    share = own.shape[0]
    core = place[0] % 2
    at = window(place[0] // 2, 2 * share)
    columns = jnp.concatenate([near[:, at].astype(f32), far[:, at].astype(f32)], axis=0)
    low, high = columns[:, :share], columns[:, share:]
    mine = jnp.where(core == 0, low, high).astype(bf16)
    other = jnp.where(core == 0, high, low).astype(bf16)
    sums = jnp.dot(mine, own[...], preferred_element_type=f32) + jnp.dot(
        other, mate[...], preferred_element_type=f32
    )
    half = near.shape[0]
    total[...] = sums
    message[:half, :] = sums[half:].astype(bf16)
    message[half:, :] = sums[:half].astype(bf16)


def turn(x, groups, bit):
    rows = x.shape[0] // (2 * groups)
    at = [h * groups + (k ^ bit) for h in range(2) for k in range(groups)]
    return jnp.concatenate([x[i * rows : (i + 1) * rows] for i in at], axis=0)


def merge_body(groups, total, got, out, *messages):
    sums = total[...] + got[...].astype(f32)
    out[...] = sums
    for k in range(1, groups):
        messages[k - 1][...] = turn(sums, groups, k).astype(bf16)


def up_body(groups, place, total, bias, own, mate, part, *refs):
    got, outs = refs[: groups - 1], refs[groups - 1 :]
    sums = total[...]
    for g in got:
        sums = sums + g[...].astype(f32)
    hidden = jnp.maximum(sums + bias[...], 0.0).astype(bf16)
    core = place[0] % 2
    mine = jnp.dot(hidden, own[...], preferred_element_type=f32)
    other = jnp.dot(hidden, mate[...], preferred_element_type=f32)
    both = jnp.concatenate([jnp.where(core == 0, mine, other), jnp.where(core == 0, other, mine)], axis=1)
    at = window(place[0] // 2, both.shape[1])
    rows = outs[0].shape[0]
    for q in range(2 * groups):
        some = slice(q * rows, (q + 1) * rows)
        outs[q][...] = part[some, :].astype(outs[q].dtype)
        outs[q][:, at] = (part[some, at] + both[some]).astype(outs[q].dtype)


def last_body(groups, *refs):
    sums, out = refs[:groups], refs[groups]
    total = sums[0][...]
    for k in range(1, groups):
        total = total + sums[k][...].astype(f32)
    out[...] = total.astype(bf16)


def act_body(step, near, far, w_own, w_mate, b_own, b_mate, mask, out):
    total = jnp.zeros(out.shape, f32)
    for i in range(near.shape[1] // step):
        at = slice(i * step, (i + 1) * step)
        rows = jnp.concatenate([near[:, at], far[:, at]], axis=0)
        both = jnp.concatenate([w_own[at, :], w_mate[at, :]], axis=1)
        total = total + jnp.dot(rows, both, preferred_element_type=f32)
    bias = jnp.concatenate([b_own[...], b_mate[...]], axis=1)
    out[...] = (jnp.maximum(total + bias, 0.0) * mask[...]).astype(bf16)


def part_body(step, act, w_own, w_mate, out):
    for i in range(out.shape[1] // step):
        at = slice(i * step, (i + 1) * step)
        both = jnp.concatenate([w_own[:, at], w_mate[:, at]], axis=0)
        out[:, at] = jnp.dot(act[...], both, preferred_element_type=f32)


def activity(lists, counts, block_slot):
    groups, top = lists.shape
    nblocks = block_slot.shape[0]
    names = jnp.arange(nblocks, dtype=jnp.int32)
    live = (jnp.arange(top, dtype=jnp.int32)[None, :] < counts[:, None]).astype(jnp.int32)
    hits = (lists[:, :, None] == names[None, None, :]).astype(jnp.int32) * live[:, :, None]
    by_block = jnp.sum(hits, axis=1)
    placed = (block_slot[:, None] == names[None, :]).astype(jnp.int32)
    return jnp.sum(by_block[:, :, None] * placed[None, :, :], axis=1)


def shards(
    hidden,
    ln_gain,
    ln_shift,
    lists,
    counts,
    block_slot,
    w_in,
    b_in,
    w_out,
    low_in,
    low_bias,
    low_out,
):
    devices = lax.axis_size("blk")
    position = lax.axis_index("blk")
    row_dev, width = hidden.shape
    groups = lists.shape[0]
    share, rank = low_in.shape
    block = w_in.shape[1]
    assert devices == 4 * groups
    plane = position // 4
    place = jnp.reshape(position, (1,)).astype(jnp.int32)
    some, rows = groups * row_dev, 2 * groups * row_dev

    def across(x, k):
        return lax.ppermute(x, "blk", [(i, i ^ (4 * k)) for i in range(devices)])

    def beside(x):
        return lax.ppermute(x, "blk", [(i, i ^ 2) for i in range(devices)])

    def core(x):
        return lax.ppermute(x, "blk", [(i, i ^ 1) for i in range(devices)])

    def shape(*dims, dtype=bf16):
        return jax.ShapeDtypeStruct(dims, dtype)

    gain, shift, bias = ln_gain.reshape(1, width), ln_shift.reshape(1, width), b_in.reshape(1, block)
    span = 2 * share

    held = [hidden] + [across(hidden, k) for k in range(1, groups)]
    w_in_mate = core(w_in)
    early, bias_mate = lax.optimization_barrier((hidden, core(bias)))
    beyond = [beside(h) for h in [early] + held[1:]]
    beyond[0], lists, counts, block_slot = lax.optimization_barrier((beyond[0], lists, counts, block_slot))

    table = activity(lists, counts, block_slot)
    by = plane ^ jnp.arange(groups)
    at = position ^ jnp.arange(2)
    relate = (by[:, None] == jnp.arange(groups)[None, :])[:, None, :, None]
    choose = (at[:, None] == jnp.arange(devices)[None, :])[None, :, None, :]
    live = jnp.sum(jnp.where(relate & choose, table[None, None], 0), axis=(2, 3)).astype(f32)
    mask = jnp.broadcast_to(live[None, :, None, :, None], (2, groups, row_dev, 2, block)).reshape(rows, 2 * block)

    low_in_sent, mask = lax.optimization_barrier((low_in, mask))
    low_in_mate = core(low_in_sent)
    near = (hidden, gain, shift, low_in, w_in, w_out, low_out)
    *near, mask, beyond[0] = lax.optimization_barrier((*near, mask, beyond[0]))
    near = call(
        functools.partial(load_body, len(near)),
        [shape(*x.shape, dtype=x.dtype) for x in near],
        [HBM] * len(near),
        16,
        [pltpu.SemaphoreType.DMA((len(near),))],
        8 * MIB,
    )(*[pltpu.with_memory_space_constraint(x, pltpu.HBM) for x in near])
    hidden_near, gain, shift, low_in, w_in, w_out_near, low_out_near = near
    *_, w_in_mate, w_out_sent, low_out_sent = lax.optimization_barrier(
        (*held, *beyond[: groups // 2], w_in_mate, w_out, low_out)
    )
    w_out_mate, low_out_mate = core(w_out_sent), core(low_out_sent)
    held[0] = hidden_near

    soon = groups // 2
    normed, first = call(
        functools.partial(early_body, groups, soon),
        [shape(some, width), shape(soon * row_dev, width)],
        [VMEM] * (groups + soon + 2),
        16,
        (),
        4 * MIB,
    )(*held, *beyond[:soon], gain, shift)
    far, total, message = call(
        functools.partial(norm_body, groups - soon),
        [shape(some, width), shape(rows, rank, dtype=f32), shape(rows, rank)],
        [SMEM] + [VMEM] * (groups - soon + 6),
        16,
        (),
        4 * MIB,
    )(place, *beyond[soon:], normed, first, gain, shift, low_in, low_in_mate)
    got = beside(message)
    step = piece(width, 2048)
    act = call(
        functools.partial(act_body, step),
        [shape(rows, 2 * block)],
        [VMEM] * 7,
        16,
        (),
        4 * MIB,
    )(normed, far, w_in, w_in_mate, bias, bias_mate, mask)[0]
    total, *messages = call(
        functools.partial(merge_body, groups),
        [shape(rows, rank, dtype=f32)] + [shape(rows, rank)] * (groups - 1),
        [VMEM] * 2,
        16,
    )(total, got)
    got = [across(messages[k - 1], k) for k in range(groups - 1, 0, -1)]
    part = call(
        functools.partial(part_body, step),
        [shape(rows, width, dtype=f32)],
        [VMEM] * 3,
        16,
        (),
        6 * MIB,
    )(act, w_out_near, w_out_mate)[0]
    parts = call(
        functools.partial(up_body, groups),
        [shape(row_dev, width, dtype=f32)] * groups + [shape(row_dev, width)] * groups,
        [SMEM] + [VMEM] * (groups + 4),
        16,
        (),
        6 * MIB,
    )(place, total, low_bias.reshape(1, rank), low_out_near, low_out_mate, part, *got)

    sums = []
    for k in range(groups - 1, -1, -1):
        here = parts[k] + beside(parts[groups + k]).astype(f32)
        sums.append(across(here.astype(bf16), k) if k else here)
    return call(functools.partial(last_body, groups), [shape(row_dev, width)], [VMEM] * groups, 16)(*sums[::-1])[0]


def solution(mesh):
    return jax.shard_map(
        shards,
        mesh=mesh,
        in_specs=(
            P(("rep", "blk"), None),
            P(),
            P(),
            P("rep", None),
            P("rep"),
            P(),
            P(None, "blk"),
            P("blk"),
            P("blk", None),
            P("blk", None),
            P(),
            P(None, "blk"),
        ),
        out_specs=P(("rep", "blk"), None),
        check_vma=False,
    )
```
